32 devices in a mesh: shard: 16 (over z, y, x), tensor: 2 (over core).
Axes of the slice: x: 2, y: 2, z: 4, core: 2. Of those that a mesh axis runs over, the one named last changes fastest.
Arguments:
- tokens: bfloat16 [256, 197, 384], P('shard'), may hold values from -6 to 6
- cotangent: bfloat16 [256, 197, 384], P('shard'), may hold values from -6 to 6
- ln1_gain: bfloat16 [2, 384], P(None, 'shard'), may hold values from 0.5 to 1.5
- ln1_bias: bfloat16 [2, 384], P(None, 'shard'), may hold values from -3 to 3
- w_qkv: bfloat16 [2, 384, 3, 6, 64], P(None, 'shard', None, 'tensor'), may hold values from -0.3125 to 0.3125
- b_qv: bfloat16 [2, 2, 6, 64], P(None, None, 'tensor', 'shard'), may hold values from -3 to 3
- w_proj: bfloat16 [2, 6, 64, 384], P(None, 'tensor', None, 'shard'), may hold values from -1.25 to 1.25
- b_proj: bfloat16 [2, 384], P(None, 'shard'), may hold values from -3 to 3
- ln2_gain: bfloat16 [2, 384], P(None, 'shard'), may hold values from 0.5 to 1.5
- ln2_bias: bfloat16 [2, 384], P(None, 'shard'), may hold values from -3 to 3
- w_up: bfloat16 [2, 384, 1536], P(None, 'shard', 'tensor'), may hold values from -0.3125 to 0.3125
- b_up: bfloat16 [2, 12, 128], P(None, 'tensor', 'shard'), may hold values from -3 to 3
- w_down: bfloat16 [2, 1536, 384], P(None, 'tensor', 'shard'), may hold values from -0.15625 to 0.15625
- b_down: bfloat16 [2, 384], P(None, 'shard'), may hold values from -3 to 3
Outputs:
- output: bfloat16 [256, 197, 384], P('shard')
- grad_tokens: float32 [256, 197, 384], P('shard')
- grad_ln1_gain: float32 [2, 384], P(None, 'shard')
- grad_ln1_bias: float32 [2, 384], P(None, 'shard')
- grad_w_qkv: float32 [2, 384, 3, 6, 64], P(None, 'shard', None, 'tensor')
- grad_b_qv: float32 [2, 2, 6, 64], P(None, None, 'tensor', 'shard')
- grad_w_proj: float32 [2, 6, 64, 384], P(None, 'tensor', None, 'shard')
- grad_b_proj: float32 [2, 384], P(None, 'shard')
- grad_ln2_gain: float32 [2, 384], P(None, 'shard')
- grad_ln2_bias: float32 [2, 384], P(None, 'shard')
- grad_w_up: float32 [2, 384, 1536], P(None, 'shard', 'tensor')
- grad_b_up: float32 [2, 12, 128], P(None, 'tensor', 'shard')
- grad_w_down: float32 [2, 1536, 384], P(None, 'tensor', 'shard')
- grad_b_down: float32 [2, 384], P(None, 'shard')
The draws below stay inside these ranges and needn't reach their ends.
All inputs are finite; a program needn't handle non-finite values.
Results may differ from the reference program's by a relative error of at most 0.013.
Values may be sent and summed in bfloat16 or wider, within the bound.
No kernel may reach another device: no remote copies, remote signals or barrier semaphores. Data moves between devices by JAX's collectives and lax.ppermute only.
A program may use at most 256 MiB of HBM per device.

```python
import jax
import jax.numpy as jnp
from jax import lax

D = 384
HEADS = 6
HEAD_DIM = 64
FF = 1536
SEQ = 197
LANES = 128
LAYERS = 2
IMG_DEV = 16
IMAGES = 256
N_SHARD = 16


def levels(rng, dims, shards, smallest, largest):
    factor_of, own = 1.0, jax.random.fold_in(rng, 6)
    for position, blocks in shards:
        heights = jnp.exp(jax.random.uniform(jax.random.fold_in(own, position), (blocks,), jnp.float32, smallest / len(shards), largest / len(shards)))
        factor_of = factor_of * jnp.repeat(heights, dims[position] // blocks).reshape([-1 if axis == position else 1 for axis in range(len(dims))])
    return factor_of


def gaussian(own_key, dims, width, limit, pieces=(), dtype=jnp.bfloat16):
    array = width * jax.random.normal(own_key, dims, jnp.float32)
    if pieces:
        array = array * levels(own_key, dims, pieces, -0.22, 0.18)
    return jnp.clip(array, -limit, limit).astype(dtype)


def setup_inputs(seed: int = 0) -> dict:
    splits = jax.random.split(jax.random.key(seed), 15)
    tokens = gaussian(splits[0], (IMAGES, SEQ, D), 1.0, 6.0, ((0, 16),))
    cotangent = gaussian(splits[1], (IMAGES, SEQ, D), 1.0, 6.0, ((0, 16),))
    ln1_gain = jnp.clip(1.0 + 0.1 * jax.random.normal(splits[2], (LAYERS, D), jnp.float32), 0.5, 1.5).astype(jnp.bfloat16)
    ln1_bias = gaussian(splits[3], (LAYERS, D), 0.5, 3.0, ((1, 16),))
    w_qkv = gaussian(splits[4], (LAYERS, D, 3, HEADS, HEAD_DIM), D ** -0.5, 0.3125, ((1, 16), (3, 2)))
    b_qv = gaussian(splits[5], (LAYERS, 2, HEADS, HEAD_DIM), 0.5, 3.0, ((2, 2), (3, 16)))
    w_proj = gaussian(splits[6], (LAYERS, HEADS, HEAD_DIM, D), (D // 16) ** -0.5, 1.25, ((1, 2), (3, 16)))
    b_proj = gaussian(splits[7], (LAYERS, D), 0.5, 3.0, ((1, 16),))
    ln2_gain = jnp.clip(1.0 + 0.1 * jax.random.normal(splits[8], (LAYERS, D), jnp.float32), 0.5, 1.5).astype(jnp.bfloat16)
    ln2_bias = gaussian(splits[9], (LAYERS, D), 0.5, 3.0, ((1, 16),))
    w_up = gaussian(splits[10], (LAYERS, D, FF), D ** -0.5, 0.3125, ((1, 16), (2, 2)))
    b_up = gaussian(splits[11], (LAYERS, FF // LANES, LANES), 0.5, 3.0, ((1, 2), (2, 16)))
    w_down = gaussian(splits[12], (LAYERS, FF, D), FF ** -0.5, 0.15625, ((1, 2), (2, 16)))
    b_down = gaussian(splits[13], (LAYERS, D), 0.5, 3.0, ((1, 16),))
    return dict(tokens=tokens, cotangent=cotangent, ln1_gain=ln1_gain, ln1_bias=ln1_bias, w_qkv=w_qkv, b_qv=b_qv, w_proj=w_proj, b_proj=b_proj, ln2_gain=ln2_gain, ln2_bias=ln2_bias, w_up=w_up, b_up=b_up, w_down=w_down, b_down=b_down)


@jax.custom_vjp
def low(v):
    return lax.optimization_barrier(v.astype(jnp.bfloat16)).astype(jnp.float32)

@jax.custom_vjp
def low_back(v):
    return v

def low_keep(v):
    return (low(v), None)

def low_pass(kept, grad):
    return (grad,)

def back_keep(v):
    return (v, None)

def back_low(kept, grad):
    return (low(grad),)
low.defvjp(low_keep, low_pass)
low_back.defvjp(back_keep, back_low)
epsilon = 1e-06
inv_root_two = 0.7071067811865476

def normalize(values, gain_vec, shift_vec):
    centred = values - lax.optimization_barrier(jnp.mean(values, -1, keepdims=True))
    spread = lax.rsqrt(lax.optimization_barrier(jnp.mean(centred * centred, -1, keepdims=True)) + epsilon)
    return centred * spread * gain_vec + shift_vec

def gelu_exact(values):
    return 0.5 * values * (1.0 + lax.erf(values * inv_root_two))

def matmul(left, right):
    return jnp.dot(left, right, precision=lax.Precision.HIGHEST)

def forward(images, params):
    ln1_gain, ln1_bias, w_qkv, b_qv, w_proj, b_proj, ln2_gain, ln2_bias, w_up, b_up, w_down, b_down = params
    stream = images
    count = images.shape[0]
    for layer_index in range(LAYERS):
        normed = low(normalize(stream, ln1_gain[layer_index], ln1_bias[layer_index]))
        mixed = matmul(normed, w_qkv[layer_index].reshape(D, 3 * D)).reshape(count, SEQ, 3, HEADS, HEAD_DIM)
        queries = low(low_back(mixed[:, :, 0] + b_qv[layer_index, 0]))
        key_rows = low(low_back(mixed[:, :, 1]))
        value_rows = low(low_back(mixed[:, :, 2] + b_qv[layer_index, 1]))
        scores = low_back(jnp.einsum('gqhd,gkhd->ghqk', queries, key_rows, precision=lax.Precision.HIGHEST) * HEAD_DIM ** (-0.5))
        probs = low(jax.nn.softmax(scores, axis=-1))
        attended = jnp.einsum('ghqk,gkhd->gqhd', probs, value_rows, precision=lax.Precision.HIGHEST)
        attended = low(low_back(attended)).reshape(count, SEQ, D)
        branch = low_back(matmul(attended, w_proj[layer_index].reshape(D, D)))
        stream = stream + branch + b_proj[layer_index]
        normed_two = low(normalize(stream, ln2_gain[layer_index], ln2_bias[layer_index]))
        pre_act = low_back(matmul(normed_two, w_up[layer_index]) + b_up[layer_index].reshape(FF))
        active = low(gelu_exact(pre_act))
        stream = stream + low_back(matmul(active, w_down[layer_index])) + b_down[layer_index]
    return stream

def reference(tokens, cotangent, ln1_gain, ln1_bias, w_qkv, b_qv, w_proj, b_proj, ln2_gain, ln2_bias, w_up, b_up, w_down, b_down):
    params = tuple((weight.astype(jnp.float32) for weight in (ln1_gain, ln1_bias, w_qkv, b_qv, w_proj, b_proj, ln2_gain, ln2_bias, w_up, b_up, w_down, b_down)))
    image_groups = tokens.astype(jnp.float32).reshape(N_SHARD, IMG_DEV, SEQ, D)
    cot_groups = cotangent.astype(jnp.float32).reshape(N_SHARD, IMG_DEV, SEQ, D)

    def one_group(summed, group_pair):
        group_in, group_cot = group_pair
        result, pullback = jax.vjp(forward, group_in, params)
        grad_in, grad_params = pullback(group_cot)
        return (jax.tree.map(jnp.add, summed, grad_params), (result.astype(jnp.bfloat16), grad_in))
    start = jax.tree.map(jnp.zeros_like, params)
    grads, (results, grad_groups) = lax.scan(one_group, start, (image_groups, cot_groups))
    return (results.reshape(IMAGES, SEQ, D), grad_groups.reshape(IMAGES, SEQ, D), grads[0], grads[1], grads[2], grads[3], grads[4], grads[5], grads[6], grads[7], grads[8], grads[9], grads[10], grads[11])
```

```python
import functools

import jax
import jax.numpy as jnp
from jax import lax
from jax.experimental import pallas as pl
from jax.experimental.pallas import tpu as pltpu
from jax.sharding import PartitionSpec as P

bf16, f32 = jnp.bfloat16, jnp.float32
epsilon = 1e-06
inv_root_two = 0.7071067811865476
inv_root_two_pi = 0.3989422804014327
log2_e = 1.4426950408889634
NN, NT, TN = ((1,), (0,)), ((1,), (1,)), ((0,), (0,))
VMEM_LIMIT = 60 * 2**20
GROUP = 2
HEAD = 64
LANES = 128


def dot(a, b, dims):
    return lax.dot_general(a, b, (dims, ((), ())), preferred_element_type=f32)


def qv_places(width, shards, half):
    heads = width // HEAD // 2
    per, unit = width // shards, HEAD // shards
    n = lax.broadcasted_iota(jnp.int32, (width, 3 * width), 0)
    m = lax.broadcasted_iota(jnp.int32, (width, 3 * width), 1)
    owner, rest = n // per, n % per
    part, rest = rest // (heads * unit), rest % (heads * unit)
    place = part * 2 * width + half * (width // 2) + (rest // unit) * HEAD + owner * unit + rest % unit
    return jnp.where(place == m, 1.0, 0.0).astype(bf16)


def up_places(width, shards):
    per, unit = width // shards, LANES // shards
    n = lax.broadcasted_iota(jnp.int32, (width, width), 0)
    m = lax.broadcasted_iota(jnp.int32, (width, width), 1)
    owner, rest = n // per, n % per
    place = (rest // unit) * LANES + owner * unit + rest % unit
    return jnp.where(place == m, 1.0, 0.0).astype(bf16)


def expand_vec(vec_refs, table, shards):
    width = vec_refs[0].shape[0]
    table[...] = jnp.zeros_like(table)
    to_up = up_places(width, shards)
    qkv = None
    for half, ref in enumerate(vec_refs):
        rows = ref[...].astype(f32).T[:16]
        if half == 0:
            table[0:6, 0:width] = rows[0:6]
        low = rows.astype(bf16)
        placed = dot(low, qv_places(width, shards, half), NN)
        qkv = placed if qkv is None else qkv + placed
        ups = dot(low, to_up, NN)
        for k in range(2):
            at = (2 * half + k) * width
            table[7:8, at : at + width] = ups[7 + k : 8 + k]
    table[6:7, 0 : 3 * width] = qkv[6:7]


def pack_vec(table, outs, shards):
    width = outs[0].shape[0]
    to_up = up_places(width, shards)
    full = table[...].astype(bf16)
    for half, (ref, at) in enumerate(outs_at(outs)):
        qv = dot(full[:, : 3 * width], qv_places(width, shards, half), NT)
        rows = [table[0:6, 0:width], qv[6:7]]
        for k in range(2):
            first = (2 * half + k) * width
            rows.append(dot(full[:, first : first + width], to_up, NT)[7:8])
        index = lax.broadcasted_iota(jnp.int32, (LANES, width), 0)
        block = jnp.zeros((LANES, width), f32)
        for r in range(9):
            row = rows[0][r : r + 1] if r < 6 else rows[r - 5]
            block = jnp.where(index == r, row, block)
        ref[:, at : at + LANES] = block.T.astype(bf16)


def outs_at(outs):
    return [(ref, ref.shape[1] - LANES) for ref in outs]


def norm_parts(x):
    c = x - jnp.mean(x, -1, keepdims=True)
    s = lax.rsqrt(jnp.mean(c * c, -1, keepdims=True) + epsilon)
    return c * s, s


def norm_back(dh, u, s, gain):
    t = dh * gain
    return s * (t - jnp.mean(t, -1, keepdims=True) - u * jnp.mean(t * u, -1, keepdims=True))


def row_sum(x):
    return jnp.sum(x, 0, keepdims=True)


def halves_of_lanes(x):
    low = lax.broadcasted_iota(jnp.int32, x.shape, 1) < HEAD
    zero = jnp.zeros_like(x)
    return jnp.where(low, x, zero), jnp.where(low, zero, x)


def join_lanes(a, b):
    return jnp.where(lax.broadcasted_iota(jnp.int32, a.shape, 1) < HEAD, a, b)


def probs_t(scores, length):
    row = lax.broadcasted_iota(jnp.int32, scores.shape, 0)
    scores = jnp.where(row < length, scores, -1e30)
    high = jnp.max(scores, 0, keepdims=True)
    e = jnp.exp2((scores - high) * (HEAD**-0.5 * log2_e))
    return (e * (1.0 / jnp.sum(e, 0, keepdims=True))).astype(bf16)


def attention(qkv, p_ref, o_ref, width, length):
    for j in range(width // LANES):
        at = LANES * j
        q = qkv[:, at : at + LANES]
        k = qkv[:, width + at : width + at + LANES]
        v = qkv[:, 2 * width + at : 2 * width + at + LANES]
        out = []
        for h, q_one in enumerate(halves_of_lanes(q)):
            p = probs_t(dot(k, q_one, NT), length)
            p_ref[2 * j + h] = p
            out.append(dot(p, v, TN))
        o_ref[:, at : at + LANES] = join_lanes(*out).astype(bf16)


def attention_back(qkv, p_ref, do, dz_ref, width):
    for j in range(width // LANES):
        at = LANES * j
        q = qkv[:, at : at + LANES]
        k = qkv[:, width + at : width + at + LANES]
        v = qkv[:, 2 * width + at : 2 * width + at + LANES]
        do_pair = do[:, at : at + LANES]
        found = []
        for h, v_one in enumerate(halves_of_lanes(v)):
            p = p_ref[2 * j + h]
            dp = dot(v_one, do_pair, NT)
            pf = p.astype(f32)
            t = pf * dp
            ds = (t - pf * row_sum(t)).astype(bf16)
            found.append((dot(ds, k, TN), dot(ds, q, NN), dot(p, do_pair, NN)))
        for part in range(3):
            x = join_lanes(found[0][part], found[1][part])
            if part < 2:
                x = x * HEAD**-0.5
            dz_ref[:, part * width + at : part * width + at + LANES] = x.astype(bf16)


def place_attn_weights(a_refs, w_qkv, w_proj):
    width = w_qkv.shape[0]
    half = width // 2
    for i, ref in enumerate(a_refs):
        for part in range(3):
            to = part * width + i * half
            w_qkv[:, to : to + half] = ref[:, part * half : (part + 1) * half]
        w_proj[:, i * half : (i + 1) * half] = ref[:, 3 * half : 4 * half]


def store_attn_grads(acc_qkv, acc_proj, outs):
    width = acc_qkv.shape[0]
    half = width // 2
    for i, ref in enumerate(outs):
        for part in range(3):
            at = part * width + i * half
            ref[:, part * half : (part + 1) * half] = acc_qkv[:, at : at + half].astype(bf16)
        ref[:, 3 * half : 4 * half] = acc_proj[:, i * half : (i + 1) * half].astype(bf16)


def store_mlp_grads(acc_up, acc_down, outs):
    half = acc_up.shape[1] // 2
    for i, ref in enumerate(outs):
        ref[:, :half] = acc_up[:, i * half : (i + 1) * half].astype(bf16)
        ref[:, half:] = acc_down[:, i * half : (i + 1) * half].astype(bf16)


def attn_forward(x, table, w_qkv, w_proj, qkv, p_all, o_all, mid, length):
    group, rows, width = x.shape
    gain, shift = table[0:1, :width], table[1:2, :width]
    xs = x[...].reshape(group * rows, width)
    u, _ = norm_parts(xs)
    h = (u * gain + shift).astype(bf16)
    z = dot(h, w_qkv[...], NN) + table[6:7, : 3 * width]
    qkv[...] = z.astype(bf16).reshape(qkv.shape)
    for g in range(group):
        attention(qkv.at[g], p_all.at[g], o_all.at[g], width, length)
    o = o_all[...].reshape(group * rows, width)
    a = dot(o, w_proj[...], NT)
    mid[...] = (xs + a + table[2:3, :width]).reshape(mid.shape)


def mlp_forward(mid, table, m_refs, g_all, slope_all):
    group, rows, width = mid.shape
    ms = mid[...].reshape(group * rows, width)
    u, _ = norm_parts(ms)
    h = (u * table[3:4, :width] + table[4:5, :width]).astype(bf16)
    half = m_refs[0].shape[1] // 2
    total = None
    for i, ref in enumerate(m_refs):
        cols = slice(i * half, (i + 1) * half)
        pre = dot(h, ref[:, :half], NN) + table[7:8, cols]
        phi = 0.5 * (1.0 + lax.erf(pre * inv_root_two))
        g = (pre * phi).astype(bf16)
        g_all[:, :, cols] = g.reshape(group, rows, half)
        slope = phi + pre * jnp.exp(-0.5 * pre * pre) * inv_root_two_pi
        slope_all[:, :, cols] = slope.astype(bf16).reshape(group, rows, half)
        t = dot(g, ref[:, half:], NT)
        total = t if total is None else total + t
    return ms + total + table[5:6, :width]


def mlp_backward(e, mid, table, sums, m_refs, g_all, slope_all, acc_up, acc_down):
    group, rows, width = mid.shape
    half = m_refs[0].shape[1] // 2
    sums[5:6, :width] += row_sum(e)
    e_low = e.astype(bf16)
    u, s = norm_parts(mid[...].reshape(group * rows, width))
    gain = table[3:4, :width]
    h = (u * gain + table[4:5, :width]).astype(bf16)
    dh = None
    for i, ref in enumerate(m_refs):
        cols = slice(i * half, (i + 1) * half)
        dg = dot(e_low, ref[:, half:], NN)
        slope = slope_all[:, :, cols].reshape(group * rows, half).astype(f32)
        dpre = (dg * slope).astype(bf16)
        sums[7:8, cols] += row_sum(dpre.astype(f32))
        acc_up[:, cols] += dot(h, dpre, TN)
        acc_down[:, cols] += dot(e_low, g_all[:, :, cols].reshape(group * rows, half), TN)
        t = dot(dpre, ref[:, :half], NT)
        dh = t if dh is None else dh + t
    sums[3:4, :width] += row_sum(dh * u)
    sums[4:5, :width] += row_sum(dh)
    return e + norm_back(dh, u, s, gain)


def attn_backward(dmid, x, table, sums, w_qkv, w_proj, qkv, p_all, o_all, dz, acc_qkv, acc_proj):
    group, rows, width = x.shape
    sums[2:3, :width] += row_sum(dmid)
    da = dmid.astype(bf16)
    acc_proj[...] += dot(da, o_all[...].reshape(group * rows, width), TN)
    do = dot(da, w_proj[...], NN).astype(bf16)
    for g in range(group):
        attention_back(qkv.at[g], p_all.at[g], do[g * rows : (g + 1) * rows], dz.at[g], width)
    dzs = dz[...].reshape(group * rows, 3 * width)
    sums[6:7, : 3 * width] += row_sum(dzs.astype(f32))
    u, s = norm_parts(x[...].reshape(group * rows, width))
    gain = table[0:1, :width]
    h = (u * gain + table[1:2, :width]).astype(bf16)
    acc_qkv[...] += dot(h, dzs, TN)
    dh = dot(dzs, w_qkv[...], NT)
    sums[0:1, :width] += row_sum(dh * u)
    sums[1:2, :width] += row_sum(dh)
    return dmid + norm_back(dh, u, s, gain)


def load_padded(ref, scratch, first):
    @pl.when(first)
    def _():
        scratch[...] = jnp.zeros_like(scratch)

    for g in range(ref.shape[0]):
        scratch[g, : ref.shape[1], :] = ref[g].astype(f32)


def kernel_attn_forward(shards, core, tok, a_mine, a_other, qkv, p_all, o_all, mid, table, x, w_qkv, w_proj):
    first = pl.program_id(0) == 0

    @pl.when(first)
    def _():
        place_attn_weights((a_mine, a_other), w_qkv, w_proj)
        width = w_qkv.shape[0]
        expand_vec([r.at[:, 2 * width :] for r in (a_mine, a_other)], table, shards)

    load_padded(tok, x, first)
    attn_forward(x, table, w_qkv, w_proj, qkv, p_all, o_all, mid, tok.shape[1])


def kernel_mlp_forward(mid, table, m_mine, m_other, stream, g_all, slope_all):
    out = mlp_forward(mid, table, (m_mine, m_other), g_all, slope_all)
    stream[...] = out.reshape(stream.shape)


def kernel_layer_both(
    shards, core, x, cot, a_mine, a_other, m_mine, m_other,
    out, e_out, ga_mine, ga_other, gm_mine, gm_other,
    table, sums, w_qkv, w_proj, qkv, p_all, o_all, mid, g_all, slope_all, e, dz,
    acc_qkv, acc_proj, acc_up, acc_down,
):
    step = pl.program_id(0)
    first = step == 0
    width = w_qkv.shape[0]

    @pl.when(first)
    def _():
        place_attn_weights((a_mine, a_other), w_qkv, w_proj)
        expand_vec([r.at[:, 2 * width :] for r in (a_mine, a_other)], table, shards)
        for ref in (sums, acc_qkv, acc_proj, acc_up, acc_down):
            ref[...] = jnp.zeros_like(ref)

    length = cot.shape[1]
    group, rows, _ = x.shape
    load_padded(cot, e, first)
    attn_forward(x, table, w_qkv, w_proj, qkv, p_all, o_all, mid, length)
    result = mlp_forward(mid, table, (m_mine, m_other), g_all, slope_all)
    for g in range(group):
        out[g] = result[g * rows : g * rows + length].astype(bf16)
    dmid = mlp_backward(
        e[...].reshape(group * rows, width), mid, table, sums, (m_mine, m_other),
        g_all, slope_all, acc_up, acc_down,
    )
    back = attn_backward(
        dmid, x, table, sums, w_qkv, w_proj, qkv, p_all, o_all, dz, acc_qkv, acc_proj
    )
    e_out[...] = back.reshape(e_out.shape)

    @pl.when(step == pl.num_programs(0) - 1)
    def _():
        store_attn_grads(acc_qkv, acc_proj, (ga_mine, ga_other))
        store_mlp_grads(acc_up, acc_down, (gm_mine, gm_other))
        pack_vec(sums, (ga_mine, ga_other), shards)


def kernel_mlp_backward(
    e, mid, table, g_all, slope_all, m_mine, m_other,
    dmid, sums, gm_mine, gm_other, acc_up, acc_down,
):
    step = pl.program_id(0)

    @pl.when(step == 0)
    def _():
        for ref in (sums, acc_up, acc_down):
            ref[...] = jnp.zeros_like(ref)

    group, rows, width = mid.shape
    back = mlp_backward(
        e[...].reshape(group * rows, width), mid, table, sums, (m_mine, m_other),
        g_all, slope_all, acc_up, acc_down,
    )
    dmid[...] = back.reshape(dmid.shape)

    @pl.when(step == pl.num_programs(0) - 1)
    def _():
        store_mlp_grads(acc_up, acc_down, (gm_mine, gm_other))


def kernel_attn_backward(
    shards, core, dmid, tok, table, sums_in, qkv, p_all, o_all, a_mine, a_other,
    grad, ga_mine, ga_other, sums, x, w_qkv, w_proj, dz, acc_qkv, acc_proj,
):
    step = pl.program_id(0)
    first = step == 0

    @pl.when(first)
    def _():
        place_attn_weights((a_mine, a_other), w_qkv, w_proj)
        sums[...] = sums_in[...]
        for ref in (acc_qkv, acc_proj):
            ref[...] = jnp.zeros_like(ref)

    load_padded(tok, x, first)
    group, rows, width = x.shape
    back = attn_backward(
        dmid[...].reshape(group * rows, width), x, table, sums, w_qkv, w_proj,
        qkv, p_all, o_all, dz, acc_qkv, acc_proj,
    )
    for g in range(group):
        grad[g] = back[g * rows : g * rows + tok.shape[1]].astype(grad.dtype)

    @pl.when(step == pl.num_programs(0) - 1)
    def _():
        store_attn_grads(acc_qkv, acc_proj, (ga_mine, ga_other))
        pack_vec(sums, (ga_mine, ga_other), shards)


def whole(shape):
    zeros = (0,) * len(shape)
    return pl.BlockSpec(shape, lambda i, *_: zeros, pipeline_mode=pl.Buffered(1))


def whole_out(shape):
    zeros = (0,) * len(shape)
    return pl.BlockSpec(shape, lambda i, *_: zeros)


def by_group(shape):
    rest = (0,) * (len(shape) - 1)
    return pl.BlockSpec((GROUP, *shape[1:]), lambda i, *_: (i, *rest))


def by_group_of_core(shape, steps):
    rest = (0,) * (len(shape) - 1)
    return pl.BlockSpec((GROUP, *shape[1:]), lambda i, core: (core[0] * steps + i, *rest))


def call(kernel, steps, core, args, in_specs, outs, out_specs, scratch, flops, name):
    moved = sum(a.size * a.dtype.itemsize for a in args)
    moved += sum(o.size * o.dtype.itemsize for o in outs)
    return pl.pallas_call(
        kernel,
        out_shape=outs,
        grid_spec=pltpu.PrefetchScalarGridSpec(
            num_scalar_prefetch=0 if core is None else 1,
            grid=(steps,),
            in_specs=in_specs,
            out_specs=out_specs,
            scratch_shapes=[pltpu.VMEM(s, d) for s, d in scratch],
        ),
        compiler_params=pltpu.CompilerParams(vmem_limit_bytes=VMEM_LIMIT),
        cost_estimate=pl.CostEstimate(flops=int(flops), bytes_accessed=int(moved), transcendentals=0),
        name=name,
    )(*(() if core is None else (core,)), *args)


def arr(shape, dtype):
    return jax.ShapeDtypeStruct(shape, dtype)


def bit_groups(shards):
    bits = [1 << k for k in range(shards.bit_length() - 1)]
    groups = [bits[k : k + 2] for k in range(0, len(bits), 2)]
    return groups[::-1]


def masks_of(group):
    masks = [0]
    for b in group:
        masks = masks + [m | b for m in masks]
    return masks


def exchange(x, mask, shards):
    return lax.ppermute(x, "shard", [(i, i ^ mask) for i in range(shards)])


def swap_cores(x):
    return lax.ppermute(x, "tensor", [(0, 1), (1, 0)])


def gather_rows(x, shards):
    me = lax.axis_index("shard")
    lead = ()
    x = x[None]
    for group in bit_groups(shards):
        masks = masks_of(group)
        got = [x if m == 0 else exchange(x, m, shards) for m in masks]
        for k, b in enumerate(group):
            flag = (me & b) != 0
            got = [jnp.where(flag, got[i ^ (1 << k)], got[i]) for i in range(len(got))]
        x = jnp.stack(got, 1).reshape(-1, *x.shape[1:])
    return x.reshape(-1, x.shape[-1])


def scatter_sum(mine, other, shards):
    me = lax.axis_index("shard")
    width = mine.shape[0] // shards
    h = mine.astype(f32) + swap_cores(other).astype(f32)
    h = h.astype(bf16).reshape(shards, width, -1)
    groups = bit_groups(shards)[::-1]
    for n, group in enumerate(groups):
        masks = masks_of(group)
        count = len(masks)
        h = h.reshape(-1, count, *h.shape[1:])
        here = (me // group[0]) % count
        total = lax.dynamic_index_in_dim(h, here, 1, keepdims=False).astype(f32)
        for k, m in enumerate(masks[1:], 1):
            piece = lax.dynamic_index_in_dim(h, here ^ k, 1, keepdims=False)
            total = total + exchange(piece, m, shards).astype(f32)
        h = total if n == len(groups) - 1 else total.astype(bf16)
    return h.reshape(width, -1)


def body(
    tokens, cotangent, ln1_gain, ln1_bias, w_qkv, b_qv, w_proj, b_proj,
    ln2_gain, ln2_bias, w_up, b_up, w_down, b_down, *, shards,
):
    images_all, length, width = tokens.shape
    layers = ln1_gain.shape[0]
    per = ln1_gain.shape[1]
    images = images_all // 2
    steps = images // GROUP
    rows = -(-length // 16) * 16
    hidden = 2 * w_up.shape[2]
    heads = width // HEAD
    t = lax.axis_index("tensor")
    core = t.astype(jnp.int32).reshape(1)

    packed_a, packed_m = [], []
    for l in range(layers):
        columns = [ln1_gain[l], ln1_bias[l], b_proj[l], ln2_gain[l], ln2_bias[l], b_down[l]]
        columns += [b_qv[l].reshape(per), *b_up[l].reshape(2, per)]
        vec = jnp.stack(columns, 1)
        vec = jnp.pad(vec, ((0, 0), (0, LANES - vec.shape[1])))
        packed_a.append(
            jnp.concatenate(
                [w_qkv[l].reshape(per, -1), w_proj[l].reshape(-1, per).T, vec], axis=1
            )
        )
        packed_m.append(jnp.concatenate([w_up[l], w_down[l].T], axis=1))

    ca, cm = packed_a[0].shape[1], packed_m[0].shape[1]

    def gathered(x):
        mine = gather_rows(x, shards)
        return mine, swap_cores(mine)

    wa = [None] * layers
    wm = [None] * layers
    wa[0] = gathered(packed_a[0])
    wm[0] = gathered(packed_m[0])
    both = gather_rows(jnp.concatenate([packed_a[1], packed_m[1]], 1), shards)
    both_other = swap_cores(both)
    wa[1] = (both[:, :ca], both_other[:, :ca])
    wm[1] = (both[:, ca:], both_other[:, ca:])

    tok = images * length
    proj_flops = 2 * tok * width
    attn_flops = images * heads * 4 * length * length * HEAD
    aspec, mspec = whole((width, ca)), whole((width, cm))
    table_shape = (16, hidden)
    tspec = whole(table_shape)
    half_shape = (images, length, width)
    pad_shape = (images, rows, width)
    qkv_shape = (images, rows, 3 * width)
    p_shape = (images, heads, rows, rows)
    g_shape = (images, rows, hidden)

    def g_of(shape):
        return (GROUP, *shape[1:])

    qkv, p_all, o_all, mid, table = call(
        functools.partial(kernel_attn_forward, shards), steps, core,
        (tokens, *wa[0]),
        [by_group_of_core(tokens.shape, steps), aspec, aspec],
        [arr(qkv_shape, bf16), arr(p_shape, bf16), arr(pad_shape, bf16), arr(pad_shape, f32), arr(table_shape, f32)],
        [by_group(qkv_shape), by_group(p_shape), by_group(pad_shape), by_group(pad_shape), whole_out(table_shape)],
        [(g_of(pad_shape), f32), ((width, 3 * width), bf16), ((width, width), bf16)],
        4 * proj_flops * width + attn_flops, "attn_forward",
    )
    stream, g_all, slope_all = call(
        kernel_mlp_forward, steps, None,
        (mid, table, *wm[0]),
        [by_group(pad_shape), tspec, mspec, mspec],
        [arr(pad_shape, f32), arr(g_shape, bf16), arr(g_shape, bf16)],
        [by_group(pad_shape), by_group(g_shape), by_group(g_shape)],
        [], 2 * proj_flops * hidden, "mlp_forward",
    )
    out, e, ga_mine, ga_other, gm_mine, gm_other = call(
        functools.partial(kernel_layer_both, shards), steps, core,
        (stream, cotangent, *wa[1], *wm[1]),
        [by_group(pad_shape), by_group_of_core(tokens.shape, steps), aspec, aspec, mspec, mspec],
        [arr(half_shape, bf16), arr(pad_shape, f32)] + [arr((width, ca), bf16)] * 2 + [arr((width, cm), bf16)] * 2,
        [by_group(half_shape), by_group(pad_shape)] + [whole_out((width, ca))] * 2 + [whole_out((width, cm))] * 2,
        [
            (table_shape, f32), (table_shape, f32), ((width, 3 * width), bf16), ((width, width), bf16),
            (g_of(qkv_shape), bf16), (g_of(p_shape), bf16), (g_of(pad_shape), bf16), (g_of(pad_shape), f32),
            (g_of(g_shape), bf16), (g_of(g_shape), bf16), (g_of(pad_shape), f32), (g_of(qkv_shape), bf16),
            ((width, 3 * width), f32), ((width, width), f32), ((width, hidden), f32), ((width, hidden), f32),
        ],
        3 * (4 * proj_flops * width + 2 * proj_flops * hidden) + 3.5 * attn_flops, "layer_both",
    )
    sums_1a = scatter_sum(ga_mine, ga_other, shards)
    sums_1m = scatter_sum(gm_mine, gm_other, shards)
    out_other = swap_cores(out)
    dmid, sums, gm_mine, gm_other = call(
        kernel_mlp_backward, steps, None,
        (e, mid, table, g_all, slope_all, *wm[0]),
        [by_group(pad_shape), by_group(pad_shape), tspec, by_group(g_shape), by_group(g_shape), mspec, mspec],
        [arr(pad_shape, f32), arr(table_shape, f32)] + [arr((width, cm), bf16)] * 2,
        [by_group(pad_shape), whole_out(table_shape)] + [whole_out((width, cm))] * 2,
        [((width, hidden), f32), ((width, hidden), f32)],
        4 * proj_flops * hidden, "mlp_backward",
    )
    sums_0m = scatter_sum(gm_mine, gm_other, shards)
    grad, ga_mine, ga_other = call(
        functools.partial(kernel_attn_backward, shards), steps, core,
        (dmid, tokens, table, sums, qkv, p_all, o_all, *wa[0]),
        [by_group(pad_shape), by_group_of_core(tokens.shape, steps), tspec, tspec, by_group(qkv_shape),
         by_group(p_shape), by_group(pad_shape), aspec, aspec],
        [arr(half_shape, bf16)] + [arr((width, ca), bf16)] * 2,
        [by_group(half_shape)] + [whole_out((width, ca))] * 2,
        [
            (table_shape, f32), (g_of(pad_shape), f32), ((width, 3 * width), bf16), ((width, width), bf16),
            (g_of(qkv_shape), bf16), ((width, 3 * width), f32), ((width, width), f32),
        ],
        8 * proj_flops * width + 2.5 * attn_flops, "attn_backward",
    )
    sums_0a = scatter_sum(ga_mine, ga_other, shards)
    grad_other = swap_cores(grad)

    def both_halves(mine, other):
        return jnp.where(t == 0, jnp.concatenate([mine, other]), jnp.concatenate([other, mine]))

    sa = jnp.stack([sums_0a, sums_1a])
    sm = jnp.stack([sums_0m, sums_1m])
    half = width // 2
    vec = sa[:, :, 4 * half :]
    return (
        both_halves(out, out_other),
        both_halves(grad, grad_other).astype(f32),
        vec[:, :, 0],
        vec[:, :, 1],
        sa[:, :, : 3 * half].reshape(w_qkv.shape),
        vec[:, :, 6].reshape(b_qv.shape),
        jnp.swapaxes(sa[:, :, 3 * half : 4 * half], 1, 2).reshape(w_proj.shape),
        vec[:, :, 2],
        vec[:, :, 3],
        vec[:, :, 4],
        sm[:, :, : hidden // 2],
        jnp.swapaxes(vec[:, :, 7:9], 1, 2).reshape(b_up.shape),
        jnp.swapaxes(sm[:, :, hidden // 2 :], 1, 2),
        vec[:, :, 5],
    )


def solution(mesh):
    args = (
        P("shard", None, None),
        P("shard", None, None),
        P(None, "shard"),
        P(None, "shard"),
        P(None, "shard", None, "tensor", None),
        P(None, None, "tensor", "shard"),
        P(None, "tensor", None, "shard"),
        P(None, "shard"),
        P(None, "shard"),
        P(None, "shard"),
        P(None, "shard", "tensor"),
        P(None, "tensor", "shard"),
        P(None, "tensor", "shard"),
        P(None, "shard"),
    )
    return jax.shard_map(
        functools.partial(body, shards=mesh.shape["shard"]),
        mesh=mesh,
        in_specs=args,
        out_specs=args,
        check_vma=False,
    )
```

```python
import functools

import jax
import jax.numpy as jnp
from jax import lax
from jax.experimental import pallas as pl
from jax.experimental.pallas import tpu as pltpu
from jax.sharding import PartitionSpec as P

bf16, f32 = jnp.bfloat16, jnp.float32
epsilon = 1e-06
inv_root_two = 0.7071067811865476
inv_root_two_pi = 0.3989422804014327
log2_e = 1.4426950408889634
NN, NT, TN = ((1,), (0,)), ((1,), (1,)), ((0,), (0,))
VMEM_LIMIT = 60 * 2**20
GROUP = 2
HEAD = 64
LANES = 128


def dot(a, b, dims):
    return lax.dot_general(a, b, (dims, ((), ())), preferred_element_type=f32)


QV_AT, UP_AT = 16, 24


def qv_places(width, shards, half):
    per, unit, span = width // shards, HEAD // shards, width // 2
    m = lax.broadcasted_iota(jnp.int32, (1, 3 * width), 1)
    part, within = m // width, m % width
    head, place = (within % span) // HEAD, within % HEAD
    row = (place // unit) * per + (part // 2) * (span // HEAD) + head
    row = jnp.where((part != 1) & (within // span == half), row, -1)
    lane = lax.broadcasted_iota(jnp.int32, (LANES, 3 * width), 0)
    return row, jnp.where(lane == QV_AT + place % unit, 1.0, 0.0).astype(bf16)


def up_places(width, shards, half_hidden):
    per, unit = width // shards, LANES // shards
    m = lax.broadcasted_iota(jnp.int32, (1, half_hidden), 1)
    row = ((m % LANES) // unit) * per + m // LANES
    lane = lax.broadcasted_iota(jnp.int32, (LANES, half_hidden), 0)
    return row, jnp.where(lane == UP_AT + m % unit, 1.0, 0.0).astype(bf16)


def at_row(row, values):
    n = lax.broadcasted_iota(jnp.int32, values.shape, 0)
    return jnp.where(n == row, values, 0.0)


def unit_rows(rows, columns):
    r = lax.broadcasted_iota(jnp.int32, (rows, columns), 0)
    c = lax.broadcasted_iota(jnp.int32, (rows, columns), 1)
    return jnp.where(r == c, 1.0, 0.0).astype(bf16)


def expand_vec(vec_refs, table, shards):
    width = vec_refs[0].shape[0]
    half_hidden = table.shape[1] // 2
    table[...] = jnp.zeros_like(table)
    up_row, up_pick = up_places(width, shards, half_hidden)
    qkv = None
    for half, ref in enumerate(vec_refs):
        block = ref[...]
        if half == 0:
            table[0:6, 0:width] = dot(unit_rows(16, LANES), block, NT)[0:6]
        qv_row, qv_pick = qv_places(width, shards, half)
        placed = row_sum(at_row(qv_row, dot(block, qv_pick, NN)))
        qkv = placed if qkv is None else qkv + placed
        at = half * half_hidden
        table[7:8, at : at + half_hidden] = row_sum(at_row(up_row, dot(block, up_pick, NN)))
    table[6:7, 0 : 3 * width] = qkv


def pack_vec(table, outs, shards):
    width = outs[0].shape[0]
    half_hidden = table.shape[1] // 2
    index = lax.broadcasted_iota(jnp.int32, (16, width), 0)
    rows = jnp.where(index < 6, table[0:16, :width], 0.0).astype(bf16)
    six = dot(rows, unit_rows(16, LANES), TN)
    up_row, up_pick = up_places(width, shards, half_hidden)
    for half, ref in enumerate(outs):
        qv_row, qv_pick = qv_places(width, shards, half)
        qkv = jnp.broadcast_to(table[6:7, : 3 * width], (width, 3 * width))
        block = six + dot(at_row(qv_row, qkv).astype(bf16), qv_pick, NT)
        at = half * half_hidden
        ups = jnp.broadcast_to(table[7:8, at : at + half_hidden], (width, half_hidden))
        block = block + dot(at_row(up_row, ups).astype(bf16), up_pick, NT)
        ref[...] = block.astype(bf16)


def kernel_pack(
    ln1_gain, ln1_bias, b_proj, ln2_gain, ln2_bias, b_down, w_qkv, b_qv, w_proj, w_up, b_up, w_down,
    first_attn, first_mlp, rest, rows, vec,
):
    layers, parts, heads, per, _ = w_qkv.shape
    half = heads * HEAD
    ca, cm = first_attn.shape[1], first_mlp.shape[1]
    for l in range(layers):
        attn = first_attn if l == 0 else rest.at[:, :ca]
        mlp = first_mlp if l == 0 else rest.at[:, ca:]
        for h in range(heads):
            for part in range(parts):
                at = part * half + h * HEAD
                attn[:, at : at + HEAD] = w_qkv[l, part, h]
            at = parts * half + h * HEAD
            attn[:, at : at + HEAD] = w_proj[l, h]
        rows[...] = jnp.zeros_like(rows)
        for j, ref in enumerate((ln1_gain, ln1_bias, b_proj, ln2_gain, ln2_bias, b_down)):
            rows[j : j + 1, :per] = ref[l : l + 1, :].astype(f32)
        vec[...] = jnp.zeros_like(vec)
        vec[:, 0:16] = dot(unit_rows(per, LANES), rows[...].astype(bf16), NT)
        unit = b_qv.shape[3]
        for h in range(heads):
            for part in range(2):
                r = part * heads + h
                vec[r : r + 1, QV_AT : QV_AT + unit] = b_qv[l, h, part : part + 1, :].astype(f32)
        unit = b_up.shape[2]
        for r in range(b_up.shape[0]):
            vec[r : r + 1, UP_AT : UP_AT + unit] = b_up[r, l : l + 1, :].astype(f32)
        attn[:, ca - LANES :] = vec[...].astype(bf16)
        mlp[:, : cm // 2] = w_up[l]
        mlp[:, cm // 2 :] = w_down[l]


def kernel_unpack(count, *refs):
    pieces, outs = refs[: 3 * count], refs[3 * count :]
    sixes, (w_qkv, b_qv, w_proj, w_up, b_up, w_down) = outs[:6], outs[6:]
    layers, parts, heads, per, _ = w_qkv.shape
    half = heads * HEAD
    hidden = w_up.shape[2]

    def total(group, cols):
        found = [ref[:, cols].astype(f32) for ref in pieces[group * count : (group + 1) * count]]
        return functools.reduce(lambda a, b: a + b, found)

    ca = parts * half + half + LANES
    for l in range(layers):
        attn, mlp, base = (0, 1, 0) if l == 0 else (2, 2, ca)
        whole_attn = total(attn, slice(0, ca))
        for h in range(heads):
            for part in range(parts):
                at = part * half + h * HEAD
                w_qkv[l, part, h] = whole_attn[:, at : at + HEAD]
            at = parts * half + h * HEAD
            w_proj[l, h] = whole_attn[:, at : at + HEAD]
        vec = whole_attn[:, ca - LANES :]
        columns = vec.T
        for j, ref in enumerate(sixes):
            ref[l : l + 1, :] = columns[j : j + 1, :per]
        unit = b_qv.shape[3]
        for h in range(heads):
            for part in range(2):
                r = part * heads + h
                b_qv[l, h, part : part + 1, :] = vec[r : r + 1, QV_AT : QV_AT + unit]
        unit = b_up.shape[2]
        for r in range(b_up.shape[0]):
            b_up[r, l : l + 1, :] = vec[r : r + 1, UP_AT : UP_AT + unit]
        w_up[l] = total(mlp, slice(base, base + hidden))
        w_down[l] = total(mlp, slice(base + hidden, base + 2 * hidden))


def norm_parts(x):
    c = x - jnp.mean(x, -1, keepdims=True)
    s = lax.rsqrt(jnp.mean(c * c, -1, keepdims=True) + epsilon)
    return c * s, s


def norm_back(dh, u, s, gain):
    t = dh * gain
    return s * (t - jnp.mean(t, -1, keepdims=True) - u * jnp.mean(t * u, -1, keepdims=True))


def row_sum(x):
    return jnp.sum(x, 0, keepdims=True)


def halves_of_lanes(x):
    low = lax.broadcasted_iota(jnp.int32, x.shape, 1) < HEAD
    zero = jnp.zeros_like(x)
    return jnp.where(low, x, zero), jnp.where(low, zero, x)


def probs_t(scores, length):
    row = lax.broadcasted_iota(jnp.int32, scores.shape, 0)
    scores = jnp.where(row < length, scores, -1e30)
    high = jnp.max(scores, 0, keepdims=True)
    e = jnp.exp2((scores - high) * (HEAD**-0.5 * log2_e))
    return (e * (1.0 / jnp.sum(e, 0, keepdims=True))).astype(bf16)


def pair(qkv, width, at):
    return [qkv[:, part * width + at : part * width + at + LANES] for part in range(3)]


def attention(qkv, p_ref, o_ref, width, length):
    for j in range(width // LANES):
        at = LANES * j
        q, k, v = pair(qkv, width, at)
        out = None
        for h, (q_one, v_one) in enumerate(zip(halves_of_lanes(q), halves_of_lanes(v))):
            p = probs_t(dot(k, q_one, NT), length)
            p_ref[2 * j + h] = p
            one = dot(p, v_one, TN)
            out = one if out is None else out + one
        o_ref[:, at : at + LANES] = out.astype(bf16)


def attention_back(qkv, p_ref, do, dz_ref, width):
    for j in range(width // LANES):
        at = LANES * j
        q, k, v = pair(qkv, width, at)
        do_pair = do[:, at : at + LANES]
        sums = [None] * 3
        split = zip(*(halves_of_lanes(x) for x in (q, k, v, do_pair)))
        for h, (q_one, k_one, v_one, do_one) in enumerate(split):
            p = p_ref[2 * j + h]
            pf = p.astype(f32)
            t = pf * dot(v_one, do_pair, NT)
            ds = ((t - pf * row_sum(t)) * HEAD**-0.5).astype(bf16)
            found = (dot(ds, k_one, TN), dot(ds, q_one, NN), dot(p, do_one, NN))
            sums = [x if y is None else x + y for x, y in zip(found, sums)]
        for part in range(3):
            dz_ref[:, part * width + at : part * width + at + LANES] = sums[part].astype(bf16)


def place_attn_weights(a_refs, w_qkv, w_proj):
    width = w_qkv.shape[0]
    half = width // 2
    for i, ref in enumerate(a_refs):
        for part in range(3):
            to = part * width + i * half
            w_qkv[:, to : to + half] = ref[:, part * half : (part + 1) * half]
        w_proj[:, i * half : (i + 1) * half] = ref[:, 3 * half : 4 * half]


def store_attn_grads(acc_qkv, acc_proj, outs):
    width = acc_qkv.shape[0]
    half = width // 2
    for i, ref in enumerate(outs):
        for part in range(3):
            at = part * width + i * half
            ref[:, part * half : (part + 1) * half] = acc_qkv[:, at : at + half].astype(bf16)
        ref[:, 3 * half : 4 * half] = acc_proj[:, i * half : (i + 1) * half].astype(bf16)


def store_mlp_grads(acc_up, acc_down, outs):
    half = acc_up.shape[1] // 2
    for i, ref in enumerate(outs):
        ref[:, :half] = acc_up[:, i * half : (i + 1) * half].astype(bf16)
        ref[:, half:] = acc_down[:, i * half : (i + 1) * half].astype(bf16)


def attn_forward(x, table, w_qkv, w_proj, qkv, p_all, o_all, mid, length):
    group, rows, width = x.shape
    gain, shift = table[0:1, :width], table[1:2, :width]
    xs = x[...].reshape(group * rows, width)
    u, _ = norm_parts(xs)
    h = (u * gain + shift).astype(bf16)
    z = dot(h, w_qkv[...], NN) + table[6:7, : 3 * width]
    qkv[...] = z.astype(bf16).reshape(qkv.shape)
    for g in range(group):
        attention(qkv.at[g], p_all.at[g], o_all.at[g], width, length)
    o = o_all[...].reshape(group * rows, width)
    a = dot(o, w_proj[...], NT)
    mid[...] = (xs + a + table[2:3, :width]).reshape(mid.shape)


def mlp_forward(mid, table, m_refs, g_all, slope_all):
    group, rows, width = mid.shape
    ms = mid[...].reshape(group * rows, width)
    u, _ = norm_parts(ms)
    h = (u * table[3:4, :width] + table[4:5, :width]).astype(bf16)
    half = m_refs[0].shape[1] // 2
    total = None
    for i, ref in enumerate(m_refs):
        cols = slice(i * half, (i + 1) * half)
        pre = dot(h, ref[:, :half], NN) + table[7:8, cols]
        phi = 0.5 * (1.0 + lax.erf(pre * inv_root_two))
        g = (pre * phi).astype(bf16)
        g_all[:, :, cols] = g.reshape(group, rows, half)
        slope = phi + pre * jnp.exp(-0.5 * pre * pre) * inv_root_two_pi
        slope_all[:, :, cols] = slope.astype(bf16).reshape(group, rows, half)
        t = dot(g, ref[:, half:], NT)
        total = t if total is None else total + t
    return ms + total + table[5:6, :width]


def mlp_backward(e, mid, table, sums, m_refs, g_all, slope_all, acc_up, acc_down):
    group, rows, width = mid.shape
    half = m_refs[0].shape[1] // 2
    sums[5:6, :width] += row_sum(e)
    e_low = e.astype(bf16)
    u, s = norm_parts(mid[...].reshape(group * rows, width))
    gain = table[3:4, :width]
    h = (u * gain + table[4:5, :width]).astype(bf16)
    dh = None
    for i, ref in enumerate(m_refs):
        cols = slice(i * half, (i + 1) * half)
        dg = dot(e_low, ref[:, half:], NN)
        slope = slope_all[:, :, cols].reshape(group * rows, half).astype(f32)
        dpre = (dg * slope).astype(bf16)
        sums[7:8, cols] += row_sum(dpre.astype(f32))
        acc_up[:, cols] += dot(h, dpre, TN)
        acc_down[:, cols] += dot(e_low, g_all[:, :, cols].reshape(group * rows, half), TN)
        t = dot(dpre, ref[:, :half], NT)
        dh = t if dh is None else dh + t
    sums[3:4, :width] += row_sum(dh * u)
    sums[4:5, :width] += row_sum(dh)
    return e + norm_back(dh, u, s, gain)


def attn_backward(dmid, x, table, sums, w_qkv, w_proj, qkv, p_all, o_all, dz, acc_qkv, acc_proj):
    group, rows, width = x.shape
    sums[2:3, :width] += row_sum(dmid)
    da = dmid.astype(bf16)
    acc_proj[...] += dot(da, o_all[...].reshape(group * rows, width), TN)
    do = dot(da, w_proj[...], NN).astype(bf16)
    for g in range(group):
        attention_back(qkv.at[g], p_all.at[g], do[g * rows : (g + 1) * rows], dz.at[g], width)
    dzs = dz[...].reshape(group * rows, 3 * width)
    sums[6:7, : 3 * width] += row_sum(dzs.astype(f32))
    u, s = norm_parts(x[...].reshape(group * rows, width))
    gain = table[0:1, :width]
    h = (u * gain + table[1:2, :width]).astype(bf16)
    acc_qkv[...] += dot(h, dzs, TN)
    dh = dot(dzs, w_qkv[...], NT)
    sums[0:1, :width] += row_sum(dh * u)
    sums[1:2, :width] += row_sum(dh)
    return dmid + norm_back(dh, u, s, gain)


def spread_images(ref, flat):
    for j in range(flat.shape[0]):
        part = ref[:, :, j * LANES : (j + 1) * LANES]
        flat[j] = part.astype(f32).reshape(flat.shape[1:])


def image_rows(image, images, length):
    return pl.ds(image, length, stride=images)


def load_images(flat, x, images, length):
    step = pl.program_id(0)

    @pl.when(step == 0)
    def _():
        x[...] = jnp.zeros_like(x)

    for g in range(x.shape[0]):
        for j in range(flat.shape[0]):
            found = flat[j, image_rows(step * x.shape[0] + g, images, length), :]
            x[g, :length, j * LANES : (j + 1) * LANES] = found


def store_images(value, flat, out, rows, also):
    step = pl.program_id(0)
    length, images, _ = out.shape
    group = value.shape[0] // rows
    for g in range(group):
        for j in range(flat.shape[0]):
            part = value[g * rows : g * rows + length, j * LANES : (j + 1) * LANES]
            flat[j, image_rows(step * group + g, images, length), :] = part

    @pl.when(step == pl.num_programs(0) - 1)
    def _():
        for j in range(flat.shape[0]):
            part = flat[j].reshape(length, images, LANES)
            part = part.astype(out.dtype)
            out[:, :, j * LANES : (j + 1) * LANES] = part
            also[:, :, j * LANES : (j + 1) * LANES] = part.astype(also.dtype)


def kernel_fill(core, half, full_in, full):
    full[...] = half[...].astype(full.dtype)


def vec_of(ref):
    return ref.at[:, ref.shape[1] - LANES :]


def kernel_attn_forward(
    shards, core, tok, a_mine, a_other, x_all, qkv, p_all, o_all, mid, table, flat, x, w_qkv, w_proj
):
    @pl.when(pl.program_id(0) == 0)
    def _():
        place_attn_weights((a_mine, a_other), w_qkv, w_proj)
        expand_vec([vec_of(r) for r in (a_mine, a_other)], table, shards)
        spread_images(tok, flat)

    length, images, _ = tok.shape
    load_images(flat, x, images, length)
    x_all[...] = x[...].astype(bf16)
    attn_forward(x, table, w_qkv, w_proj, qkv, p_all, o_all, mid, length)


def kernel_mlp_forward(mid, table, m_mine, m_other, stream, g_all, slope_all):
    out = mlp_forward(mid, table, (m_mine, m_other), g_all, slope_all)
    stream[...] = out.reshape(stream.shape)


def kernel_layer_both(
    shards, ca, core, x, cot, w_mine, w_other,
    out, out_full, e_out, g_mine, g_other,
    table, sums, w_qkv, w_proj, qkv, p_all, o_all, mid, g_all, slope_all, flat_in, flat_out, e, dz,
    acc_qkv, acc_proj, acc_up, acc_down,
):
    step = pl.program_id(0)
    width = w_qkv.shape[0]
    a_refs = [r.at[:, :ca] for r in (w_mine, w_other)]
    m_refs = [r.at[:, ca:] for r in (w_mine, w_other)]

    @pl.when(step == 0)
    def _():
        place_attn_weights(a_refs, w_qkv, w_proj)
        expand_vec([vec_of(r) for r in a_refs], table, shards)
        spread_images(cot, flat_in)
        for ref in (sums, acc_qkv, acc_proj, acc_up, acc_down):
            ref[...] = jnp.zeros_like(ref)

    length, images, _ = cot.shape
    group, rows, _ = x.shape
    load_images(flat_in, e, images, length)
    attn_forward(x, table, w_qkv, w_proj, qkv, p_all, o_all, mid, length)
    result = mlp_forward(mid, table, m_refs, g_all, slope_all)
    store_images(result, flat_out, out, rows, out_full)
    dmid = mlp_backward(
        e[...].reshape(group * rows, width), mid, table, sums, m_refs, g_all, slope_all, acc_up, acc_down
    )
    back = attn_backward(
        dmid, x, table, sums, w_qkv, w_proj, qkv, p_all, o_all, dz, acc_qkv, acc_proj
    )
    e_out[...] = back.reshape(e_out.shape)

    @pl.when(step == pl.num_programs(0) - 1)
    def _():
        ga = [r.at[:, :ca] for r in (g_mine, g_other)]
        store_attn_grads(acc_qkv, acc_proj, ga)
        store_mlp_grads(acc_up, acc_down, [r.at[:, ca:] for r in (g_mine, g_other)])
        pack_vec(sums, [vec_of(r) for r in ga], shards)


def kernel_mlp_backward(
    e, mid, table, g_all, slope_all, m_mine, m_other,
    dmid, sums, gm_mine, gm_other, acc_up, acc_down,
):
    step = pl.program_id(0)

    @pl.when(step == 0)
    def _():
        for ref in (sums, acc_up, acc_down):
            ref[...] = jnp.zeros_like(ref)

    group, rows, width = mid.shape
    back = mlp_backward(
        e[...].reshape(group * rows, width), mid, table, sums, (m_mine, m_other),
        g_all, slope_all, acc_up, acc_down,
    )
    dmid[...] = back.reshape(dmid.shape)

    @pl.when(step == pl.num_programs(0) - 1)
    def _():
        store_mlp_grads(acc_up, acc_down, (gm_mine, gm_other))


def kernel_attn_backward(
    shards, core, dmid, x_all, table, sums_in, qkv, p_all, o_all, a_mine, a_other,
    grad, grad_full, ga_mine, ga_other, sums, flat, x, w_qkv, w_proj, dz, acc_qkv, acc_proj,
):
    step = pl.program_id(0)

    @pl.when(step == 0)
    def _():
        place_attn_weights((a_mine, a_other), w_qkv, w_proj)
        sums[...] = sums_in[...]
        for ref in (acc_qkv, acc_proj):
            ref[...] = jnp.zeros_like(ref)

    x[...] = x_all[...].astype(f32)
    group, rows, width = x.shape
    back = attn_backward(
        dmid[...].reshape(group * rows, width), x, table, sums, w_qkv, w_proj,
        qkv, p_all, o_all, dz, acc_qkv, acc_proj,
    )
    store_images(back, flat, grad, rows, grad_full)

    @pl.when(step == pl.num_programs(0) - 1)
    def _():
        store_attn_grads(acc_qkv, acc_proj, (ga_mine, ga_other))
        pack_vec(sums, [vec_of(r) for r in (ga_mine, ga_other)], shards)


def whole(shape):
    zeros = (0,) * len(shape)
    return pl.BlockSpec(shape, lambda i, *_: zeros, pipeline_mode=pl.Buffered(1))


def whole_out(shape):
    zeros = (0,) * len(shape)
    return pl.BlockSpec(shape, lambda i, *_: zeros)


def by_group(shape):
    rest = (0,) * (len(shape) - 1)
    return pl.BlockSpec((GROUP, *shape[1:]), lambda i, *_: (i, *rest))


def of_core(shape):
    return pl.BlockSpec(
        (shape[0], shape[1] // 2, shape[2]), lambda i, core: (0, core[0], 0), pipeline_mode=pl.Buffered(1)
    )


def call(kernel, steps, core, args, in_specs, outs, out_specs, scratch, flops, name):
    moved = sum(a.size * a.dtype.itemsize for a in args)
    moved += sum(o.size * o.dtype.itemsize for o in outs)
    return pl.pallas_call(
        kernel,
        out_shape=outs,
        grid_spec=pltpu.PrefetchScalarGridSpec(
            num_scalar_prefetch=0 if core is None else 1,
            grid=(steps,),
            in_specs=in_specs,
            out_specs=out_specs,
            scratch_shapes=[pltpu.VMEM(s, d) for s, d in scratch],
        ),
        compiler_params=pltpu.CompilerParams(vmem_limit_bytes=VMEM_LIMIT),
        cost_estimate=pl.CostEstimate(flops=int(flops), bytes_accessed=int(moved), transcendentals=0),
        name=name,
    )(*(() if core is None else (core,)), *args)


def fill_other(core, half, full):
    length, images, width = half.shape
    steps = 1
    return pl.pallas_call(
        kernel_fill,
        out_shape=arr(full.shape, full.dtype),
        grid_spec=pltpu.PrefetchScalarGridSpec(
            num_scalar_prefetch=1,
            grid=(steps,),
            in_specs=[
                pl.BlockSpec((length // steps, images, width), lambda i, core: (i, 0, 0)),
                pl.BlockSpec(memory_space=pl.ANY),
            ],
            out_specs=pl.BlockSpec((length // steps, images, width), lambda i, core: (i, 1 - core[0], 0)),
        ),
        input_output_aliases={2: 0},
        compiler_params=pltpu.CompilerParams(vmem_limit_bytes=VMEM_LIMIT),
        name="fill_other",
    )(core, half, full)


def in_vmem(kernel, args, outs, scratch, name):
    spec = pl.BlockSpec(memory_space=pltpu.VMEM)
    return pl.pallas_call(
        kernel,
        out_shape=outs,
        in_specs=[spec] * len(args),
        out_specs=[spec] * len(outs),
        scratch_shapes=[pltpu.VMEM(s, d) for s, d in scratch],
        compiler_params=pltpu.CompilerParams(vmem_limit_bytes=VMEM_LIMIT),
        name=name,
    )(*args)


def arr(shape, dtype):
    return jax.ShapeDtypeStruct(shape, dtype)


def after(x, *others):
    return lax.optimization_barrier((x, *others))[0]


def after_all(xs, *others):
    return list(lax.optimization_barrier((*xs, *others))[: len(xs)])


def bit_groups(shards):
    bits = [1 << k for k in range(shards.bit_length() - 1)]
    groups = [bits[k : k + 2] for k in range(0, len(bits), 2)]
    return groups[::-1]


def masks_of(group):
    masks = [0]
    for b in group:
        masks = masks + [m | b for m in masks]
    return masks


def exchange(x, mask, shards):
    return lax.ppermute(x, "shard", [(i, i ^ mask) for i in range(shards)])


def swap_cores(x):
    return lax.ppermute(x, "tensor", [(0, 1), (1, 0)])


def fetch(x, group, shards):
    return [x if m == 0 else exchange(x, m, shards) for m in masks_of(group)]


def in_order(got, group):
    me = lax.axis_index("shard")
    for k, b in enumerate(group):
        flag = (me & b) != 0
        got = [jnp.where(flag, got[i ^ (1 << k)], got[i]) for i in range(len(got))]
    return jnp.stack(got, 1).reshape(-1, *got[0].shape[1:])


def flat_rows(x):
    return x.reshape(-1, x.shape[-1])


def pieces_for(h, group):
    count = len(masks_of(group))
    h = h.reshape(-1, count, *h.shape[1:])
    here = (lax.axis_index("shard") // group[0]) % count
    return [lax.dynamic_index_in_dim(h, here ^ k, 1, keepdims=False) for k in range(count)]


def send_pieces(pieces, group, shards):
    return [p if m == 0 else exchange(p, m, shards) for p, m in zip(pieces, masks_of(group))]


def add_up(found):
    return functools.reduce(lambda a, b: a + b, [f.astype(f32) for f in found])


def core_sum(mine, other, shards):
    h = mine.astype(f32) + swap_cores(other).astype(f32)
    return h.astype(bf16).reshape(shards, mine.shape[0] // shards, -1)


def body(
    tokens, cotangent, ln1_gain, ln1_bias, w_qkv, b_qv, w_proj, b_proj,
    ln2_gain, ln2_bias, w_up, b_up, w_down, b_down, *, shards,
):
    images_all, length, width = tokens.shape
    layers, per = ln1_gain.shape
    images = images_all // 2
    steps = images // GROUP
    rows = -(-length // 16) * 16
    hidden = 2 * w_up.shape[2]
    heads = width // HEAD
    ca, cm = 2 * width + LANES, hidden
    t = lax.axis_index("tensor")
    core = t.astype(jnp.int32).reshape(1)
    groups = bit_groups(shards)

    def turned(which):
        one = [(0, 1)] * 6 + [(0, 2, 3, 1, 4), (0, 2, 1, 3), (0, 1, 3, 2), (0, 1, 2), (1, 0, 2), (0, 2, 1)]
        back = [tuple(sorted(range(len(p)), key=lambda i: p[i])) for p in one]
        return one if which == "in" else back

    raw = (ln1_gain, ln1_bias, b_proj, ln2_gain, ln2_bias, b_down, w_qkv, b_qv, w_proj, w_up, b_up, w_down)
    raw = [x.transpose(p) for x, p in zip(raw, turned("in"))]
    first_attn, first_mlp, rest = in_vmem(
        kernel_pack, raw,
        [arr((per, ca), bf16), arr((per, cm), bf16), arr((per, ca + cm), bf16)],
        [((16, LANES), f32), ((per, LANES), f32)], "pack",
    )

    def early(x, stages):
        x = x[None]
        for group in stages:
            x = in_order(fetch(x, group, shards), group)
        return x

    last, before = groups[-1], groups[-2]
    z0 = early(first_attn, groups[:-1])
    got_a0 = fetch(z0, last, shards)
    m0 = early(after(first_mlp, z0), groups[:-1])
    a0 = flat_rows(in_order(got_a0, last))
    a0_other = swap_cores(a0)
    m0, rest = after_all((m0, rest), a0)
    got_m0 = fetch(m0, last, shards)
    got_l1 = fetch(early(rest, groups[:-2]), before, shards)

    tok = images * length
    proj_flops = 2 * tok * width
    attn_flops = images * heads * 4 * length * length * HEAD
    aspec, mspec, wspec = whole((width, ca)), whole((width, cm)), whole((width, ca + cm))
    table_shape = (16, hidden)
    tspec = whole(table_shape)
    half_shape = (length, images, width)
    flat_shape = (width // LANES, length * images, LANES)
    pad_shape = (images, rows, width)
    qkv_shape = (images, rows, 3 * width)
    p_shape = (images, heads, rows, rows)
    g_shape = (images, rows, hidden)
    tokens_in, cotangent_in = (x.transpose(1, 0, 2) for x in (tokens, cotangent))

    def g_of(shape):
        return (GROUP, *shape[1:])

    x_all, qkv, p_all, o_all, mid, table = call(
        functools.partial(kernel_attn_forward, shards), steps, core,
        (tokens_in, a0, a0_other),
        [of_core(tokens_in.shape), aspec, aspec],
        [arr(pad_shape, bf16), arr(qkv_shape, bf16), arr(p_shape, bf16), arr(pad_shape, bf16),
         arr(pad_shape, f32), arr(table_shape, f32)],
        [by_group(pad_shape), by_group(qkv_shape), by_group(p_shape), by_group(pad_shape), by_group(pad_shape),
         whole_out(table_shape)],
        [(flat_shape, f32), (g_of(pad_shape), f32), ((width, 3 * width), bf16), ((width, width), bf16)],
        4 * proj_flops * width + attn_flops, "attn_forward",
    )
    got = after_all(got_m0 + got_l1, mid)
    m0, l1 = got[: len(got_m0)], got[len(got_m0) :]
    m0 = flat_rows(in_order(m0, last))
    m0_other = swap_cores(m0)
    l1 = in_order(l1, before)
    stream, g_all, slope_all = call(
        kernel_mlp_forward, steps, None,
        (mid, table, m0, m0_other),
        [by_group(pad_shape), tspec, mspec, mspec],
        [arr(pad_shape, f32), arr(g_shape, bf16), arr(g_shape, bf16)],
        [by_group(pad_shape), by_group(g_shape), by_group(g_shape)],
        [], 2 * proj_flops * hidden, "mlp_forward",
    )
    l1 = flat_rows(in_order(after_all(fetch(l1, last, shards), stream), last))
    l1_other = swap_cores(l1)
    out, out_full, e, g1_mine, g1_other = call(
        functools.partial(kernel_layer_both, shards, ca), steps, core,
        (stream, cotangent_in, l1, l1_other),
        [by_group(pad_shape), of_core(tokens_in.shape), wspec, wspec],
        [arr(half_shape, bf16), arr(tokens_in.shape, bf16), arr(pad_shape, f32)] + [arr((width, ca + cm), bf16)] * 2,
        [whole_out(half_shape), of_core(tokens_in.shape), by_group(pad_shape)] + [whole_out((width, ca + cm))] * 2,
        [
            (table_shape, f32), (table_shape, f32), ((width, 3 * width), bf16), ((width, width), bf16),
            (g_of(qkv_shape), bf16), (g_of(p_shape), bf16), (g_of(pad_shape), bf16), (g_of(pad_shape), f32),
            (g_of(g_shape), bf16), (g_of(g_shape), bf16), (flat_shape, f32), (flat_shape, f32),
            (g_of(pad_shape), f32), (g_of(qkv_shape), bf16),
            ((width, 3 * width), f32), ((width, width), f32), ((width, hidden), f32), ((width, hidden), f32),
        ],
        3 * (4 * proj_flops * width + 2 * proj_flops * hidden) + 3.5 * attn_flops, "layer_both",
    )
    h1 = pieces_for(core_sum(g1_mine, g1_other, shards), last)
    out_other = swap_cores(out)
    e = after(e, *h1)
    dmid, sums, gm_mine, gm_other = call(
        kernel_mlp_backward, steps, None,
        (e, mid, table, g_all, slope_all, m0, m0_other),
        [by_group(pad_shape), by_group(pad_shape), tspec, by_group(g_shape), by_group(g_shape), mspec, mspec],
        [arr(pad_shape, f32), arr(table_shape, f32)] + [arr((width, cm), bf16)] * 2,
        [by_group(pad_shape), whole_out(table_shape)] + [whole_out((width, cm))] * 2,
        [((width, hidden), f32), ((width, hidden), f32)],
        4 * proj_flops * hidden, "mlp_backward",
    )
    middle = groups[:-1][::-1]
    h1 = add_up(after_all(send_pieces(h1, last, shards), dmid)).astype(bf16)
    h1 = pieces_for(h1, middle[0])
    h0m = pieces_for(core_sum(gm_mine, gm_other, shards), last)
    dmid = after(dmid, *h0m, *h1)
    grad, grad_full, ga_mine, ga_other = call(
        functools.partial(kernel_attn_backward, shards), steps, core,
        (dmid, x_all, table, sums, qkv, p_all, o_all, a0, a0_other),
        [by_group(pad_shape), by_group(pad_shape), tspec, tspec, by_group(qkv_shape),
         by_group(p_shape), by_group(pad_shape), aspec, aspec],
        [arr(half_shape, bf16), arr(tokens_in.shape, f32)] + [arr((width, ca), bf16)] * 2,
        [whole_out(half_shape), of_core(tokens_in.shape)] + [whole_out((width, ca))] * 2,
        [
            (table_shape, f32), (flat_shape, f32), (g_of(pad_shape), f32), ((width, 3 * width), bf16),
            ((width, width), bf16), (g_of(qkv_shape), bf16), ((width, 3 * width), f32), ((width, width), f32),
        ],
        8 * proj_flops * width + 2.5 * attn_flops, "attn_backward",
    )
    h0m = send_pieces(h0m, last, shards)
    h1 = send_pieces(h1, middle[0], shards)
    n = len(h0m)
    got = after_all(h0m + h1 + [ga_mine, ga_other, grad], grad)
    h0m, h1, (ga_mine, ga_other, grad) = got[:n], got[n:-3], got[-3:]
    h0a = send_pieces(pieces_for(core_sum(ga_mine, ga_other, shards), last), last, shards)
    grad_other = swap_cores(grad)
    h0m = send_pieces(pieces_for(add_up(h0m).astype(bf16), middle[0]), middle[0], shards)
    h0a = send_pieces(pieces_for(add_up(h0a).astype(bf16), middle[0]), middle[0], shards)
    for group in middle[1:]:
        h0a, h0m, h1 = (
            send_pieces(pieces_for(add_up(h).astype(bf16), group), group, shards) for h in (h0a, h0m, h1)
        )

    out_full = fill_other(core, out_other, out_full)
    grad_full = fill_other(core, grad_other, grad_full)
    h0a = after_all(h0a, out_full, grad_full)
    grads = in_vmem(
        functools.partial(kernel_unpack, len(h1)),
        [x.reshape(per, -1) for h in (h0a, h0m, h1) for x in h],
        [arr(x.shape, f32) for x in raw], [], "unpack",
    )
    grads = [g.transpose(p) for g, p in zip(grads, turned("out"))]
    g1, b1, bp, g2, b2, bd, gq, gb, gp, gu, gbu, gd = grads
    return (
        out_full.transpose(1, 0, 2), grad_full.transpose(1, 0, 2),
        g1, b1, gq, gb, gp, bp, g2, b2, gu, gbu, gd, bd,
    )


def solution(mesh):
    args = (
        P("shard", None, None),
        P("shard", None, None),
        P(None, "shard"),
        P(None, "shard"),
        P(None, "shard", None, "tensor", None),
        P(None, None, "tensor", "shard"),
        P(None, "tensor", None, "shard"),
        P(None, "shard"),
        P(None, "shard"),
        P(None, "shard"),
        P(None, "shard", "tensor"),
        P(None, "tensor", "shard"),
        P(None, "tensor", "shard"),
        P(None, "shard"),
    )
    return jax.shard_map(
        functools.partial(body, shards=mesh.shape["shard"]),
        mesh=mesh,
        in_specs=args,
        out_specs=args,
        check_vma=False,
    )
```

```python
import functools
import math

import jax
import jax.numpy as jnp
from jax import lax
from jax.experimental import pallas as pl
from jax.experimental.pallas import tpu as pltpu
from jax.sharding import PartitionSpec as P

bf16, f32 = jnp.bfloat16, jnp.float32
epsilon = 1e-06
inv_root_two = 0.7071067811865476
inv_root_two_pi = 0.3989422804014327
log2_e = 1.4426950408889634
NN, NT, TN = ((1,), (0,)), ((1,), (1,)), ((0,), (0,))
VMEM_LIMIT = 60 * 2**20
GROUP = 2
HEAD = 64
LANES = 128


def dot(a, b, dims):
    return lax.dot_general(a, b, (dims, ((), ())), preferred_element_type=f32)


QV_AT, UP_AT = 16, 24


def owner_rows(width, shards, place):
    n = lax.broadcasted_iota(jnp.int32, (width, LANES), 0)
    m = lax.broadcasted_iota(jnp.int32, (width, LANES), 1)
    per = width // shards
    return n // per == (m % place) // (place // shards)


def lane_picks(at, unit):
    r = lax.broadcasted_iota(jnp.int32, (LANES, LANES), 0)
    m = lax.broadcasted_iota(jnp.int32, (LANES, LANES), 1)
    return jnp.where(r == at + m % unit, 1.0, 0.0).astype(bf16)


def rank_rows(width, shards):
    r = lax.broadcasted_iota(jnp.int32, (16, width), 0)
    n = lax.broadcasted_iota(jnp.int32, (16, width), 1)
    return jnp.where(n % (width // shards) == r, 1.0, 0.0).astype(bf16)


def unit_rows(rows, columns):
    r = lax.broadcasted_iota(jnp.int32, (rows, columns), 0)
    c = lax.broadcasted_iota(jnp.int32, (rows, columns), 1)
    return jnp.where(r == c, 1.0, 0.0).astype(bf16)


def qv_spots(width, half):
    heads = width // HEAD // 2
    for part in range(2):
        for h in range(heads):
            yield part * heads + h, part * 2 * width + half * (width // 2) + h * HEAD


def up_spots(hidden, half):
    rows = hidden // 2 // LANES
    return [(r, (half * rows + r) * LANES) for r in range(rows)]


def expand_vec(vec_refs, table, shards):
    width, hidden = vec_refs[0].shape[0], table.shape[1]
    table[...] = jnp.zeros_like(table)
    ranks = rank_rows(width, shards)
    for half, ref in enumerate(vec_refs):
        block = ref[...]
        if half == 0:
            table[0:6, 0:width] = dot(unit_rows(16, LANES), block, NT)[0:6]
        for at, place, row, spots in (
            (QV_AT, HEAD, 6, qv_spots(width, half)),
            (UP_AT, LANES, 7, up_spots(hidden, half)),
        ):
            found = dot(block, lane_picks(at, place // shards), NN)
            found = jnp.where(owner_rows(width, shards, place), found, 0.0).astype(bf16)
            found = dot(ranks, found, NN)
            for r, first in spots:
                table[row : row + 1, first : first + place] = found[r : r + 1, :place]


def pack_vec(table, outs, rows, shards):
    width, hidden = outs[0].shape[0], table.shape[1]
    index = lax.broadcasted_iota(jnp.int32, (16, width), 0)
    six = jnp.where(index < 6, table[0:16, :width], 0.0).astype(bf16)
    six = dot(six, unit_rows(16, LANES), TN)
    ranks = rank_rows(width, shards)
    for half, ref in enumerate(outs):
        block = six
        for at, place, row, spots in (
            (QV_AT, HEAD, 6, qv_spots(width, half)),
            (UP_AT, LANES, 7, up_spots(hidden, half)),
        ):
            rows[...] = jnp.zeros_like(rows)
            for r, first in spots:
                rows[r : r + 1, :place] = table[row : row + 1, first : first + place]
            found = dot(ranks, rows[...].astype(bf16), TN)
            lane = lax.broadcasted_iota(jnp.int32, (width, LANES), 1)
            found = jnp.where(owner_rows(width, shards, place) & (lane < place), found, 0.0).astype(bf16)
            block = block + dot(found, lane_picks(at, place // shards), NT)
        ref[...] = block.astype(bf16)


def kernel_pack(
    ln1_gain, ln1_bias, b_proj, ln2_gain, ln2_bias, b_down, w_qkv, b_qv, w_proj, w_up, b_up, w_down,
    first_attn, first_mlp, later_attn, later_mlp, rows, vec,
):
    layers, parts, heads, per, _ = w_qkv.shape
    half = heads * HEAD
    ca, cm = first_attn.shape[1], first_mlp.shape[1]
    for l in range(layers):
        attn, mlp = (first_attn, first_mlp) if l == 0 else (later_attn, later_mlp)
        for h in range(heads):
            for part in range(parts):
                at = part * half + h * HEAD
                attn[:, at : at + HEAD] = w_qkv[l, part, h]
            at = parts * half + h * HEAD
            attn[:, at : at + HEAD] = w_proj[l, h]
        rows[...] = jnp.zeros_like(rows)
        for j, ref in enumerate((ln1_gain, ln1_bias, b_proj, ln2_gain, ln2_bias, b_down)):
            rows[j : j + 1, :per] = ref[l : l + 1, :].astype(f32)
        vec[...] = jnp.zeros_like(vec)
        vec[:, 0:16] = dot(unit_rows(per, LANES), rows[...].astype(bf16), NT)
        unit = b_qv.shape[3]
        for h in range(heads):
            for part in range(2):
                r = part * heads + h
                vec[r : r + 1, QV_AT : QV_AT + unit] = b_qv[l, h, part : part + 1, :].astype(f32)
        unit = b_up.shape[2]
        for r in range(b_up.shape[0]):
            vec[r : r + 1, UP_AT : UP_AT + unit] = b_up[r, l : l + 1, :].astype(f32)
        attn[:, ca - LANES :] = vec[...].astype(bf16)
        mlp[:, : cm // 2] = w_up[l]
        mlp[:, cm // 2 :] = w_down[l]


def kernel_unpack(count, *refs):
    pieces, outs = refs[: 3 * count], refs[3 * count :]
    sixes, (w_qkv, b_qv, w_proj, w_up, b_up, w_down) = outs[:6], outs[6:]
    layers, parts, heads, per, _ = w_qkv.shape
    half = heads * HEAD
    hidden = w_up.shape[2]

    def total(group, cols):
        found = [ref[:, cols].astype(f32) for ref in pieces[group * count : (group + 1) * count]]
        return functools.reduce(lambda a, b: a + b, found)

    ca = parts * half + half + LANES
    for l in range(layers):
        attn, mlp, base = (0, 1, 0) if l == 0 else (2, 2, ca)
        whole_attn = total(attn, slice(0, ca))
        for h in range(heads):
            for part in range(parts):
                at = part * half + h * HEAD
                w_qkv[l, part, h] = whole_attn[:, at : at + HEAD]
            at = parts * half + h * HEAD
            w_proj[l, h] = whole_attn[:, at : at + HEAD]
        vec = whole_attn[:, ca - LANES :]
        columns = vec.T
        for j, ref in enumerate(sixes):
            ref[l : l + 1, :] = columns[j : j + 1, :per]
        unit = b_qv.shape[3]
        for h in range(heads):
            for part in range(2):
                r = part * heads + h
                b_qv[l, h, part : part + 1, :] = vec[r : r + 1, QV_AT : QV_AT + unit]
        unit = b_up.shape[2]
        for r in range(b_up.shape[0]):
            b_up[r, l : l + 1, :] = vec[r : r + 1, UP_AT : UP_AT + unit]
        w_up[l] = total(mlp, slice(base, base + hidden))
        w_down[l] = total(mlp, slice(base + hidden, base + 2 * hidden))


def norm_parts(x):
    c = x - jnp.mean(x, -1, keepdims=True)
    s = lax.rsqrt(jnp.mean(c * c, -1, keepdims=True) + epsilon)
    return c * s, s


def norm_back(dh, u, s, gain):
    t = dh * gain
    return s * (t - jnp.mean(t, -1, keepdims=True) - u * jnp.mean(t * u, -1, keepdims=True))


def row_sum(x):
    return jnp.sum(x, 0, keepdims=True)


def halves_of_lanes(x):
    low = lax.broadcasted_iota(jnp.int32, x.shape, 1) < HEAD
    zero = jnp.zeros_like(x)
    return jnp.where(low, x, zero), jnp.where(low, zero, x)


def probs_t(scores, length):
    row = lax.broadcasted_iota(jnp.int32, scores.shape, 0)
    scores = jnp.where(row < length, scores, -1e30)
    high = jnp.max(scores, 0, keepdims=True)
    e = jnp.exp2((scores - high) * (HEAD**-0.5 * log2_e))
    return (e * (1.0 / jnp.sum(e, 0, keepdims=True))).astype(bf16)


def pair(qkv, width, at):
    return [qkv[:, part * width + at : part * width + at + LANES] for part in range(3)]


def attention(qkv, p_ref, o_ref, width, length):
    for j in range(width // LANES):
        at = LANES * j
        q, k, v = pair(qkv, width, at)
        out = None
        for h, (q_one, v_one) in enumerate(zip(halves_of_lanes(q), halves_of_lanes(v))):
            p = probs_t(dot(k, q_one, NT), length)
            p_ref[2 * j + h] = p
            one = dot(p, v_one, TN)
            out = one if out is None else out + one
        o_ref[:, at : at + LANES] = out.astype(bf16)


def attention_back(qkv, p_ref, do, dz_ref, width):
    for j in range(width // LANES):
        at = LANES * j
        q, k, v = pair(qkv, width, at)
        do_pair = do[:, at : at + LANES]
        sums = [None] * 3
        split = zip(*(halves_of_lanes(x) for x in (q, k, v, do_pair)))
        for h, (q_one, k_one, v_one, do_one) in enumerate(split):
            p = p_ref[2 * j + h]
            pf = p.astype(f32)
            t = pf * dot(v_one, do_pair, NT)
            ds = ((t - pf * row_sum(t)) * HEAD**-0.5).astype(bf16)
            found = (dot(ds, k_one, TN), dot(ds, q_one, NN), dot(p, do_one, NN))
            sums = [x if y is None else x + y for x, y in zip(found, sums)]
        for part in range(3):
            dz_ref[:, part * width + at : part * width + at + LANES] = sums[part].astype(bf16)


def place_attn_weights(a_refs, w_qkv, w_proj):
    width = w_qkv.shape[0]
    half = width // 2
    for i, ref in enumerate(a_refs):
        for part in range(3):
            to = part * width + i * half
            w_qkv[:, to : to + half] = ref[:, part * half : (part + 1) * half]
        w_proj[:, i * half : (i + 1) * half] = ref[:, 3 * half : 4 * half]


def store_attn_grads(acc_qkv, acc_proj, outs):
    width = acc_qkv.shape[0]
    half = width // 2
    for i, ref in enumerate(outs):
        for part in range(3):
            at = part * width + i * half
            ref[:, part * half : (part + 1) * half] = acc_qkv[:, at : at + half].astype(bf16)
        ref[:, 3 * half : 4 * half] = acc_proj[:, i * half : (i + 1) * half].astype(bf16)


def store_mlp_grads(acc_up, acc_down, outs):
    half = acc_up.shape[1] // 2
    for i, ref in enumerate(outs):
        ref[:, :half] = acc_up[:, i * half : (i + 1) * half].astype(bf16)
        ref[:, half:] = acc_down[:, i * half : (i + 1) * half].astype(bf16)


def attn_forward(x, table, w_qkv, w_proj, qkv, p_all, o_all, mid, length):
    group, rows, width = x.shape
    gain, shift = table[0:1, :width], table[1:2, :width]
    xs = x[...].reshape(group * rows, width)
    u, _ = norm_parts(xs)
    h = (u * gain + shift).astype(bf16)
    z = dot(h, w_qkv[...], NN) + table[6:7, : 3 * width]
    qkv[...] = z.astype(bf16).reshape(qkv.shape)
    for g in range(group):
        attention(qkv.at[g], p_all.at[g], o_all.at[g], width, length)
    o = o_all[...].reshape(group * rows, width)
    a = dot(o, w_proj[...], NT)
    mid[...] = (xs + a + table[2:3, :width]).reshape(mid.shape)


def mlp_forward(mid, table, m_refs, g_all, slope_all):
    group, rows, width = mid.shape
    ms = mid[...].reshape(group * rows, width)
    u, _ = norm_parts(ms)
    h = (u * table[3:4, :width] + table[4:5, :width]).astype(bf16)
    half = m_refs[0].shape[1] // 2
    total = None
    for i, ref in enumerate(m_refs):
        cols = slice(i * half, (i + 1) * half)
        pre = dot(h, ref[:, :half], NN) + table[7:8, cols]
        phi = 0.5 * (1.0 + lax.erf(pre * inv_root_two))
        g = (pre * phi).astype(bf16)
        g_all[:, :, cols] = g.reshape(group, rows, half)
        slope = phi + pre * jnp.exp(-0.5 * pre * pre) * inv_root_two_pi
        slope_all[:, :, cols] = slope.astype(bf16).reshape(group, rows, half)
        t = dot(g, ref[:, half:], NT)
        total = t if total is None else total + t
    return ms + total + table[5:6, :width]


def mlp_backward(e, mid, table, sums, m_refs, g_all, slope_all, acc_up, acc_down):
    group, rows, width = mid.shape
    half = m_refs[0].shape[1] // 2
    sums[5:6, :width] += row_sum(e)
    e_low = e.astype(bf16)
    u, s = norm_parts(mid[...].reshape(group * rows, width))
    gain = table[3:4, :width]
    h = (u * gain + table[4:5, :width]).astype(bf16)
    dh = None
    for i, ref in enumerate(m_refs):
        cols = slice(i * half, (i + 1) * half)
        dg = dot(e_low, ref[:, half:], NN)
        slope = slope_all[:, :, cols].reshape(group * rows, half).astype(f32)
        dpre = (dg * slope).astype(bf16)
        sums[7:8, cols] += row_sum(dpre.astype(f32))
        acc_up[:, cols] += dot(h, dpre, TN)
        acc_down[:, cols] += dot(e_low, g_all[:, :, cols].reshape(group * rows, half), TN)
        t = dot(dpre, ref[:, :half], NT)
        dh = t if dh is None else dh + t
    sums[3:4, :width] += row_sum(dh * u)
    sums[4:5, :width] += row_sum(dh)
    return e + norm_back(dh, u, s, gain)


def attn_backward(dmid, x, table, sums, w_qkv, w_proj, qkv, p_all, o_all, dz, acc_qkv, acc_proj):
    group, rows, width = x.shape
    sums[2:3, :width] += row_sum(dmid)
    da = dmid.astype(bf16)
    acc_proj[...] += dot(da, o_all[...].reshape(group * rows, width), TN)
    do = dot(da, w_proj[...], NN).astype(bf16)
    for g in range(group):
        attention_back(qkv.at[g], p_all.at[g], do[g * rows : (g + 1) * rows], dz.at[g], width)
    dzs = dz[...].reshape(group * rows, 3 * width)
    sums[6:7, : 3 * width] += row_sum(dzs.astype(f32))
    u, s = norm_parts(x[...].reshape(group * rows, width))
    gain = table[0:1, :width]
    h = (u * gain + table[1:2, :width]).astype(bf16)
    acc_qkv[...] += dot(h, dzs, TN)
    dh = dot(dzs, w_qkv[...], NT)
    sums[0:1, :width] += row_sum(dh * u)
    sums[1:2, :width] += row_sum(dh)
    return dmid + norm_back(dh, u, s, gain)


def turn_rows(images, tokens):
    r = lax.broadcasted_iota(jnp.int32, (tokens * images, images * tokens), 0)
    c = lax.broadcasted_iota(jnp.int32, (tokens * images, images * tokens), 1)
    return jnp.where((r % images == c // tokens) & (r // images == c % tokens), 1.0, 0.0).astype(bf16)


def token_runs(length):
    return [(at, min(32, length - at)) for at in range(0, length, 32)]


def spread_images(ref, x_all):
    length, images, width = ref.shape
    x_all[...] = jnp.zeros_like(x_all)
    turn = turn_rows(images, 32)
    for at, count in token_runs(length):
        part = ref[at : at + count].astype(f32).reshape(count * images, width).astype(bf16)
        whole_turn = turn if count == 32 else turn_rows(images, 32)[: count * images]
        found = dot(whole_turn, part, TN)
        for i in range(images):
            x_all[i, at : at + count, :] = found[i * 32 : i * 32 + count].astype(x_all.dtype)


def join_images(all_images, out):
    length, images, width = out.shape
    turn = turn_rows(images, 32)
    for at, count in token_runs(length):
        rows = jnp.concatenate([all_images[i, at : at + 32, :] for i in range(images)], 0)
        found = dot(turn[: count * images], rows, NN).reshape(count, images, width)
        out[at : at + count] = found.astype(out.dtype)


def group_rows(x_all, group):
    return x_all[pl.ds(pl.program_id(0) * group, group)].astype(f32)


def kernel_place(core, mine, other, full):
    images = mine.shape[1]
    for c in range(2):
        @pl.when(core[0] == c)
        def _():
            full[:, c * images : (c + 1) * images, :] = mine[...].astype(full.dtype)
            full[:, (1 - c) * images : (2 - c) * images, :] = other[...].astype(full.dtype)


def vec_of(ref):
    return ref.at[:, ref.shape[1] - LANES :]


def start_attn_forward(a_mine, a_other, table, w_qkv, w_proj, shards):
    place_attn_weights((a_mine, a_other), w_qkv, w_proj)
    expand_vec([vec_of(r) for r in (a_mine, a_other)], table, shards)


def kernel_first_attn_forward(
    shards, core, tok, a_mine, a_other, x_all, qkv, p_all, o_all, mid, table, x, w_qkv, w_proj
):
    @pl.when(pl.program_id(0) == 0)
    def _():
        start_attn_forward(a_mine, a_other, table, w_qkv, w_proj, shards)
        spread_images(tok, x_all)

    x[...] = group_rows(x_all, x.shape[0])
    attn_forward(x, table, w_qkv, w_proj, qkv, p_all, o_all, mid, tok.shape[0])


def kernel_attn_forward(shards, length, x, a_mine, a_other, qkv, p_all, o_all, mid, table, w_qkv, w_proj):
    @pl.when(pl.program_id(0) == 0)
    def _():
        start_attn_forward(a_mine, a_other, table, w_qkv, w_proj, shards)

    attn_forward(x, table, w_qkv, w_proj, qkv, p_all, o_all, mid, length)


def kernel_mlp_forward(mid, table, m_mine, m_other, stream, g_all, slope_all):
    out = mlp_forward(mid, table, (m_mine, m_other), g_all, slope_all)
    stream[...] = out.reshape(stream.shape)


def kernel_mlp_both(
    core, mid, cot, table, m_mine, m_other,
    out, dmid, sums, gm_mine, gm_other, g_all, slope_all, cot_all, out_all, acc_up, acc_down,
):
    step = pl.program_id(0)

    @pl.when(step == 0)
    def _():
        spread_images(cot, cot_all)
        for ref in (out_all, sums, acc_up, acc_down):
            ref[...] = jnp.zeros_like(ref)

    group, rows, width = mid.shape
    m_refs = (m_mine, m_other)
    result = mlp_forward(mid, table, m_refs, g_all, slope_all)
    for g in range(group):
        out_all[step * group + g, :rows, :] = result[g * rows : (g + 1) * rows].astype(bf16)
    e = group_rows(cot_all, group).reshape(group * rows, width)
    back = mlp_backward(e, mid, table, sums, m_refs, g_all, slope_all, acc_up, acc_down)
    dmid[...] = back.reshape(dmid.shape)

    @pl.when(step == pl.num_programs(0) - 1)
    def _():
        store_mlp_grads(acc_up, acc_down, (gm_mine, gm_other))
        join_images(out_all, out)


def kernel_mlp_backward(
    e, mid, table, g_all, slope_all, m_mine, m_other,
    dmid, sums, gm_mine, gm_other, acc_up, acc_down,
):
    step = pl.program_id(0)

    @pl.when(step == 0)
    def _():
        for ref in (sums, acc_up, acc_down):
            ref[...] = jnp.zeros_like(ref)

    group, rows, width = mid.shape
    back = mlp_backward(
        e[...].reshape(group * rows, width), mid, table, sums, (m_mine, m_other),
        g_all, slope_all, acc_up, acc_down,
    )
    dmid[...] = back.reshape(dmid.shape)

    @pl.when(step == pl.num_programs(0) - 1)
    def _():
        store_mlp_grads(acc_up, acc_down, (gm_mine, gm_other))


def attn_backward_step(
    shards, dmid, x, table, sums_in, qkv, p_all, o_all, a_mine, a_other,
    ga_mine, ga_other, sums, vec_rows, w_qkv, w_proj, dz, acc_qkv, acc_proj, keep, finish,
):
    step = pl.program_id(0)

    @pl.when(step == 0)
    def _():
        place_attn_weights((a_mine, a_other), w_qkv, w_proj)
        sums[...] = sums_in[...]
        for ref in (acc_qkv, acc_proj):
            ref[...] = jnp.zeros_like(ref)

    group, rows, width = x.shape
    back = attn_backward(
        dmid[...].reshape(group * rows, width), x, table, sums, w_qkv, w_proj,
        qkv, p_all, o_all, dz, acc_qkv, acc_proj,
    )
    keep(back)

    @pl.when(step == pl.num_programs(0) - 1)
    def _():
        store_attn_grads(acc_qkv, acc_proj, (ga_mine, ga_other))
        pack_vec(sums, [vec_of(r) for r in (ga_mine, ga_other)], vec_rows, shards)
        finish()


def kernel_attn_backward(shards, dmid, x, table, sums_in, qkv, p_all, o_all, a_mine, a_other, e_out, *rest):
    def keep(back):
        e_out[...] = back.reshape(e_out.shape)

    attn_backward_step(
        shards, dmid, x, table, sums_in, qkv, p_all, o_all, a_mine, a_other, *rest, keep, lambda: None
    )


def kernel_first_attn_backward(
    shards, dmid, x_low, table, sums_in, qkv, p_all, o_all, a_mine, a_other, grad, *rest
):
    *rest, grad_all, x = rest
    step = pl.program_id(0)
    group, rows, _ = x.shape

    @pl.when(step == 0)
    def _():
        grad_all[...] = jnp.zeros_like(grad_all)

    def keep(back):
        for g in range(group):
            grad_all[step * group + g, :rows, :] = back[g * rows : (g + 1) * rows].astype(bf16)

    x[...] = x_low[...].astype(f32)
    attn_backward_step(
        shards, dmid, x, table, sums_in, qkv, p_all, o_all, a_mine, a_other, *rest, keep,
        lambda: join_images(grad_all, grad),
    )


def whole(shape):
    zeros = (0,) * len(shape)
    return pl.BlockSpec(shape, lambda i, *_: zeros, pipeline_mode=pl.Buffered(1))


def whole_out(shape):
    zeros = (0,) * len(shape)
    return pl.BlockSpec(shape, lambda i, *_: zeros)


def by_group(shape):
    rest = (0,) * (len(shape) - 1)
    return pl.BlockSpec((GROUP, *shape[1:]), lambda i, *_: (i, *rest))


def of_core(shape):
    return pl.BlockSpec(
        (shape[0], shape[1] // 2, shape[2]), lambda i, core: (0, core[0], 0), pipeline_mode=pl.Buffered(1)
    )


def call(kernel, steps, core, args, in_specs, outs, out_specs, scratch, flops, name, limit=32):
    moved = sum(a.size * a.dtype.itemsize for a in args)
    moved += sum(math.prod(o.shape) * o.dtype.itemsize for o in outs)
    return pl.pallas_call(
        kernel,
        out_shape=outs,
        grid_spec=pltpu.PrefetchScalarGridSpec(
            num_scalar_prefetch=0 if core is None else 1,
            grid=(steps,),
            in_specs=in_specs,
            out_specs=out_specs,
            scratch_shapes=[pltpu.VMEM(s, d) for s, d in scratch],
        ),
        compiler_params=pltpu.CompilerParams(vmem_limit_bytes=limit * 2**20),
        cost_estimate=pl.CostEstimate(flops=int(flops), bytes_accessed=int(moved), transcendentals=0),
        name=name,
    )(*(() if core is None else (core,)), *args)


def both_cores(core, mine, other, dtype, parts=4):
    length, images, width = mine.shape
    run = -(-length // parts)
    block = pl.BlockSpec((run, images, width), lambda i, core: (i, 0, 0))
    return pl.pallas_call(
        kernel_place,
        out_shape=arr((length, 2 * images, width), dtype),
        grid_spec=pltpu.PrefetchScalarGridSpec(
            num_scalar_prefetch=1,
            grid=(parts,),
            in_specs=[block, block],
            out_specs=pl.BlockSpec((run, 2 * images, width), lambda i, core: (i, 0, 0)),
        ),
        compiler_params=pltpu.CompilerParams(vmem_limit_bytes=16 * 2**20),
        name="both_cores",
    )(core, mine, other)


def in_vmem(kernel, args, outs, scratch, name):
    spec = pl.BlockSpec(memory_space=pltpu.VMEM)
    return pl.pallas_call(
        kernel,
        out_shape=outs,
        in_specs=[spec] * len(args),
        out_specs=[spec] * len(outs),
        scratch_shapes=[pltpu.VMEM(s, d) for s, d in scratch],
        compiler_params=pltpu.CompilerParams(vmem_limit_bytes=VMEM_LIMIT),
        name=name,
    )(*args)


def arr(shape, dtype):
    return jax.ShapeDtypeStruct(shape, dtype)


def in_hbm(shape, dtype):
    return pltpu.HBM(shape, dtype)


def kept(*arrays):
    return [pltpu.with_memory_space_constraint(x, pltpu.HBM) for x in arrays]


def after(x, *others):
    return lax.optimization_barrier((x, *others))[0]


def after_all(xs, *others):
    return list(lax.optimization_barrier((*xs, *others))[: len(xs)])


def bit_groups(shards):
    bits = [1 << k for k in range(shards.bit_length() - 1)]
    groups = [bits[k : k + 2] for k in range(0, len(bits), 2)]
    return groups[::-1]


def masks_of(group):
    masks = [0]
    for b in group:
        masks = masks + [m | b for m in masks]
    return masks


def exchange(x, mask, shards):
    return lax.ppermute(x, "shard", [(i, i ^ mask) for i in range(shards)])


def swap_cores(x):
    return lax.ppermute(x, "tensor", [(0, 1), (1, 0)])


def fetch(x, group, shards):
    return [x if m == 0 else exchange(x, m, shards) for m in masks_of(group)]


def in_order(got, group):
    me = lax.axis_index("shard")
    for k, b in enumerate(group):
        flag = (me & b) != 0
        got = [jnp.where(flag, got[i ^ (1 << k)], got[i]) for i in range(len(got))]
    return jnp.stack(got, 1).reshape(-1, *got[0].shape[1:])


def flat_rows(x):
    return x.reshape(-1, x.shape[-1])


def pieces_for(h, group):
    count = len(masks_of(group))
    h = h.reshape(-1, count, *h.shape[1:])
    here = (lax.axis_index("shard") // group[0]) % count
    return [lax.dynamic_index_in_dim(h, here ^ k, 1, keepdims=False) for k in range(count)]


def send_pieces(pieces, group, shards):
    return [p if m == 0 else exchange(p, m, shards) for p, m in zip(pieces, masks_of(group))]


def add_up(found):
    return functools.reduce(lambda a, b: a + b, [f.astype(f32) for f in found])


def core_sum(mine, other, shards):
    h = mine.astype(f32) + other.astype(f32)
    return h.astype(bf16).reshape(shards, mine.shape[0] // shards, -1)


def body(
    tokens, cotangent, ln1_gain, ln1_bias, w_qkv, b_qv, w_proj, b_proj,
    ln2_gain, ln2_bias, w_up, b_up, w_down, b_down, *, shards,
):
    images_all, length, width = tokens.shape
    layers, per = ln1_gain.shape
    images = images_all // 2
    steps = images // GROUP
    rows = -(-length // 16) * 16
    hidden = 2 * w_up.shape[2]
    heads = width // HEAD
    ca, cm = 2 * width + LANES, hidden
    t = lax.axis_index("tensor")
    core = t.astype(jnp.int32).reshape(1)
    groups = bit_groups(shards)

    def turned(which):
        one = [(0, 1)] * 6 + [(0, 2, 3, 1, 4), (0, 2, 1, 3), (0, 1, 3, 2), (0, 1, 2), (1, 0, 2), (0, 2, 1)]
        back = [tuple(sorted(range(len(p)), key=lambda i: p[i])) for p in one]
        return one if which == "in" else back

    raw = (ln1_gain, ln1_bias, b_proj, ln2_gain, ln2_bias, b_down, w_qkv, b_qv, w_proj, w_up, b_up, w_down)
    raw = [x.transpose(p) for x, p in zip(raw, turned("in"))]
    first_attn, first_mlp, later_attn, later_mlp = in_vmem(
        kernel_pack, raw, [arr((per, c), bf16) for c in (ca, cm, ca, cm)],
        [((16, LANES), f32), ((per, LANES), f32)], "pack",
    )

    def early(x, stages):
        x = x[None]
        for group in stages:
            x = in_order(fetch(x, group, shards), group)
        return x

    last, before = groups[-1], groups[-2]
    z0 = early(first_attn, groups[:-1])
    got_a0 = fetch(z0, last, shards)
    m0 = early(after(first_mlp, z0), groups[:-1])
    a0 = flat_rows(in_order(got_a0, last))
    a0_other = swap_cores(a0)
    m0, later = after_all((m0, jnp.concatenate([later_attn, later_mlp], 1)), a0)
    got_m0 = fetch(m0, last, shards)
    got_l1 = fetch(early(later, groups[:-2]), before, shards)

    tok = images * length
    proj_flops = 2 * tok * width
    attn_flops = images * heads * 4 * length * length * HEAD
    aspec, mspec = whole((width, ca)), whole((width, cm))
    table_shape = (16, hidden)
    tspec = whole(table_shape)
    half_shape = (length, images, width)
    pad_shape = (images, rows, width)
    join_shape = (images, -(-length // 32) * 32, width)
    vec_shape = (16, LANES)
    qkv_shape = (images, rows, 3 * width)
    p_shape = (images, heads, rows, rows)
    g_shape = (images, rows, hidden)
    tokens_in, cotangent_in = (x.transpose(1, 0, 2) for x in (tokens, cotangent))

    def g_of(shape):
        return (GROUP, *shape[1:])

    saved = [in_hbm(qkv_shape, bf16), in_hbm(p_shape, bf16), in_hbm(pad_shape, bf16),
             arr(pad_shape, f32), arr(table_shape, f32)]
    saved_specs = [by_group(qkv_shape), by_group(p_shape), by_group(pad_shape), by_group(pad_shape),
                   whole_out(table_shape)]
    attn_weights = [((width, 3 * width), bf16), ((width, width), bf16)]
    mlp_sums = [((width, hidden), f32), ((width, hidden), f32)]
    forward_flops = 4 * proj_flops * width + attn_flops
    x_all, qkv, p_all, o_all, mid, table = call(
        functools.partial(kernel_first_attn_forward, shards), steps, core,
        (tokens_in, a0, a0_other),
        [of_core(tokens_in.shape), aspec, aspec],
        [in_hbm(pad_shape, bf16)] + saved, [whole_out(pad_shape)] + saved_specs,
        [(g_of(pad_shape), f32)] + attn_weights, forward_flops, "attn_forward_0",
    )
    got = after_all(got_m0 + got_l1, mid)
    m0, l1 = got[: len(got_m0)], got[len(got_m0) :]
    m0 = flat_rows(in_order(m0, last))
    m0_other = swap_cores(m0)
    l1 = in_order(l1, before)
    got_a1 = fetch(l1[:, :, :ca], last, shards)
    stream, g_all, slope_all = call(
        kernel_mlp_forward, steps, None,
        (mid, table, m0, m0_other),
        [by_group(pad_shape), tspec, mspec, mspec],
        [arr(pad_shape, f32), in_hbm(g_shape, bf16), in_hbm(g_shape, bf16)],
        [by_group(pad_shape), by_group(g_shape), by_group(g_shape)],
        [], 2 * proj_flops * hidden, "mlp_forward",
    )
    a1 = flat_rows(in_order(after_all(got_a1, stream), last))
    a1_other = swap_cores(a1)
    got_m1 = fetch(after(l1[:, :, ca:], a1), last, shards)
    qkv1, p1, o1, mid1, table1 = call(
        functools.partial(kernel_attn_forward, shards, length), steps, None,
        (stream, a1, a1_other),
        [by_group(pad_shape), aspec, aspec], saved, saved_specs,
        attn_weights, forward_flops, "attn_forward_1",
    )
    m1 = flat_rows(in_order(after_all(got_m1, mid1), last))
    m1_other = swap_cores(m1)
    out, dmid1, sums1, gm1_mine, gm1_other = call(
        kernel_mlp_both, steps, core,
        (mid1, cotangent_in, table1, m1, m1_other),
        [by_group(pad_shape), of_core(tokens_in.shape), tspec, mspec, mspec],
        [arr(half_shape, bf16), arr(pad_shape, f32), arr(table_shape, f32)] + [arr((width, cm), bf16)] * 2,
        [whole_out(half_shape), by_group(pad_shape), whole_out(table_shape)] + [whole_out((width, cm))] * 2,
        [(g_of(g_shape), bf16), (g_of(g_shape), bf16), (pad_shape, bf16), (join_shape, bf16)] + mlp_sums,
        6 * proj_flops * hidden, "mlp_both", 40,
    )
    back_specs = [by_group(pad_shape), by_group(pad_shape), tspec, tspec, by_group(qkv_shape),
                  by_group(p_shape), by_group(pad_shape), aspec, aspec]
    back_scratch = [
        (table_shape, f32), (vec_shape, f32), *attn_weights, (g_of(qkv_shape), bf16),
        ((width, 3 * width), f32), ((width, width), f32),
    ]
    ga_outs, ga_specs = [arr((width, ca), bf16)] * 2, [whole_out((width, ca))] * 2
    back_flops = 8 * proj_flops * width + 2.5 * attn_flops
    hm1 = swap_cores(gm1_other)
    e, ga1_mine, ga1_other = call(
        functools.partial(kernel_attn_backward, shards), steps, None,
        (dmid1, stream, table1, sums1, *kept(qkv1, p1, o1), a1, a1_other),
        back_specs, [arr(pad_shape, f32)] + ga_outs, [by_group(pad_shape)] + ga_specs,
        back_scratch, back_flops, "attn_backward_1",
    )
    hm1, ga1_mine, ga1_other = after_all((hm1, ga1_mine, ga1_other), e)
    h1 = core_sum(
        jnp.concatenate([ga1_mine, gm1_mine], 1), jnp.concatenate([swap_cores(ga1_other), hm1], 1), shards
    )
    h1 = pieces_for(h1, last)
    out_other = swap_cores(out)
    e = after(e, *h1)
    dmid, sums, gm_mine, gm_other = call(
        kernel_mlp_backward, steps, None,
        (e, mid, table, *kept(g_all, slope_all), m0, m0_other),
        [by_group(pad_shape), by_group(pad_shape), tspec, by_group(g_shape), by_group(g_shape), mspec, mspec],
        [arr(pad_shape, f32), arr(table_shape, f32)] + [arr((width, cm), bf16)] * 2,
        [by_group(pad_shape), whole_out(table_shape)] + [whole_out((width, cm))] * 2,
        mlp_sums, 4 * proj_flops * hidden, "mlp_backward",
    )
    middle = groups[:-1][::-1]
    h1 = add_up(after_all(send_pieces(h1, last, shards), dmid)).astype(bf16)
    h1 = pieces_for(h1, middle[0])
    h0m = pieces_for(core_sum(gm_mine, swap_cores(gm_other), shards), last)
    dmid = after(dmid, *h0m, *h1)
    grad, ga_mine, ga_other = call(
        functools.partial(kernel_first_attn_backward, shards), steps, None,
        (dmid, *kept(x_all), table, sums, *kept(qkv, p_all, o_all), a0, a0_other),
        back_specs, [arr(half_shape, bf16)] + ga_outs, [whole_out(half_shape)] + ga_specs,
        back_scratch + [(join_shape, bf16), (g_of(pad_shape), f32)], back_flops, "attn_backward_0",
    )
    h0m = send_pieces(h0m, last, shards)
    h1 = send_pieces(h1, middle[0], shards)
    n = len(h0m)
    got = after_all(h0m + h1 + [ga_mine, ga_other, grad], grad)
    h0m, h1, (ga_mine, ga_other, grad) = got[:n], got[n:-3], got[-3:]
    h0m = send_pieces(pieces_for(add_up(h0m).astype(bf16), middle[0]), middle[0], shards)
    h0a = send_pieces(pieces_for(core_sum(ga_mine, swap_cores(ga_other), shards), last), last, shards)
    grad_other = swap_cores(grad)
    h0a, h0m = after_all(h0a, *h0m), after_all(h0m, *h0a)
    h0a = send_pieces(pieces_for(add_up(h0a).astype(bf16), middle[0]), middle[0], shards)
    for group in middle[1:]:
        h0a, h0m, h1 = (
            send_pieces(pieces_for(add_up(h).astype(bf16), group), group, shards) for h in (h0a, h0m, h1)
        )

    out_full = both_cores(core, out, out_other, bf16)
    grad_full = both_cores(core, grad, grad_other, f32)
    h0a = after_all(h0a, out_full, grad_full)
    grads = in_vmem(
        functools.partial(kernel_unpack, len(h1)),
        [x.reshape(per, -1) for h in (h0a, h0m, h1) for x in h],
        [arr(x.shape, f32) for x in raw], [], "unpack",
    )
    grads = [g.transpose(p) for g, p in zip(grads, turned("out"))]
    g1, b1, bp, g2, b2, bd, gq, gb, gp, gu, gbu, gd = grads
    return (
        out_full.transpose(1, 0, 2), grad_full.transpose(1, 0, 2),
        g1, b1, gq, gb, gp, bp, g2, b2, gu, gbu, gd, bd,
    )


def solution(mesh):
    args = (
        P("shard", None, None),
        P("shard", None, None),
        P(None, "shard"),
        P(None, "shard"),
        P(None, "shard", None, "tensor", None),
        P(None, None, "tensor", "shard"),
        P(None, "tensor", None, "shard"),
        P(None, "shard"),
        P(None, "shard"),
        P(None, "shard"),
        P(None, "shard", "tensor"),
        P(None, "tensor", "shard"),
        P(None, "tensor", "shard"),
        P(None, "shard"),
    )
    return jax.shard_map(
        functools.partial(body, shards=mesh.shape["shard"]),
        mesh=mesh,
        in_specs=args,
        out_specs=args,
        check_vma=False,
    )
```

```python
import functools
import math

import jax
import jax.numpy as jnp
from jax import lax
from jax.experimental import pallas as pl
from jax.experimental.pallas import tpu as pltpu
from jax.sharding import PartitionSpec as P

bf16, f32 = jnp.bfloat16, jnp.float32
epsilon = 1e-06
inv_root_two = 0.7071067811865476
inv_root_two_pi = 0.3989422804014327
log2_e = 1.4426950408889634
NN, NT, TN = ((1,), (0,)), ((1,), (1,)), ((0,), (0,))
VMEM_LIMIT = 60 * 2**20
GROUP = 2
HEAD = 64
LANES = 128


def dot(a, b, dims):
    return lax.dot_general(a, b, (dims, ((), ())), preferred_element_type=f32)


QV_AT, UP_AT = 16, 24


def owner_rows(width, shards, place):
    n = lax.broadcasted_iota(jnp.int32, (width, LANES), 0)
    m = lax.broadcasted_iota(jnp.int32, (width, LANES), 1)
    per = width // shards
    return n // per == (m % place) // (place // shards)


def lane_picks(at, unit):
    r = lax.broadcasted_iota(jnp.int32, (LANES, LANES), 0)
    m = lax.broadcasted_iota(jnp.int32, (LANES, LANES), 1)
    return jnp.where(r == at + m % unit, 1.0, 0.0).astype(bf16)


def rank_rows(width, shards):
    r = lax.broadcasted_iota(jnp.int32, (16, width), 0)
    n = lax.broadcasted_iota(jnp.int32, (16, width), 1)
    return jnp.where(n % (width // shards) == r, 1.0, 0.0).astype(bf16)


def unit_rows(rows, columns):
    r = lax.broadcasted_iota(jnp.int32, (rows, columns), 0)
    c = lax.broadcasted_iota(jnp.int32, (rows, columns), 1)
    return jnp.where(r == c, 1.0, 0.0).astype(bf16)


def qv_spots(width, half):
    heads = width // HEAD // 2
    for part in range(2):
        for h in range(heads):
            yield part * heads + h, part * 2 * width + half * (width // 2) + h * HEAD


def up_spots(hidden, half):
    rows = hidden // 2 // LANES
    return [(r, (half * rows + r) * LANES) for r in range(rows)]


def expand_vec(vec_refs, table, shards):
    width, hidden = vec_refs[0].shape[0], table.shape[1]
    table[...] = jnp.zeros_like(table)
    ranks = rank_rows(width, shards)
    for half, ref in enumerate(vec_refs):
        block = ref[...]
        if half == 0:
            table[0:6, 0:width] = dot(unit_rows(16, LANES), block, NT)[0:6]
        for at, place, row, spots in (
            (QV_AT, HEAD, 6, qv_spots(width, half)),
            (UP_AT, LANES, 7, up_spots(hidden, half)),
        ):
            found = dot(block, lane_picks(at, place // shards), NN)
            found = jnp.where(owner_rows(width, shards, place), found, 0.0).astype(bf16)
            found = dot(ranks, found, NN)
            for r, first in spots:
                table[row : row + 1, first : first + place] = found[r : r + 1, :place]


def pack_vec(table, outs, rows, shards):
    width, hidden = outs[0].shape[0], table.shape[1]
    index = lax.broadcasted_iota(jnp.int32, (16, width), 0)
    six = jnp.where(index < 6, table[0:16, :width], 0.0).astype(bf16)
    six = dot(six, unit_rows(16, LANES), TN)
    ranks = rank_rows(width, shards)
    for half, ref in enumerate(outs):
        block = six
        for at, place, row, spots in (
            (QV_AT, HEAD, 6, qv_spots(width, half)),
            (UP_AT, LANES, 7, up_spots(hidden, half)),
        ):
            rows[...] = jnp.zeros_like(rows)
            for r, first in spots:
                rows[r : r + 1, :place] = table[row : row + 1, first : first + place]
            found = dot(ranks, rows[...].astype(bf16), TN)
            lane = lax.broadcasted_iota(jnp.int32, (width, LANES), 1)
            found = jnp.where(owner_rows(width, shards, place) & (lane < place), found, 0.0).astype(bf16)
            block = block + dot(found, lane_picks(at, place // shards), NT)
        ref[...] = block.astype(bf16)


def kernel_pack(
    ln1_gain, ln1_bias, b_proj, ln2_gain, ln2_bias, b_down, w_qkv, b_qv, w_proj, w_up, b_up, w_down,
    first_attn, first_mlp, later_attn, later_mlp, rows, vec,
):
    layers, parts, heads, per, _ = w_qkv.shape
    half = heads * HEAD
    ca, cm = first_attn.shape[1], first_mlp.shape[1]
    for l in range(layers):
        attn, mlp = (first_attn, first_mlp) if l == 0 else (later_attn, later_mlp)
        for h in range(heads):
            for part in range(parts):
                at = part * half + h * HEAD
                attn[:, at : at + HEAD] = w_qkv[l, part, h]
            at = parts * half + h * HEAD
            attn[:, at : at + HEAD] = w_proj[l, h]
        rows[...] = jnp.zeros_like(rows)
        for j, ref in enumerate((ln1_gain, ln1_bias, b_proj, ln2_gain, ln2_bias, b_down)):
            rows[j : j + 1, :per] = ref[l : l + 1, :].astype(f32)
        vec[...] = jnp.zeros_like(vec)
        vec[:, 0:16] = dot(unit_rows(per, LANES), rows[...].astype(bf16), NT)
        unit = b_qv.shape[3]
        for h in range(heads):
            for part in range(2):
                r = part * heads + h
                vec[r : r + 1, QV_AT : QV_AT + unit] = b_qv[l, h, part : part + 1, :].astype(f32)
        unit = b_up.shape[2]
        for r in range(b_up.shape[0]):
            vec[r : r + 1, UP_AT : UP_AT + unit] = b_up[r, l : l + 1, :].astype(f32)
        attn[:, ca - LANES :] = vec[...].astype(bf16)
        mlp[:, : cm // 2] = w_up[l]
        mlp[:, cm // 2 :] = w_down[l]


def kernel_unpack(count, *refs):
    pieces, outs = refs[: 3 * count], refs[3 * count :]
    sixes, (w_qkv, b_qv, w_proj, w_up, b_up, w_down) = outs[:6], outs[6:]
    layers, parts, heads, per, _ = w_qkv.shape
    half = heads * HEAD
    hidden = w_up.shape[2]

    def total(group, cols):
        found = [ref[:, cols].astype(f32) for ref in pieces[group * count : (group + 1) * count]]
        return functools.reduce(lambda a, b: a + b, found)

    ca = parts * half + half + LANES
    for l in range(layers):
        attn, mlp, base = (0, 1, 0) if l == 0 else (2, 2, ca)
        whole_attn = total(attn, slice(0, ca))
        for h in range(heads):
            for part in range(parts):
                at = part * half + h * HEAD
                w_qkv[l, part, h] = whole_attn[:, at : at + HEAD]
            at = parts * half + h * HEAD
            w_proj[l, h] = whole_attn[:, at : at + HEAD]
        vec = whole_attn[:, ca - LANES :]
        columns = vec.T
        for j, ref in enumerate(sixes):
            ref[l : l + 1, :] = columns[j : j + 1, :per]
        unit = b_qv.shape[3]
        for h in range(heads):
            for part in range(2):
                r = part * heads + h
                b_qv[l, h, part : part + 1, :] = vec[r : r + 1, QV_AT : QV_AT + unit]
        unit = b_up.shape[2]
        for r in range(b_up.shape[0]):
            b_up[r, l : l + 1, :] = vec[r : r + 1, UP_AT : UP_AT + unit]
        w_up[l] = total(mlp, slice(base, base + hidden))
        w_down[l] = total(mlp, slice(base + hidden, base + 2 * hidden))


def norm_parts(x):
    c = x - jnp.mean(x, -1, keepdims=True)
    s = lax.rsqrt(jnp.mean(c * c, -1, keepdims=True) + epsilon)
    return c * s, s


def norm_back(dh, u, s, gain):
    t = dh * gain
    return s * (t - jnp.mean(t, -1, keepdims=True) - u * jnp.mean(t * u, -1, keepdims=True))


def row_sum(x):
    return jnp.sum(x, 0, keepdims=True)


def halves_of_lanes(x):
    low = lax.broadcasted_iota(jnp.int32, x.shape, 1) < HEAD
    zero = jnp.zeros_like(x)
    return jnp.where(low, x, zero), jnp.where(low, zero, x)


def probs_t(scores, length):
    row = lax.broadcasted_iota(jnp.int32, scores.shape, 0)
    scores = jnp.where(row < length, scores, -1e30)
    high = jnp.max(scores, 0, keepdims=True)
    e = jnp.exp2((scores - high) * (HEAD**-0.5 * log2_e))
    return (e * (1.0 / jnp.sum(e, 0, keepdims=True))).astype(bf16)


def pair(qkv, width, at):
    return [qkv[:, part * width + at : part * width + at + LANES] for part in range(3)]


def attention(qkv, p_ref, o_ref, width, length):
    images, pairs = qkv.shape[0], width // LANES

    def probs(j):
        found = []
        for g in range(images):
            q, k, _ = pair(qkv.at[g], width, LANES * j)
            found.append([probs_t(dot(k, q_one, NT), length) for q_one in halves_of_lanes(q)])
        return found

    def mix(j, found):
        at = LANES * j
        for g in range(images):
            v = pair(qkv.at[g], width, at)[2]
            parts = [dot(p, v_one, TN) for p, v_one in zip(found[g], halves_of_lanes(v))]
            o_ref[g, :, at : at + LANES] = (parts[0] + parts[1]).astype(bf16)
            for h, p in enumerate(found[g]):
                p_ref[g, 2 * j + h] = p

    in_turn(pairs, probs, mix, 1)


def in_turn(count, first, second, ahead):
    waiting = []
    for j in range(count):
        waiting.append((j, first(j)))
        if len(waiting) > ahead:
            second(*waiting.pop(0))
    for item in waiting:
        second(*item)


def attention_back(qkv, p_ref, do, dz_ref, width):
    images, rows, _ = qkv.shape

    def slopes(j):
        at = LANES * j
        found = []
        for g in range(images):
            v = pair(qkv.at[g], width, at)[2]
            do_pair = do[g * rows : (g + 1) * rows, at : at + LANES]
            for h, v_one in enumerate(halves_of_lanes(v)):
                pf = p_ref[g, 2 * j + h].astype(f32)
                t = pf * dot(v_one, do_pair, NT)
                found.append((t - pf * row_sum(t)).astype(bf16))
        return found

    def products(j, found):
        at = LANES * j
        for g in range(images):
            q, k, _ = pair(qkv.at[g], width, at)
            do_pair = do[g * rows : (g + 1) * rows, at : at + LANES]
            sums = [None] * 3
            split = zip(*(halves_of_lanes(x) for x in (q * HEAD**-0.5, k * HEAD**-0.5, do_pair)))
            for h, (q_one, k_one, do_one) in enumerate(split):
                ds = found[2 * g + h]
                parts = (dot(ds, k_one, TN), dot(ds, q_one, NN), dot(p_ref[g, 2 * j + h], do_one, NN))
                sums = [x if y is None else x + y for x, y in zip(parts, sums)]
            for part in range(3):
                dz_ref[g, :, part * width + at : part * width + at + LANES] = sums[part].astype(bf16)

    in_turn(width // LANES, slopes, products, 1)


def place_attn_weights(a_refs, w_qkv, w_proj):
    width = w_qkv.shape[0]
    half = width // 2
    for i, ref in enumerate(a_refs):
        for part in range(3):
            to = part * width + i * half
            w_qkv[:, to : to + half] = ref[:, part * half : (part + 1) * half]
        w_proj[:, i * half : (i + 1) * half] = ref[:, 3 * half : 4 * half]


def store_attn_grads(acc_qkv, acc_proj, outs):
    width = acc_qkv.shape[0]
    half = width // 2
    for i, ref in enumerate(outs):
        for part in range(3):
            at = part * width + i * half
            ref[:, part * half : (part + 1) * half] = acc_qkv[:, at : at + half].astype(bf16)
        ref[:, 3 * half : 4 * half] = acc_proj[:, i * half : (i + 1) * half].astype(bf16)


def store_mlp_grads(acc_up, acc_down, outs):
    half = acc_up.shape[1] // 2
    for i, ref in enumerate(outs):
        ref[:, :half] = acc_up[:, i * half : (i + 1) * half].astype(bf16)
        ref[:, half:] = acc_down[:, i * half : (i + 1) * half].astype(bf16)


def attn_forward(x, table, w_qkv, w_proj, qkv, p_all, o_all, mid, length):
    group, rows, width = x.shape
    gain, shift = table[0:1, :width], table[1:2, :width]
    xs = x[...].reshape(group * rows, width)
    u, _ = norm_parts(xs)
    h = (u * gain + shift).astype(bf16)
    z = dot(h, w_qkv[...], NN) + table[6:7, : 3 * width]
    qkv[...] = z.astype(bf16).reshape(qkv.shape)
    attention(qkv, p_all, o_all, width, length)
    o = o_all[...].reshape(group * rows, width)
    a = dot(o, w_proj[...], NT)
    mid[...] = (xs + a + table[2:3, :width]).reshape(mid.shape)


def mlp_forward(mid, table, m_refs, g_all, slope_all):
    group, rows, width = mid.shape
    ms = mid[...].reshape(group * rows, width)
    u, _ = norm_parts(ms)
    h = (u * table[3:4, :width] + table[4:5, :width]).astype(bf16)
    half = m_refs[0].shape[1] // 2
    pres = [dot(h, ref[:, :half], NN) for ref in m_refs]
    total = None
    for i, (ref, pre) in enumerate(zip(m_refs, pres)):
        cols = slice(i * half, (i + 1) * half)
        pre = pre + table[7:8, cols]
        phi = 0.5 * (1.0 + lax.erf(pre * inv_root_two))
        g = (pre * phi).astype(bf16)
        g_all[:, :, cols] = g.reshape(group, rows, half)
        slope = phi + pre * jnp.exp(-0.5 * pre * pre) * inv_root_two_pi
        slope_all[:, :, cols] = slope.astype(bf16).reshape(group, rows, half)
        t = dot(g, ref[:, half:], NT)
        total = t if total is None else total + t
    return ms + total + table[5:6, :width]


def mlp_backward(e, mid, table, sums, m_refs, g_all, slope_all, acc_up, acc_down):
    group, rows, width = mid.shape
    half = m_refs[0].shape[1] // 2
    sums[5:6, :width] += row_sum(e)
    e_low = e.astype(bf16)
    u, s = norm_parts(mid[...].reshape(group * rows, width))
    gain = table[3:4, :width]
    h = (u * gain + table[4:5, :width]).astype(bf16)
    dgs = [dot(e_low, ref[:, half:], NN) for ref in m_refs]
    dpres = []
    for i, dg in enumerate(dgs):
        slope = slope_all[:, :, i * half : (i + 1) * half].reshape(group * rows, half).astype(f32)
        dpres.append((dg * slope).astype(bf16))
    dh = dot(dpres[0], m_refs[0][:, :half], NT) + dot(dpres[1], m_refs[1][:, :half], NT)
    for i, dpre in enumerate(dpres):
        cols = slice(i * half, (i + 1) * half)
        acc_up[:, cols] += dot(h, dpre, TN)
        acc_down[:, cols] += dot(e_low, g_all[:, :, cols].reshape(group * rows, half), TN)
        sums[7:8, cols] += row_sum(dpre.astype(f32))
    sums[3:4, :width] += row_sum(dh * u)
    sums[4:5, :width] += row_sum(dh)
    return e + norm_back(dh, u, s, gain)


def attn_backward(dmid, x, table, sums, w_qkv, w_proj, qkv, p_all, o_all, dz, acc_qkv, acc_proj):
    group, rows, width = x.shape
    sums[2:3, :width] += row_sum(dmid)
    da = dmid.astype(bf16)
    do = dot(da, w_proj[...], NN).astype(bf16)
    acc_proj[...] += dot(da, o_all[...].reshape(group * rows, width), TN)
    u, s = norm_parts(x[...].reshape(group * rows, width))
    gain = table[0:1, :width]
    h = (u * gain + table[1:2, :width]).astype(bf16)
    attention_back(qkv, p_all, do, dz, width)
    dzs = dz[...].reshape(group * rows, 3 * width)
    dh = dot(dzs, w_qkv[...], NT)
    acc_qkv[...] += dot(h, dzs, TN)
    sums[6:7, : 3 * width] += row_sum(dzs.astype(f32))
    sums[0:1, :width] += row_sum(dh * u)
    sums[1:2, :width] += row_sum(dh)
    return dmid + norm_back(dh, u, s, gain)


def turn_rows(images, tokens):
    r = lax.broadcasted_iota(jnp.int32, (tokens * images, images * tokens), 0)
    c = lax.broadcasted_iota(jnp.int32, (tokens * images, images * tokens), 1)
    return jnp.where((r % images == c // tokens) & (r // images == c % tokens), 1.0, 0.0).astype(bf16)


def token_runs(length):
    return [(at, min(32, length - at)) for at in range(0, length, 32)]


def spread_images(ref, x_all):
    length, images, width = ref.shape
    x_all[...] = jnp.zeros_like(x_all)
    turn = turn_rows(images, 32)
    for at, count in token_runs(length):
        part = ref[at : at + count].astype(f32).reshape(count * images, width).astype(bf16)
        whole_turn = turn if count == 32 else turn_rows(images, 32)[: count * images]
        found = dot(whole_turn, part, TN)
        for i in range(images):
            x_all[i, at : at + count, :] = found[i * 32 : i * 32 + count].astype(x_all.dtype)


def join_images(all_images, out):
    length, images, width = out.shape
    turn = turn_rows(images, 32)
    for at, count in token_runs(length):
        rows = jnp.concatenate([all_images[i, at : at + 32, :] for i in range(images)], 0)
        found = dot(turn[: count * images], rows, NN).reshape(count, images, width)
        out[at : at + count] = found.astype(out.dtype)


def group_rows(x_all, group):
    return x_all[pl.ds(pl.program_id(0) * group, group)].astype(f32)


def kernel_place(core, mine, other, full):
    images = mine.shape[1]
    for c in range(2):
        @pl.when(core[0] == c)
        def _():
            full[:, c * images : (c + 1) * images, :] = mine[...].astype(full.dtype)
            full[:, (1 - c) * images : (2 - c) * images, :] = other[...].astype(full.dtype)


def vec_of(ref):
    return ref.at[:, ref.shape[1] - LANES :]


def start_attn_forward(a_mine, a_other, table, w_qkv, w_proj, shards):
    place_attn_weights((a_mine, a_other), w_qkv, w_proj)
    expand_vec([vec_of(r) for r in (a_mine, a_other)], table, shards)


def kernel_first_attn_forward(
    shards, core, tok, a_mine, a_other, x_all, qkv, p_all, o_all, mid, table, x, w_qkv, w_proj
):
    @pl.when(pl.program_id(0) == 0)
    def _():
        start_attn_forward(a_mine, a_other, table, w_qkv, w_proj, shards)
        spread_images(tok, x_all)

    x[...] = group_rows(x_all, x.shape[0])
    attn_forward(x, table, w_qkv, w_proj, qkv, p_all, o_all, mid, tok.shape[0])


def kernel_attn_forward(shards, length, x, a_mine, a_other, qkv, p_all, o_all, mid, table, w_qkv, w_proj):
    @pl.when(pl.program_id(0) == 0)
    def _():
        start_attn_forward(a_mine, a_other, table, w_qkv, w_proj, shards)

    attn_forward(x, table, w_qkv, w_proj, qkv, p_all, o_all, mid, length)


def kernel_mlp_forward(mid, table, m_mine, m_other, stream, g_all, slope_all):
    out = mlp_forward(mid, table, (m_mine, m_other), g_all, slope_all)
    stream[...] = out.reshape(stream.shape)


def kernel_mlp_both(
    core, mid, cot, table, m_mine, m_other,
    out, dmid, sums, gm_mine, gm_other, g_all, slope_all, cot_all, out_all, acc_up, acc_down,
):
    step = pl.program_id(0)

    @pl.when(step == 0)
    def _():
        spread_images(cot, cot_all)
        for ref in (out_all, sums, acc_up, acc_down):
            ref[...] = jnp.zeros_like(ref)

    group, rows, width = mid.shape
    m_refs = (m_mine, m_other)
    result = mlp_forward(mid, table, m_refs, g_all, slope_all)
    for g in range(group):
        out_all[step * group + g, :rows, :] = result[g * rows : (g + 1) * rows].astype(bf16)
    e = group_rows(cot_all, group).reshape(group * rows, width)
    back = mlp_backward(e, mid, table, sums, m_refs, g_all, slope_all, acc_up, acc_down)
    dmid[...] = back.reshape(dmid.shape)

    @pl.when(step == pl.num_programs(0) - 1)
    def _():
        store_mlp_grads(acc_up, acc_down, (gm_mine, gm_other))
        join_images(out_all, out)


def kernel_mlp_backward(
    e, mid, table, g_all, slope_all, m_mine, m_other,
    dmid, sums, gm_mine, gm_other, acc_up, acc_down,
):
    step = pl.program_id(0)

    @pl.when(step == 0)
    def _():
        for ref in (sums, acc_up, acc_down):
            ref[...] = jnp.zeros_like(ref)

    group, rows, width = mid.shape
    back = mlp_backward(
        e[...].reshape(group * rows, width), mid, table, sums, (m_mine, m_other),
        g_all, slope_all, acc_up, acc_down,
    )
    dmid[...] = back.reshape(dmid.shape)

    @pl.when(step == pl.num_programs(0) - 1)
    def _():
        store_mlp_grads(acc_up, acc_down, (gm_mine, gm_other))


def attn_backward_step(
    shards, dmid, x, table, sums_in, qkv, p_all, o_all, a_mine, a_other,
    ga_mine, ga_other, sums, vec_rows, w_qkv, w_proj, dz, acc_qkv, acc_proj, keep, finish,
):
    step = pl.program_id(0)

    @pl.when(step == 0)
    def _():
        place_attn_weights((a_mine, a_other), w_qkv, w_proj)
        sums[...] = sums_in[...]
        for ref in (acc_qkv, acc_proj):
            ref[...] = jnp.zeros_like(ref)

    group, rows, width = x.shape
    back = attn_backward(
        dmid[...].reshape(group * rows, width), x, table, sums, w_qkv, w_proj,
        qkv, p_all, o_all, dz, acc_qkv, acc_proj,
    )
    keep(back)

    @pl.when(step == pl.num_programs(0) - 1)
    def _():
        store_attn_grads(acc_qkv, acc_proj, (ga_mine, ga_other))
        pack_vec(sums, [vec_of(r) for r in (ga_mine, ga_other)], vec_rows, shards)
        finish()


def kernel_attn_backward(shards, dmid, x, table, sums_in, qkv, p_all, o_all, a_mine, a_other, e_out, *rest):
    def keep(back):
        e_out[...] = back.reshape(e_out.shape)

    attn_backward_step(
        shards, dmid, x, table, sums_in, qkv, p_all, o_all, a_mine, a_other, *rest, keep, lambda: None
    )


def kernel_first_attn_backward(
    shards, dmid, x_low, table, sums_in, qkv, p_all, o_all, a_mine, a_other, grad, *rest
):
    *rest, grad_all, x = rest
    step = pl.program_id(0)
    group, rows, _ = x.shape

    @pl.when(step == 0)
    def _():
        grad_all[...] = jnp.zeros_like(grad_all)

    def keep(back):
        for g in range(group):
            grad_all[step * group + g, :rows, :] = back[g * rows : (g + 1) * rows].astype(bf16)

    x[...] = x_low[...].astype(f32)
    attn_backward_step(
        shards, dmid, x, table, sums_in, qkv, p_all, o_all, a_mine, a_other, *rest, keep,
        lambda: join_images(grad_all, grad),
    )


def whole(shape):
    zeros = (0,) * len(shape)
    return pl.BlockSpec(shape, lambda i, *_: zeros, pipeline_mode=pl.Buffered(1))


def whole_out(shape):
    zeros = (0,) * len(shape)
    return pl.BlockSpec(shape, lambda i, *_: zeros)


def by_group(shape):
    rest = (0,) * (len(shape) - 1)
    return pl.BlockSpec((GROUP, *shape[1:]), lambda i, *_: (i, *rest))


def of_core(shape):
    return pl.BlockSpec(
        (shape[0], shape[1] // 2, shape[2]), lambda i, core: (0, core[0], 0), pipeline_mode=pl.Buffered(1)
    )


def call(kernel, steps, core, args, in_specs, outs, out_specs, scratch, flops, name, limit=32):
    moved = sum(a.size * a.dtype.itemsize for a in args)
    moved += sum(math.prod(o.shape) * o.dtype.itemsize for o in outs)
    return pl.pallas_call(
        kernel,
        out_shape=outs,
        grid_spec=pltpu.PrefetchScalarGridSpec(
            num_scalar_prefetch=0 if core is None else 1,
            grid=(steps,),
            in_specs=in_specs,
            out_specs=out_specs,
            scratch_shapes=[pltpu.VMEM(s, d) for s, d in scratch],
        ),
        compiler_params=pltpu.CompilerParams(vmem_limit_bytes=limit * 2**20),
        cost_estimate=pl.CostEstimate(flops=int(flops), bytes_accessed=int(moved), transcendentals=0),
        name=name,
    )(*(() if core is None else (core,)), *args)


def both_cores(core, mine, other, dtype, parts=4):
    length, images, width = mine.shape
    run = -(-length // parts)
    block = pl.BlockSpec((run, images, width), lambda i, core: (i, 0, 0))
    return pl.pallas_call(
        kernel_place,
        out_shape=arr((length, 2 * images, width), dtype),
        grid_spec=pltpu.PrefetchScalarGridSpec(
            num_scalar_prefetch=1,
            grid=(parts,),
            in_specs=[block, block],
            out_specs=pl.BlockSpec((run, 2 * images, width), lambda i, core: (i, 0, 0)),
        ),
        compiler_params=pltpu.CompilerParams(vmem_limit_bytes=16 * 2**20),
        name="both_cores",
    )(core, mine, other)


def in_vmem(kernel, args, outs, scratch, name):
    spec = pl.BlockSpec(memory_space=pltpu.VMEM)
    return pl.pallas_call(
        kernel,
        out_shape=outs,
        in_specs=[spec] * len(args),
        out_specs=[spec] * len(outs),
        scratch_shapes=[pltpu.VMEM(s, d) for s, d in scratch],
        compiler_params=pltpu.CompilerParams(vmem_limit_bytes=VMEM_LIMIT),
        name=name,
    )(*args)


def arr(shape, dtype):
    return jax.ShapeDtypeStruct(shape, dtype)


def in_hbm(shape, dtype):
    return pltpu.HBM(shape, dtype)


def kept(*arrays):
    return [pltpu.with_memory_space_constraint(x, pltpu.HBM) for x in arrays]


def after(x, *others):
    return lax.optimization_barrier((x, *others))[0]


def after_all(xs, *others):
    return list(lax.optimization_barrier((*xs, *others))[: len(xs)])


def bit_groups(shards):
    bits = [1 << k for k in range(shards.bit_length() - 1)]
    groups = [bits[k : k + 2] for k in range(0, len(bits), 2)]
    return groups[::-1]


def masks_of(group):
    masks = [0]
    for b in group:
        masks = masks + [m | b for m in masks]
    return masks


def exchange(x, mask, shards):
    return lax.ppermute(x, "shard", [(i, i ^ mask) for i in range(shards)])


def swap_cores(x):
    return lax.ppermute(x, "tensor", [(0, 1), (1, 0)])


def fetch(x, group, shards):
    return [x if m == 0 else exchange(x, m, shards) for m in masks_of(group)]


def in_order(got, group):
    me = lax.axis_index("shard")
    for k, b in enumerate(group):
        flag = (me & b) != 0
        got = [jnp.where(flag, got[i ^ (1 << k)], got[i]) for i in range(len(got))]
    return jnp.stack(got, 1).reshape(-1, *got[0].shape[1:])


def flat_rows(x):
    return x.reshape(-1, x.shape[-1])


def pieces_for(h, group):
    count = len(masks_of(group))
    h = h.reshape(-1, count, *h.shape[1:])
    here = (lax.axis_index("shard") // group[0]) % count
    return [lax.dynamic_index_in_dim(h, here ^ k, 1, keepdims=False) for k in range(count)]


def send_pieces(pieces, group, shards):
    return [p if m == 0 else exchange(p, m, shards) for p, m in zip(pieces, masks_of(group))]


def add_up(found):
    return functools.reduce(lambda a, b: a + b, [f.astype(f32) for f in found])


def core_pieces(pairs, group, shards):
    cut = [
        [pieces_for(x.reshape(shards, x.shape[0] // shards, -1), group) for x in pair] for pair in pairs
    ]
    return [
        jnp.concatenate([add_up([mine[k], other[k]]).astype(bf16) for mine, other in cut], -1)
        for k in range(len(masks_of(group)))
    ]


def body(
    tokens, cotangent, ln1_gain, ln1_bias, w_qkv, b_qv, w_proj, b_proj,
    ln2_gain, ln2_bias, w_up, b_up, w_down, b_down, *, shards,
):
    images_all, length, width = tokens.shape
    layers, per = ln1_gain.shape
    images = images_all // 2
    steps = images // GROUP
    rows = -(-length // 16) * 16
    hidden = 2 * w_up.shape[2]
    heads = width // HEAD
    ca, cm = 2 * width + LANES, hidden
    t = lax.axis_index("tensor")
    core = t.astype(jnp.int32).reshape(1)
    groups = bit_groups(shards)

    def turned(which):
        one = [(0, 1)] * 6 + [(0, 2, 3, 1, 4), (0, 2, 1, 3), (0, 1, 3, 2), (0, 1, 2), (1, 0, 2), (0, 2, 1)]
        back = [tuple(sorted(range(len(p)), key=lambda i: p[i])) for p in one]
        return one if which == "in" else back

    raw = (ln1_gain, ln1_bias, b_proj, ln2_gain, ln2_bias, b_down, w_qkv, b_qv, w_proj, w_up, b_up, w_down)
    raw = [x.transpose(p) for x, p in zip(raw, turned("in"))]
    first_attn, first_mlp, later_attn, later_mlp = in_vmem(
        kernel_pack, raw, [arr((per, c), bf16) for c in (ca, cm, ca, cm)],
        [((16, LANES), f32), ((per, LANES), f32)], "pack",
    )

    def early(x, stages):
        x = x[None]
        for group in stages:
            x = in_order(fetch(x, group, shards), group)
        return x

    last, before = groups[-1], groups[-2]
    z0 = early(first_attn, groups[:-1])
    got_a0 = fetch(z0, last, shards)
    m0 = early(after(first_mlp, z0), groups[:-1])
    a0 = flat_rows(in_order(got_a0, last))
    a0_other = swap_cores(a0)
    m0, later = after_all((m0, jnp.concatenate([later_attn, later_mlp], 1)), a0)
    got_m0 = fetch(m0, last, shards)
    got_l1 = fetch(early(later, groups[:-2]), before, shards)

    tok = images * length
    proj_flops = 2 * tok * width
    attn_flops = images * heads * 4 * length * length * HEAD
    aspec, mspec = whole((width, ca)), whole((width, cm))
    table_shape = (16, hidden)
    tspec = whole(table_shape)
    half_shape = (length, images, width)
    pad_shape = (images, rows, width)
    join_shape = (images, -(-length // 32) * 32, width)
    vec_shape = (16, LANES)
    qkv_shape = (images, rows, 3 * width)
    p_shape = (images, heads, rows, rows)
    g_shape = (images, rows, hidden)
    tokens_in, cotangent_in = kept(*(x.transpose(1, 0, 2) for x in (tokens, cotangent)))

    def g_of(shape):
        return (GROUP, *shape[1:])

    saved = [in_hbm(qkv_shape, bf16), in_hbm(p_shape, bf16), in_hbm(pad_shape, bf16),
             arr(pad_shape, f32), arr(table_shape, f32)]
    saved_specs = [by_group(qkv_shape), by_group(p_shape), by_group(pad_shape), by_group(pad_shape),
                   whole_out(table_shape)]
    attn_weights = [((width, 3 * width), bf16), ((width, width), bf16)]
    mlp_sums = [((width, hidden), f32), ((width, hidden), f32)]
    forward_flops = 4 * proj_flops * width + attn_flops
    x_all, qkv, p_all, o_all, mid, table = call(
        functools.partial(kernel_first_attn_forward, shards), steps, core,
        (tokens_in, a0, a0_other),
        [of_core(tokens_in.shape), aspec, aspec],
        [in_hbm(pad_shape, bf16)] + saved, [whole_out(pad_shape)] + saved_specs,
        [(g_of(pad_shape), f32)] + attn_weights, forward_flops, "attn_forward_0",
    )
    got = after_all(got_m0 + got_l1, mid)
    m0, l1 = got[: len(got_m0)], got[len(got_m0) :]
    m0 = flat_rows(in_order(m0, last))
    m0_other = swap_cores(m0)
    l1 = in_order(l1, before)
    got_a1 = fetch(l1[:, :, :ca], last, shards)
    stream, g_all, slope_all = call(
        kernel_mlp_forward, steps, None,
        (mid, table, m0, m0_other),
        [by_group(pad_shape), tspec, mspec, mspec],
        [arr(pad_shape, f32), in_hbm(g_shape, bf16), in_hbm(g_shape, bf16)],
        [by_group(pad_shape), by_group(g_shape), by_group(g_shape)],
        [], 2 * proj_flops * hidden, "mlp_forward",
    )
    a1 = flat_rows(in_order(after_all(got_a1, stream), last))
    a1_other = swap_cores(a1)
    got_m1 = fetch(after(l1[:, :, ca:], a1), last, shards)
    qkv1, p1, o1, mid1, table1 = call(
        functools.partial(kernel_attn_forward, shards, length), steps, None,
        (stream, a1, a1_other),
        [by_group(pad_shape), aspec, aspec], saved, saved_specs,
        attn_weights, forward_flops, "attn_forward_1",
    )
    m1 = flat_rows(in_order(after_all(got_m1, mid1), last))
    m1_other = swap_cores(m1)
    out, dmid1, sums1, gm1_mine, gm1_other = call(
        kernel_mlp_both, steps, core,
        (mid1, cotangent_in, table1, m1, m1_other),
        [by_group(pad_shape), of_core(tokens_in.shape), tspec, mspec, mspec],
        [arr(half_shape, bf16), arr(pad_shape, f32), arr(table_shape, f32)] + [arr((width, cm), bf16)] * 2,
        [whole_out(half_shape), by_group(pad_shape), whole_out(table_shape)] + [whole_out((width, cm))] * 2,
        [(g_of(g_shape), bf16), (g_of(g_shape), bf16), (pad_shape, bf16), (join_shape, bf16)] + mlp_sums,
        6 * proj_flops * hidden, "mlp_both", 40,
    )
    back_specs = [by_group(pad_shape), by_group(pad_shape), tspec, tspec, by_group(qkv_shape),
                  by_group(p_shape), by_group(pad_shape), aspec, aspec]
    back_scratch = [
        (table_shape, f32), (vec_shape, f32), *attn_weights, (g_of(qkv_shape), bf16),
        ((width, 3 * width), f32), ((width, width), f32),
    ]
    ga_outs, ga_specs = [arr((width, ca), bf16)] * 2, [whole_out((width, ca))] * 2
    back_flops = 8 * proj_flops * width + 2.5 * attn_flops
    hm1 = swap_cores(gm1_other)
    e, ga1_mine, ga1_other = call(
        functools.partial(kernel_attn_backward, shards), steps, None,
        (dmid1, stream, table1, sums1, *kept(qkv1, p1, o1), a1, a1_other),
        back_specs, [arr(pad_shape, f32)] + ga_outs, [by_group(pad_shape)] + ga_specs,
        back_scratch, back_flops, "attn_backward_1",
    )
    hm1, ga1_mine, ga1_other = after_all((hm1, ga1_mine, ga1_other), e)
    h1 = core_pieces([(ga1_mine, swap_cores(ga1_other)), (gm1_mine, hm1)], last, shards)
    out_other = swap_cores(out)
    e = after(e, out_other, *h1)
    dmid, sums, gm_mine, gm_other = call(
        kernel_mlp_backward, steps, None,
        (e, mid, table, *kept(g_all, slope_all), m0, m0_other),
        [by_group(pad_shape), by_group(pad_shape), tspec, by_group(g_shape), by_group(g_shape), mspec, mspec],
        [arr(pad_shape, f32), arr(table_shape, f32)] + [arr((width, cm), bf16)] * 2,
        [by_group(pad_shape), whole_out(table_shape)] + [whole_out((width, cm))] * 2,
        mlp_sums, 4 * proj_flops * hidden, "mlp_backward",
    )
    middle = groups[:-1][::-1]
    h1 = add_up(after_all(send_pieces(h1, last, shards), dmid)).astype(bf16)
    h1 = pieces_for(h1, middle[0])
    h0m = core_pieces([(gm_mine, swap_cores(gm_other))], last, shards)
    dmid = after(dmid, *h0m, *h1)
    grad, ga_mine, ga_other = call(
        functools.partial(kernel_first_attn_backward, shards), steps, None,
        (dmid, *kept(x_all), table, sums, *kept(qkv, p_all, o_all), a0, a0_other),
        back_specs, [arr(half_shape, bf16)] + ga_outs, [whole_out(half_shape)] + ga_specs,
        back_scratch + [(join_shape, bf16), (g_of(pad_shape), f32)], back_flops, "attn_backward_0",
    )
    h0m = send_pieces(h0m, last, shards)
    h1 = send_pieces(h1, middle[0], shards)
    n = len(h0m)
    got = after_all(h0m + h1 + [ga_mine, ga_other, grad], grad)
    h0m, h1, (ga_mine, ga_other, grad) = got[:n], got[n:-3], got[-3:]
    h0a = core_pieces([(ga_mine, swap_cores(ga_other))], last, shards)
    grad_other = swap_cores(grad)
    h0m = after_all(pieces_for(add_up(h0m).astype(bf16), middle[0]), grad_other, *h0a)
    h0a = send_pieces(h0a, last, shards)
    h0m = send_pieces(h0m, middle[0], shards)
    out_full = both_cores(core, out, out_other, bf16)
    got = after_all(h0a + h0m, out_full)
    h0a, h0m = got[: len(h0a)], got[len(h0a) :]
    h0a = send_pieces(pieces_for(add_up(h0a).astype(bf16), middle[0]), middle[0], shards)
    for group in middle[1:]:
        h0a, h0m, h1 = (
            send_pieces(pieces_for(add_up(h).astype(bf16), group), group, shards) for h in (h0a, h0m, h1)
        )

    grad_full = both_cores(core, grad, grad_other, f32)
    h0a = after_all(h0a, grad_full)
    grads = in_vmem(
        functools.partial(kernel_unpack, len(h1)),
        [x.reshape(per, -1) for h in (h0a, h0m, h1) for x in h],
        [arr(x.shape, f32) for x in raw], [], "unpack",
    )
    grads = [g.transpose(p) for g, p in zip(grads, turned("out"))]
    g1, b1, bp, g2, b2, bd, gq, gb, gp, gu, gbu, gd = grads
    return (
        out_full.transpose(1, 0, 2), grad_full.transpose(1, 0, 2),
        g1, b1, gq, gb, gp, bp, g2, b2, gu, gbu, gd, bd,
    )


def solution(mesh):
    args = (
        P("shard", None, None),
        P("shard", None, None),
        P(None, "shard"),
        P(None, "shard"),
        P(None, "shard", None, "tensor", None),
        P(None, None, "tensor", "shard"),
        P(None, "tensor", None, "shard"),
        P(None, "shard"),
        P(None, "shard"),
        P(None, "shard"),
        P(None, "shard", "tensor"),
        P(None, "tensor", "shard"),
        P(None, "tensor", "shard"),
        P(None, "shard"),
    )
    return jax.shard_map(
        functools.partial(body, shards=mesh.shape["shard"]),
        mesh=mesh,
        in_specs=args,
        out_specs=args,
        check_vma=False,
    )
```

```python
import functools
import math

import jax
import jax.numpy as jnp
from jax import lax
from jax.experimental import pallas as pl
from jax.experimental.pallas import tpu as pltpu
from jax.sharding import PartitionSpec as P

bf16, f32 = jnp.bfloat16, jnp.float32
epsilon = 1e-06
inv_root_two = 0.7071067811865476
inv_root_two_pi = 0.3989422804014327
log2_e = 1.4426950408889634
NN, NT, TN = ((1,), (0,)), ((1,), (1,)), ((0,), (0,))
VMEM_LIMIT = 60 * 2**20
GROUP = 2
HEAD = 64
LANES = 128


def dot(a, b, dims):
    return lax.dot_general(a, b, (dims, ((), ())), preferred_element_type=f32)


QV_AT, UP_AT = 16, 24


def owner_rows(width, shards, place):
    n = lax.broadcasted_iota(jnp.int32, (width, LANES), 0)
    m = lax.broadcasted_iota(jnp.int32, (width, LANES), 1)
    per = width // shards
    return n // per == (m % place) // (place // shards)


def lane_picks(at, unit):
    r = lax.broadcasted_iota(jnp.int32, (LANES, LANES), 0)
    m = lax.broadcasted_iota(jnp.int32, (LANES, LANES), 1)
    return jnp.where(r == at + m % unit, 1.0, 0.0).astype(bf16)


def rank_rows(width, shards):
    r = lax.broadcasted_iota(jnp.int32, (16, width), 0)
    n = lax.broadcasted_iota(jnp.int32, (16, width), 1)
    return jnp.where(n % (width // shards) == r, 1.0, 0.0).astype(bf16)


def unit_rows(rows, columns):
    r = lax.broadcasted_iota(jnp.int32, (rows, columns), 0)
    c = lax.broadcasted_iota(jnp.int32, (rows, columns), 1)
    return jnp.where(r == c, 1.0, 0.0).astype(bf16)


def qv_spots(width, half):
    heads = width // HEAD // 2
    for part in range(2):
        for h in range(heads):
            yield part * heads + h, part * 2 * width + half * (width // 2) + h * HEAD


def up_spots(hidden, half):
    rows = hidden // 2 // LANES
    return [(r, (half * rows + r) * LANES) for r in range(rows)]


def expand_vec(vec_refs, table, shards):
    width, hidden = vec_refs[0].shape[0], table.shape[1]
    table[...] = jnp.zeros_like(table)
    ranks = rank_rows(width, shards)
    for half, ref in enumerate(vec_refs):
        block = ref[...]
        if half == 0:
            table[0:6, 0:width] = dot(unit_rows(16, LANES), block, NT)[0:6]
        for at, place, row, spots in (
            (QV_AT, HEAD, 6, qv_spots(width, half)),
            (UP_AT, LANES, 7, up_spots(hidden, half)),
        ):
            found = dot(block, lane_picks(at, place // shards), NN)
            found = jnp.where(owner_rows(width, shards, place), found, 0.0).astype(bf16)
            found = dot(ranks, found, NN)
            for r, first in spots:
                table[row : row + 1, first : first + place] = found[r : r + 1, :place]


def pack_vec(table, outs, rows, shards):
    width, hidden = outs[0].shape[0], table.shape[1]
    index = lax.broadcasted_iota(jnp.int32, (16, width), 0)
    six = jnp.where(index < 6, table[0:16, :width], 0.0).astype(bf16)
    six = dot(six, unit_rows(16, LANES), TN)
    ranks = rank_rows(width, shards)
    for half, ref in enumerate(outs):
        block = six
        for at, place, row, spots in (
            (QV_AT, HEAD, 6, qv_spots(width, half)),
            (UP_AT, LANES, 7, up_spots(hidden, half)),
        ):
            rows[...] = jnp.zeros_like(rows)
            for r, first in spots:
                rows[r : r + 1, :place] = table[row : row + 1, first : first + place]
            found = dot(ranks, rows[...].astype(bf16), TN)
            lane = lax.broadcasted_iota(jnp.int32, (width, LANES), 1)
            found = jnp.where(owner_rows(width, shards, place) & (lane < place), found, 0.0).astype(bf16)
            block = block + dot(found, lane_picks(at, place // shards), NT)
        ref[...] = block.astype(bf16)


def kernel_pack(
    ln1_gain, ln1_bias, b_proj, ln2_gain, ln2_bias, b_down, w_qkv, b_qv, w_proj, w_up, b_up, w_down,
    first_attn, first_mlp, later, rows, vec,
):
    layers, parts, heads, per, _ = w_qkv.shape
    half = heads * HEAD
    ca, cm = first_attn.shape[1], first_mlp.shape[1]
    for l in range(layers):
        attn, mlp = (first_attn, first_mlp) if l == 0 else (later.at[:, :ca], later.at[:, ca:])
        for h in range(heads):
            for part in range(parts):
                at = part * half + h * HEAD
                attn[:, at : at + HEAD] = w_qkv[l, part, h]
            at = parts * half + h * HEAD
            attn[:, at : at + HEAD] = w_proj[l, h]
        rows[...] = jnp.zeros_like(rows)
        for j, ref in enumerate((ln1_gain, ln1_bias, b_proj, ln2_gain, ln2_bias, b_down)):
            rows[j : j + 1, :per] = ref[l : l + 1, :].astype(f32)
        vec[...] = jnp.zeros_like(vec)
        vec[:, 0:16] = dot(unit_rows(per, LANES), rows[...].astype(bf16), NT)
        unit = b_qv.shape[3]
        for h in range(heads):
            for part in range(2):
                r = part * heads + h
                vec[r : r + 1, QV_AT : QV_AT + unit] = b_qv[l, h, part : part + 1, :].astype(f32)
        unit = b_up.shape[2]
        for r in range(b_up.shape[0]):
            vec[r : r + 1, UP_AT : UP_AT + unit] = b_up[r, l : l + 1, :].astype(f32)
        attn[:, ca - LANES :] = vec[...].astype(bf16)
        mlp[:, : cm // 2] = w_up[l]
        mlp[:, cm // 2 :] = w_down[l]


def kernel_unpack(count, *refs):
    pieces, outs = refs[: 3 * count], refs[3 * count :]
    sixes, (w_qkv, b_qv, w_proj, w_up, b_up, w_down) = outs[:6], outs[6:]
    layers, parts, heads, per, _ = w_qkv.shape
    half = heads * HEAD
    hidden = w_up.shape[2]

    def total(group, cols):
        found = [ref[:, cols].astype(f32) for ref in pieces[group * count : (group + 1) * count]]
        return functools.reduce(lambda a, b: a + b, found)

    ca = parts * half + half + LANES
    for l in range(layers):
        attn, mlp, base = (0, 1, 0) if l == 0 else (2, 2, ca)
        whole_attn = total(attn, slice(0, ca))
        for h in range(heads):
            for part in range(parts):
                at = part * half + h * HEAD
                w_qkv[l, part, h] = whole_attn[:, at : at + HEAD]
            at = parts * half + h * HEAD
            w_proj[l, h] = whole_attn[:, at : at + HEAD]
        vec = whole_attn[:, ca - LANES :]
        columns = vec.T
        for j, ref in enumerate(sixes):
            ref[l : l + 1, :] = columns[j : j + 1, :per]
        unit = b_qv.shape[3]
        for h in range(heads):
            for part in range(2):
                r = part * heads + h
                b_qv[l, h, part : part + 1, :] = vec[r : r + 1, QV_AT : QV_AT + unit]
        unit = b_up.shape[2]
        for r in range(b_up.shape[0]):
            b_up[r, l : l + 1, :] = vec[r : r + 1, UP_AT : UP_AT + unit]
        w_up[l] = total(mlp, slice(base, base + hidden))
        w_down[l] = total(mlp, slice(base + hidden, base + 2 * hidden))


def norm_parts(x):
    c = x - jnp.mean(x, -1, keepdims=True)
    s = lax.rsqrt(jnp.mean(c * c, -1, keepdims=True) + epsilon)
    return c * s, s


def norm_back(dh, u, s, gain):
    t = dh * gain
    return s * (t - jnp.mean(t, -1, keepdims=True) - u * jnp.mean(t * u, -1, keepdims=True))


def row_sum(x):
    return jnp.sum(x, 0, keepdims=True)


def halves_of_lanes(x):
    low = lax.broadcasted_iota(jnp.int32, x.shape, 1) < HEAD
    zero = jnp.zeros_like(x)
    return jnp.where(low, x, zero), jnp.where(low, zero, x)


def probs_t(scores, length):
    row = lax.broadcasted_iota(jnp.int32, scores.shape, 0)
    scores = jnp.where(row < length, scores, -1e30)
    high = jnp.max(scores, 0, keepdims=True)
    e = jnp.exp2((scores - high) * (HEAD**-0.5 * log2_e))
    return (e * (1.0 / jnp.sum(e, 0, keepdims=True))).astype(bf16)


def pair(qkv, width, at):
    return [qkv[:, part * width + at : part * width + at + LANES] for part in range(3)]


def attention(qkv, p_ref, o_ref, width, length):
    images, pairs = qkv.shape[0], width // LANES

    def probs(j):
        found = []
        for g in range(images):
            q, k, _ = pair(qkv.at[g], width, LANES * j)
            found.append([probs_t(dot(k, q_one, NT), length) for q_one in halves_of_lanes(q)])
        return found

    def mix(j, found):
        at = LANES * j
        for g in range(images):
            v = pair(qkv.at[g], width, at)[2]
            parts = [dot(p, v_one, TN) for p, v_one in zip(found[g], halves_of_lanes(v))]
            o_ref[g, :, at : at + LANES] = (parts[0] + parts[1]).astype(bf16)
            for h, p in enumerate(found[g]):
                p_ref[g, 2 * j + h] = p

    in_turn(pairs, probs, mix, 1)


def in_turn(count, first, second, ahead):
    waiting = []
    for j in range(count):
        waiting.append((j, first(j)))
        if len(waiting) > ahead:
            second(*waiting.pop(0))
    for item in waiting:
        second(*item)


def attention_back(qkv, p_ref, do, dz_ref, width):
    images, rows, _ = qkv.shape

    def slopes(j):
        at = LANES * j
        found = []
        for g in range(images):
            v = pair(qkv.at[g], width, at)[2]
            do_pair = do[g * rows : (g + 1) * rows, at : at + LANES]
            for h, v_one in enumerate(halves_of_lanes(v)):
                pf = p_ref[g, 2 * j + h].astype(f32)
                t = pf * dot(v_one, do_pair, NT)
                found.append((t - pf * row_sum(t)).astype(bf16))
        return found

    def products(j, found):
        at = LANES * j
        for g in range(images):
            q, k, _ = pair(qkv.at[g], width, at)
            do_pair = do[g * rows : (g + 1) * rows, at : at + LANES]
            sums = [None] * 3
            split = zip(*(halves_of_lanes(x) for x in (q * HEAD**-0.5, k * HEAD**-0.5, do_pair)))
            for h, (q_one, k_one, do_one) in enumerate(split):
                ds = found[2 * g + h]
                parts = (dot(ds, k_one, TN), dot(ds, q_one, NN), dot(p_ref[g, 2 * j + h], do_one, NN))
                sums = [x if y is None else x + y for x, y in zip(parts, sums)]
            for part in range(3):
                dz_ref[g, :, part * width + at : part * width + at + LANES] = sums[part].astype(bf16)

    in_turn(width // LANES, slopes, products, 1)


def place_attn_weights(a_refs, w_qkv, w_proj):
    width = w_qkv.shape[0]
    half = width // 2
    for i, ref in enumerate(a_refs):
        for part in range(3):
            to = part * width + i * half
            w_qkv[:, to : to + half] = ref[:, part * half : (part + 1) * half]
        w_proj[:, i * half : (i + 1) * half] = ref[:, 3 * half : 4 * half]


def store_attn_grads(acc_qkv, acc_proj, outs):
    width = acc_qkv.shape[0]
    half = width // 2
    for i, ref in enumerate(outs):
        for part in range(3):
            at = part * width + i * half
            ref[:, part * half : (part + 1) * half] = acc_qkv[:, at : at + half].astype(bf16)
        ref[:, 3 * half : 4 * half] = acc_proj[:, i * half : (i + 1) * half].astype(bf16)


def store_mlp_grads(acc_up, acc_down, outs):
    half = acc_up.shape[1] // 2
    for i, ref in enumerate(outs):
        ref[:, :half] = acc_up[:, i * half : (i + 1) * half].astype(bf16)
        ref[:, half:] = acc_down[:, i * half : (i + 1) * half].astype(bf16)


def attn_forward(x, table, w_qkv, w_proj, qkv, p_all, o_all, mid, length):
    group, rows, width = x.shape
    gain, shift = table[0:1, :width], table[1:2, :width]
    xs = x[...].reshape(group * rows, width)
    u, _ = norm_parts(xs)
    h = (u * gain + shift).astype(bf16)
    z = dot(h, w_qkv[...], NN) + table[6:7, : 3 * width]
    qkv[...] = z.astype(bf16).reshape(qkv.shape)
    attention(qkv, p_all, o_all, width, length)
    o = o_all[...].reshape(group * rows, width)
    a = dot(o, w_proj[...], NT)
    mid[...] = (xs + a + table[2:3, :width]).reshape(mid.shape)


def mlp_forward(mid, table, m_refs, g_all, slope_all):
    group, rows, width = mid.shape
    ms = mid[...].reshape(group * rows, width)
    u, _ = norm_parts(ms)
    h = (u * table[3:4, :width] + table[4:5, :width]).astype(bf16)
    half = m_refs[0].shape[1] // 2
    pres = [dot(h, ref[:, :half], NN) for ref in m_refs]
    total = None
    for i, (ref, pre) in enumerate(zip(m_refs, pres)):
        cols = slice(i * half, (i + 1) * half)
        pre = pre + table[7:8, cols]
        phi = 0.5 * (1.0 + lax.erf(pre * inv_root_two))
        g = (pre * phi).astype(bf16)
        g_all[:, :, cols] = g.reshape(group, rows, half)
        slope = phi + pre * jnp.exp(-0.5 * pre * pre) * inv_root_two_pi
        slope_all[:, :, cols] = slope.astype(bf16).reshape(group, rows, half)
        t = dot(g, ref[:, half:], NT)
        total = t if total is None else total + t
    return ms + total + table[5:6, :width]


def mlp_backward(e, mid, table, sums, m_refs, g_all, slope_all, acc_up, acc_down):
    group, rows, width = mid.shape
    half = m_refs[0].shape[1] // 2
    sums[5:6, :width] += row_sum(e)
    e_low = e.astype(bf16)
    u, s = norm_parts(mid[...].reshape(group * rows, width))
    gain = table[3:4, :width]
    h = (u * gain + table[4:5, :width]).astype(bf16)
    dgs = [dot(e_low, ref[:, half:], NN) for ref in m_refs]
    dpres = []
    for i, dg in enumerate(dgs):
        slope = slope_all[:, :, i * half : (i + 1) * half].reshape(group * rows, half).astype(f32)
        dpres.append((dg * slope).astype(bf16))
    dh = dot(dpres[0], m_refs[0][:, :half], NT) + dot(dpres[1], m_refs[1][:, :half], NT)
    for i, dpre in enumerate(dpres):
        cols = slice(i * half, (i + 1) * half)
        acc_up[:, cols] += dot(h, dpre, TN)
        acc_down[:, cols] += dot(e_low, g_all[:, :, cols].reshape(group * rows, half), TN)
        sums[7:8, cols] += row_sum(dpre.astype(f32))
    sums[3:4, :width] += row_sum(dh * u)
    sums[4:5, :width] += row_sum(dh)
    return e + norm_back(dh, u, s, gain)


def attn_backward(dmid, x, table, sums, w_qkv, w_proj, qkv, p_all, o_all, dz, acc_qkv, acc_proj):
    group, rows, width = x.shape
    sums[2:3, :width] += row_sum(dmid)
    da = dmid.astype(bf16)
    do = dot(da, w_proj[...], NN).astype(bf16)
    acc_proj[...] += dot(da, o_all[...].reshape(group * rows, width), TN)
    u, s = norm_parts(x[...].reshape(group * rows, width))
    gain = table[0:1, :width]
    h = (u * gain + table[1:2, :width]).astype(bf16)
    attention_back(qkv, p_all, do, dz, width)
    dzs = dz[...].reshape(group * rows, 3 * width)
    dh = dot(dzs, w_qkv[...], NT)
    acc_qkv[...] += dot(h, dzs, TN)
    sums[6:7, : 3 * width] += row_sum(dzs.astype(f32))
    sums[0:1, :width] += row_sum(dh * u)
    sums[1:2, :width] += row_sum(dh)
    return dmid + norm_back(dh, u, s, gain)


def turn_rows(images, tokens):
    r = lax.broadcasted_iota(jnp.int32, (tokens * images, images * tokens), 0)
    c = lax.broadcasted_iota(jnp.int32, (tokens * images, images * tokens), 1)
    return jnp.where((r % images == c // tokens) & (r // images == c % tokens), 1.0, 0.0).astype(bf16)


def token_runs(length):
    return [(at, min(32, length - at)) for at in range(0, length, 32)]


def spread_images(ref, x_all):
    length, images, width = ref.shape
    x_all[...] = jnp.zeros_like(x_all)
    turn = turn_rows(images, 32)
    for at, count in token_runs(length):
        part = ref[at : at + count].astype(f32).reshape(count * images, width).astype(bf16)
        whole_turn = turn if count == 32 else turn_rows(images, 32)[: count * images]
        found = dot(whole_turn, part, TN)
        for i in range(images):
            x_all[i, at : at + count, :] = found[i * 32 : i * 32 + count].astype(x_all.dtype)


def join_images(all_images, out):
    length, images, width = out.shape
    turn = turn_rows(images, 32)
    for at, count in token_runs(length):
        rows = jnp.concatenate([all_images[i, at : at + 32, :] for i in range(images)], 0)
        found = dot(turn[: count * images], rows, NN).reshape(count, images, width)
        out[at : at + count] = found.astype(out.dtype)


def kernel_place(core, mine, other, full):
    images = mine.shape[1]
    for c in range(2):
        @pl.when(core[0] == c)
        def _():
            full[:, c * images : (c + 1) * images, :] = mine[...].astype(full.dtype)
            full[:, (1 - c) * images : (2 - c) * images, :] = other[...].astype(full.dtype)


def vec_of(ref):
    return ref.at[:, ref.shape[1] - LANES :]


def start_attn_forward(a_mine, a_other, table, w_qkv, w_proj, shards):
    place_attn_weights((a_mine, a_other), w_qkv, w_proj)
    expand_vec([vec_of(r) for r in (a_mine, a_other)], table, shards)


def kernel_spread(core, tok, cot, x_all, cot_all):
    spread_images(tok, x_all)
    spread_images(cot, cot_all)


def kernel_first_attn_forward(
    shards, length, x_low, a_mine, a_other, qkv, p_all, o_all, mid, table, w_qkv, w_proj, x
):
    @pl.when(pl.program_id(0) == 0)
    def _():
        start_attn_forward(a_mine, a_other, table, w_qkv, w_proj, shards)

    x[...] = x_low[...].astype(f32)
    attn_forward(x, table, w_qkv, w_proj, qkv, p_all, o_all, mid, length)


def kernel_attn_forward(shards, length, x, a_mine, a_other, qkv, p_all, o_all, mid, table, w_qkv, w_proj):
    @pl.when(pl.program_id(0) == 0)
    def _():
        start_attn_forward(a_mine, a_other, table, w_qkv, w_proj, shards)

    attn_forward(x, table, w_qkv, w_proj, qkv, p_all, o_all, mid, length)


def kernel_mlp_forward(mid, table, m_mine, m_other, stream, g_all, slope_all):
    out = mlp_forward(mid, table, (m_mine, m_other), g_all, slope_all)
    stream[...] = out.reshape(stream.shape)


def kernel_mlp_both(
    mid, cot, table, m_mine, m_other,
    out, dmid, sums, gm_mine, gm_other, g_all, slope_all, out_all, acc_up, acc_down,
):
    step = pl.program_id(0)

    @pl.when(step == 0)
    def _():
        for ref in (out_all, sums, acc_up, acc_down):
            ref[...] = jnp.zeros_like(ref)

    group, rows, width = mid.shape
    m_refs = (m_mine, m_other)
    result = mlp_forward(mid, table, m_refs, g_all, slope_all)
    for g in range(group):
        out_all[step * group + g, :rows, :] = result[g * rows : (g + 1) * rows].astype(bf16)
    e = cot[...].astype(f32).reshape(group * rows, width)
    back = mlp_backward(e, mid, table, sums, m_refs, g_all, slope_all, acc_up, acc_down)
    dmid[...] = back.reshape(dmid.shape)

    @pl.when(step == pl.num_programs(0) - 1)
    def _():
        store_mlp_grads(acc_up, acc_down, (gm_mine, gm_other))
        join_images(out_all, out)


def kernel_mlp_backward(
    e, mid, table, g_all, slope_all, m_mine, m_other,
    dmid, sums, gm_mine, gm_other, acc_up, acc_down,
):
    step = pl.program_id(0)

    @pl.when(step == 0)
    def _():
        for ref in (sums, acc_up, acc_down):
            ref[...] = jnp.zeros_like(ref)

    group, rows, width = mid.shape
    back = mlp_backward(
        e[...].reshape(group * rows, width), mid, table, sums, (m_mine, m_other),
        g_all, slope_all, acc_up, acc_down,
    )
    dmid[...] = back.reshape(dmid.shape)

    @pl.when(step == pl.num_programs(0) - 1)
    def _():
        store_mlp_grads(acc_up, acc_down, (gm_mine, gm_other))


def attn_backward_step(
    shards, dmid, x, table, sums_in, qkv, p_all, o_all, a_mine, a_other,
    ga_mine, ga_other, sums, vec_rows, w_qkv, w_proj, dz, acc_qkv, acc_proj, keep, finish,
):
    step = pl.program_id(0)

    @pl.when(step == 0)
    def _():
        place_attn_weights((a_mine, a_other), w_qkv, w_proj)
        sums[...] = sums_in[...]
        for ref in (acc_qkv, acc_proj):
            ref[...] = jnp.zeros_like(ref)

    group, rows, width = x.shape
    back = attn_backward(
        dmid[...].reshape(group * rows, width), x, table, sums, w_qkv, w_proj,
        qkv, p_all, o_all, dz, acc_qkv, acc_proj,
    )
    keep(back)

    @pl.when(step == pl.num_programs(0) - 1)
    def _():
        store_attn_grads(acc_qkv, acc_proj, (ga_mine, ga_other))
        pack_vec(sums, [vec_of(r) for r in (ga_mine, ga_other)], vec_rows, shards)
        finish()


def kernel_attn_backward(shards, dmid, x, table, sums_in, qkv, p_all, o_all, a_mine, a_other, e_out, *rest):
    def keep(back):
        e_out[...] = back.reshape(e_out.shape)

    attn_backward_step(
        shards, dmid, x, table, sums_in, qkv, p_all, o_all, a_mine, a_other, *rest, keep, lambda: None
    )


def kernel_first_attn_backward(
    shards, dmid, x_low, table, sums_in, qkv, p_all, o_all, a_mine, a_other, grad, *rest
):
    *rest, grad_all, x = rest
    step = pl.program_id(0)
    group, rows, _ = x.shape

    @pl.when(step == 0)
    def _():
        grad_all[...] = jnp.zeros_like(grad_all)

    def keep(back):
        for g in range(group):
            grad_all[step * group + g, :rows, :] = back[g * rows : (g + 1) * rows].astype(bf16)

    x[...] = x_low[...].astype(f32)
    attn_backward_step(
        shards, dmid, x, table, sums_in, qkv, p_all, o_all, a_mine, a_other, *rest, keep,
        lambda: join_images(grad_all, grad),
    )


def whole(shape):
    zeros = (0,) * len(shape)
    return pl.BlockSpec(shape, lambda i, *_: zeros, pipeline_mode=pl.Buffered(1))


def whole_out(shape):
    zeros = (0,) * len(shape)
    return pl.BlockSpec(shape, lambda i, *_: zeros)


def by_group(shape):
    rest = (0,) * (len(shape) - 1)
    return pl.BlockSpec((GROUP, *shape[1:]), lambda i, *_: (i, *rest))


def of_core(shape):
    return pl.BlockSpec(
        (shape[0], shape[1] // 2, shape[2]), lambda i, core: (0, core[0], 0), pipeline_mode=pl.Buffered(1)
    )


def call(kernel, steps, core, args, in_specs, outs, out_specs, scratch, flops, name, limit=32):
    moved = sum(a.size * a.dtype.itemsize for a in args)
    moved += sum(math.prod(o.shape) * o.dtype.itemsize for o in outs)
    return pl.pallas_call(
        kernel,
        out_shape=outs,
        grid_spec=pltpu.PrefetchScalarGridSpec(
            num_scalar_prefetch=0 if core is None else 1,
            grid=(steps,),
            in_specs=in_specs,
            out_specs=out_specs,
            scratch_shapes=[pltpu.VMEM(s, d) for s, d in scratch],
        ),
        compiler_params=pltpu.CompilerParams(vmem_limit_bytes=limit * 2**20),
        cost_estimate=pl.CostEstimate(flops=int(flops), bytes_accessed=int(moved), transcendentals=0),
        name=name,
    )(*(() if core is None else (core,)), *args)


def both_cores(core, mine, other, dtype, parts=4):
    length, images, width = mine.shape
    run = -(-length // parts)
    block = pl.BlockSpec((run, images, width), lambda i, core: (i, 0, 0))
    return pl.pallas_call(
        kernel_place,
        out_shape=arr((length, 2 * images, width), dtype),
        grid_spec=pltpu.PrefetchScalarGridSpec(
            num_scalar_prefetch=1,
            grid=(parts,),
            in_specs=[block, block],
            out_specs=pl.BlockSpec((run, 2 * images, width), lambda i, core: (i, 0, 0)),
        ),
        compiler_params=pltpu.CompilerParams(vmem_limit_bytes=16 * 2**20),
        name="both_cores",
    )(core, mine, other)


def in_vmem(kernel, args, outs, scratch, name):
    spec = pl.BlockSpec(memory_space=pltpu.VMEM)
    return pl.pallas_call(
        kernel,
        out_shape=outs,
        in_specs=[spec] * len(args),
        out_specs=[spec] * len(outs),
        scratch_shapes=[pltpu.VMEM(s, d) for s, d in scratch],
        compiler_params=pltpu.CompilerParams(vmem_limit_bytes=VMEM_LIMIT),
        name=name,
    )(*args)


def arr(shape, dtype):
    return jax.ShapeDtypeStruct(shape, dtype)


def in_hbm(shape, dtype):
    return pltpu.HBM(shape, dtype)


def kept(*arrays):
    return [pltpu.with_memory_space_constraint(x, pltpu.HBM) for x in arrays]


def after(x, *others):
    return lax.optimization_barrier((x, *others))[0]


def after_all(xs, *others):
    return list(lax.optimization_barrier((*xs, *others))[: len(xs)])


def bit_groups(shards):
    bits = [1 << k for k in range(shards.bit_length() - 1)]
    groups = [bits[k : k + 2] for k in range(0, len(bits), 2)]
    return groups[::-1]


def masks_of(group):
    masks = [0]
    for b in group:
        masks = masks + [m | b for m in masks]
    return masks


def exchange(x, mask, shards):
    return lax.ppermute(x, "shard", [(i, i ^ mask) for i in range(shards)])


def swap_cores(x):
    return lax.ppermute(x, "tensor", [(0, 1), (1, 0)])


def fetch(x, group, shards):
    return [x if m == 0 else exchange(x, m, shards) for m in masks_of(group)]


def in_order(got, group):
    me = lax.axis_index("shard")
    for k, b in enumerate(group):
        flag = (me & b) != 0
        got = [jnp.where(flag, got[i ^ (1 << k)], got[i]) for i in range(len(got))]
    return jnp.stack(got, 1).reshape(-1, *got[0].shape[1:])


def flat_rows(x):
    return x.reshape(-1, x.shape[-1])


def pieces_for(h, group):
    count = len(masks_of(group))
    h = h.reshape(-1, count, *h.shape[1:])
    here = (lax.axis_index("shard") // group[0]) % count
    return [lax.dynamic_index_in_dim(h, here ^ k, 1, keepdims=False) for k in range(count)]


def send_pieces(pieces, group, shards):
    return [p if m == 0 else exchange(p, m, shards) for p, m in zip(pieces, masks_of(group))]


def add_up(found):
    return functools.reduce(lambda a, b: a + b, [f.astype(f32) for f in found])


def core_pieces(pairs, group, shards):
    cut = [
        [pieces_for(x.reshape(shards, x.shape[0] // shards, -1), group) for x in pair] for pair in pairs
    ]
    return [
        jnp.concatenate([add_up([mine[k], other[k]]).astype(bf16) for mine, other in cut], -1)
        for k in range(len(masks_of(group)))
    ]


def body(
    tokens, cotangent, ln1_gain, ln1_bias, w_qkv, b_qv, w_proj, b_proj,
    ln2_gain, ln2_bias, w_up, b_up, w_down, b_down, *, shards,
):
    images_all, length, width = tokens.shape
    layers, per = ln1_gain.shape
    images = images_all // 2
    steps = images // GROUP
    rows = -(-length // 16) * 16
    hidden = 2 * w_up.shape[2]
    heads = width // HEAD
    ca, cm = 2 * width + LANES, hidden
    t = lax.axis_index("tensor")
    core = t.astype(jnp.int32).reshape(1)
    groups = bit_groups(shards)

    def turned(which):
        one = [(0, 1)] * 6 + [(0, 2, 3, 1, 4), (0, 2, 1, 3), (0, 1, 3, 2), (0, 1, 2), (1, 0, 2), (0, 2, 1)]
        back = [tuple(sorted(range(len(p)), key=lambda i: p[i])) for p in one]
        return one if which == "in" else back

    raw = (ln1_gain, ln1_bias, b_proj, ln2_gain, ln2_bias, b_down, w_qkv, b_qv, w_proj, w_up, b_up, w_down)
    raw = [x.transpose(p) for x, p in zip(raw, turned("in"))]
    first_attn, first_mlp, later = in_vmem(
        kernel_pack, raw, [arr((per, c), bf16) for c in (ca, cm, ca + cm)],
        [((16, LANES), f32), ((per, LANES), f32)], "pack",
    )

    tok = images * length
    proj_flops = 2 * tok * width
    attn_flops = images * heads * 4 * length * length * HEAD
    aspec, mspec = whole((width, ca)), whole((width, cm))
    table_shape = (16, hidden)
    tspec = whole(table_shape)
    half_shape = (length, images, width)
    pad_shape = (images, rows, width)
    join_shape = (images, -(-length // 32) * 32, width)
    vec_shape = (16, LANES)
    qkv_shape = (images, rows, 3 * width)
    p_shape = (images, heads, rows, rows)
    g_shape = (images, rows, hidden)
    tokens_in, cotangent_in = kept(*(x.transpose(1, 0, 2) for x in (tokens, cotangent)))

    def g_of(shape):
        return (GROUP, *shape[1:])


    x_all, cot_all = call(
        kernel_spread, 1, core, (tokens_in, cotangent_in), [of_core(tokens_in.shape)] * 2,
        [in_hbm(pad_shape, bf16)] * 2, [whole_out(pad_shape)] * 2, [], 0, "spread", 16,
    )

    def early(x, stages):
        x = x[None]
        for group in stages:
            x = in_order(fetch(x, group, shards), group)
        return x

    last, before = groups[-1], groups[-2]
    got_z0 = fetch(early(first_attn, groups[:-2]), before, shards)
    z0 = in_order(after_all(got_z0, x_all, cot_all), before)
    got_m0 = fetch(early(after(first_mlp, z0), groups[:-2]), before, shards)
    got_a0 = fetch(z0, last, shards)
    l1 = early(after(later, z0), groups[:-2])
    near = [exchange(l1, before[0], shards)]
    a0 = flat_rows(in_order(got_a0, last))
    a0_other = swap_cores(a0)
    *got_m0, near[0] = after_all(got_m0 + near, a0)
    far = after(l1, a0)
    got_l1 = [l1] + near + [exchange(far, m, shards) for m in masks_of(before)[2:]]
    got_m0 = fetch(in_order(got_m0, before), last, shards)

    saved = [in_hbm(qkv_shape, bf16), in_hbm(p_shape, bf16), in_hbm(pad_shape, bf16),
             arr(pad_shape, f32), arr(table_shape, f32)]
    saved_specs = [by_group(qkv_shape), by_group(p_shape), by_group(pad_shape), by_group(pad_shape),
                   whole_out(table_shape)]
    attn_weights = [((width, 3 * width), bf16), ((width, width), bf16)]
    mlp_sums = [((width, hidden), f32), ((width, hidden), f32)]
    forward_flops = 4 * proj_flops * width + attn_flops
    qkv, p_all, o_all, mid, table = call(
        functools.partial(kernel_first_attn_forward, shards, length), steps, None,
        (*kept(x_all), a0, a0_other),
        [by_group(pad_shape), aspec, aspec], saved, saved_specs,
        attn_weights + [(g_of(pad_shape), f32)], forward_flops, "attn_forward_0",
    )
    got = after_all(got_m0 + got_l1, mid)
    m0, l1 = got[: len(got_m0)], got[len(got_m0) :]
    m0 = flat_rows(in_order(m0, last))
    m0_other = swap_cores(m0)
    l1 = in_order(l1, before)
    got_a1 = fetch(l1[:, :, :ca], last, shards)
    stream, g_all, slope_all = call(
        kernel_mlp_forward, steps, None,
        (mid, table, m0, m0_other),
        [by_group(pad_shape), tspec, mspec, mspec],
        [arr(pad_shape, f32), in_hbm(g_shape, bf16), in_hbm(g_shape, bf16)],
        [by_group(pad_shape), by_group(g_shape), by_group(g_shape)],
        [], 2 * proj_flops * hidden, "mlp_forward",
    )
    a1 = flat_rows(in_order(after_all(got_a1, stream), last))
    a1_other = swap_cores(a1)
    got_m1 = fetch(after(l1[:, :, ca:], a1), last, shards)
    qkv1, p1, o1, mid1, table1 = call(
        functools.partial(kernel_attn_forward, shards, length), steps, None,
        (stream, a1, a1_other),
        [by_group(pad_shape), aspec, aspec], saved, saved_specs,
        attn_weights, forward_flops, "attn_forward_1",
    )
    m1 = flat_rows(in_order(after_all(got_m1, mid1), last))
    m1_other = swap_cores(m1)
    out, dmid1, sums1, gm1_mine, gm1_other = call(
        kernel_mlp_both, steps, None,
        (mid1, *kept(cot_all), table1, m1, m1_other),
        [by_group(pad_shape), by_group(pad_shape), tspec, mspec, mspec],
        [arr(half_shape, bf16), arr(pad_shape, f32), arr(table_shape, f32)] + [arr((width, cm), bf16)] * 2,
        [whole_out(half_shape), by_group(pad_shape), whole_out(table_shape)] + [whole_out((width, cm))] * 2,
        [(g_of(g_shape), bf16), (g_of(g_shape), bf16), (join_shape, bf16)] + mlp_sums,
        6 * proj_flops * hidden, "mlp_both", 40,
    )
    back_specs = [by_group(pad_shape), by_group(pad_shape), tspec, tspec, by_group(qkv_shape),
                  by_group(p_shape), by_group(pad_shape), aspec, aspec]
    back_scratch = [
        (table_shape, f32), (vec_shape, f32), *attn_weights, (g_of(qkv_shape), bf16),
        ((width, 3 * width), f32), ((width, width), f32),
    ]
    ga_outs, ga_specs = [arr((width, ca), bf16)] * 2, [whole_out((width, ca))] * 2
    back_flops = 8 * proj_flops * width + 2.5 * attn_flops
    hm1 = swap_cores(gm1_other)
    e, ga1_mine, ga1_other = call(
        functools.partial(kernel_attn_backward, shards), steps, None,
        (dmid1, stream, table1, sums1, *kept(qkv1, p1, o1), a1, a1_other),
        back_specs, [arr(pad_shape, f32)] + ga_outs, [by_group(pad_shape)] + ga_specs,
        back_scratch, back_flops, "attn_backward_1",
    )
    hm1, ga1_mine, ga1_other = after_all((hm1, ga1_mine, ga1_other), e)
    h1 = core_pieces([(ga1_mine, swap_cores(ga1_other)), (gm1_mine, hm1)], last, shards)
    out_other = swap_cores(out)
    e = after(e, out_other, *h1)
    dmid, sums, gm_mine, gm_other = call(
        kernel_mlp_backward, steps, None,
        (e, mid, table, *kept(g_all, slope_all), m0, m0_other),
        [by_group(pad_shape), by_group(pad_shape), tspec, by_group(g_shape), by_group(g_shape), mspec, mspec],
        [arr(pad_shape, f32), arr(table_shape, f32)] + [arr((width, cm), bf16)] * 2,
        [by_group(pad_shape), whole_out(table_shape)] + [whole_out((width, cm))] * 2,
        mlp_sums, 4 * proj_flops * hidden, "mlp_backward",
    )
    middle = groups[:-1][::-1]
    h1 = add_up(after_all(send_pieces(h1, last, shards), dmid)).astype(bf16)
    h1 = pieces_for(h1, middle[0])
    h0m = core_pieces([(gm_mine, swap_cores(gm_other))], last, shards)
    dmid = after(dmid, *h0m, *h1)
    grad, ga_mine, ga_other = call(
        functools.partial(kernel_first_attn_backward, shards), steps, None,
        (dmid, *kept(x_all), table, sums, *kept(qkv, p_all, o_all), a0, a0_other),
        back_specs, [arr(half_shape, bf16)] + ga_outs, [whole_out(half_shape)] + ga_specs,
        back_scratch + [(join_shape, bf16), (g_of(pad_shape), f32)], back_flops, "attn_backward_0",
    )
    h0m = send_pieces(h0m, last, shards)
    h1 = send_pieces(h1, middle[0], shards)
    n = len(h0m)
    got = after_all(h0m + h1 + [ga_mine, ga_other, grad], grad)
    h0m, h1, (ga_mine, ga_other, grad) = got[:n], got[n:-3], got[-3:]
    h0a = core_pieces([(ga_mine, swap_cores(ga_other))], last, shards)
    grad_other = swap_cores(after(grad, *h0a))
    h0m = after_all(pieces_for(add_up(h0m).astype(bf16), middle[0]), grad_other, *h0a)
    h0a = send_pieces(h0a, last, shards)
    h0m = send_pieces(h0m, middle[0], shards)
    out_full = both_cores(core, out, out_other, bf16)
    got = after_all(h0a + h0m, out_full)
    h0a, h0m = got[: len(h0a)], got[len(h0a) :]
    h0a = send_pieces(pieces_for(add_up(h0a).astype(bf16), middle[0]), middle[0], shards)
    for group in middle[1:]:
        h0a, h0m, h1 = (
            send_pieces(pieces_for(add_up(h).astype(bf16), group), group, shards) for h in (h0a, h0m, h1)
        )

    grad_full = both_cores(core, grad, grad_other, f32)
    h0a = after_all(h0a, grad_full)
    grads = in_vmem(
        functools.partial(kernel_unpack, len(h1)),
        [x.reshape(per, -1) for h in (h0a, h0m, h1) for x in h],
        [arr(x.shape, f32) for x in raw], [], "unpack",
    )
    grads = [g.transpose(p) for g, p in zip(grads, turned("out"))]
    g1, b1, bp, g2, b2, bd, gq, gb, gp, gu, gbu, gd = grads
    return (
        out_full.transpose(1, 0, 2), grad_full.transpose(1, 0, 2),
        g1, b1, gq, gb, gp, bp, g2, b2, gu, gbu, gd, bd,
    )


def solution(mesh):
    args = (
        P("shard", None, None),
        P("shard", None, None),
        P(None, "shard"),
        P(None, "shard"),
        P(None, "shard", None, "tensor", None),
        P(None, None, "tensor", "shard"),
        P(None, "tensor", None, "shard"),
        P(None, "shard"),
        P(None, "shard"),
        P(None, "shard"),
        P(None, "shard", "tensor"),
        P(None, "tensor", "shard"),
        P(None, "tensor", "shard"),
        P(None, "shard"),
    )
    return jax.shard_map(
        functools.partial(body, shards=mesh.shape["shard"]),
        mesh=mesh,
        in_specs=args,
        out_specs=args,
        check_vma=False,
    )
```

```python
import functools
import math

import jax
import jax.numpy as jnp
from jax import lax
from jax.experimental import pallas as pl
from jax.experimental.pallas import tpu as pltpu
from jax.sharding import PartitionSpec as P

bf16, f32 = jnp.bfloat16, jnp.float32
epsilon = 1e-06
inv_root_two = 0.7071067811865476
inv_root_two_pi = 0.3989422804014327
log2_e = 1.4426950408889634
NN, NT, TN = ((1,), (0,)), ((1,), (1,)), ((0,), (0,))
VMEM_LIMIT = 60 * 2**20
GROUP = 2
HEAD = 64
LANES = 128


def dot(a, b, dims):
    return lax.dot_general(a, b, (dims, ((), ())), preferred_element_type=f32)


QV_AT, UP_AT = 16, 24


def owner_rows(width, shards, place):
    n = lax.broadcasted_iota(jnp.int32, (width, LANES), 0)
    m = lax.broadcasted_iota(jnp.int32, (width, LANES), 1)
    per = width // shards
    return n // per == (m % place) // (place // shards)


def lane_picks(at, unit):
    r = lax.broadcasted_iota(jnp.int32, (LANES, LANES), 0)
    m = lax.broadcasted_iota(jnp.int32, (LANES, LANES), 1)
    return jnp.where(r == at + m % unit, 1.0, 0.0).astype(bf16)


def rank_rows(width, shards):
    r = lax.broadcasted_iota(jnp.int32, (16, width), 0)
    n = lax.broadcasted_iota(jnp.int32, (16, width), 1)
    return jnp.where(n % (width // shards) == r, 1.0, 0.0).astype(bf16)


def unit_rows(rows, columns):
    r = lax.broadcasted_iota(jnp.int32, (rows, columns), 0)
    c = lax.broadcasted_iota(jnp.int32, (rows, columns), 1)
    return jnp.where(r == c, 1.0, 0.0).astype(bf16)


def qv_spots(width, half):
    heads = width // HEAD // 2
    for part in range(2):
        for h in range(heads):
            yield part * heads + h, part * 2 * width + half * (width // 2) + h * HEAD


def up_spots(hidden, half):
    rows = hidden // 2 // LANES
    return [(r, (half * rows + r) * LANES) for r in range(rows)]


def expand_vec(vec_refs, table, shards):
    width, hidden = vec_refs[0].shape[0], table.shape[1]
    table[...] = jnp.zeros_like(table)
    ranks = rank_rows(width, shards)
    for half, ref in enumerate(vec_refs):
        block = ref[...]
        if half == 0:
            table[0:6, 0:width] = dot(unit_rows(16, LANES), block, NT)[0:6]
        for at, place, row, spots in (
            (QV_AT, HEAD, 6, qv_spots(width, half)),
            (UP_AT, LANES, 7, up_spots(hidden, half)),
        ):
            found = dot(block, lane_picks(at, place // shards), NN)
            found = jnp.where(owner_rows(width, shards, place), found, 0.0).astype(bf16)
            found = dot(ranks, found, NN)
            for r, first in spots:
                table[row : row + 1, first : first + place] = found[r : r + 1, :place]


def pack_vec(table, outs, rows, shards):
    width, hidden = outs[0].shape[0], table.shape[1]
    index = lax.broadcasted_iota(jnp.int32, (16, width), 0)
    six = jnp.where(index < 6, table[0:16, :width], 0.0).astype(bf16)
    six = dot(six, unit_rows(16, LANES), TN)
    ranks = rank_rows(width, shards)
    for half, ref in enumerate(outs):
        block = six
        for at, place, row, spots in (
            (QV_AT, HEAD, 6, qv_spots(width, half)),
            (UP_AT, LANES, 7, up_spots(hidden, half)),
        ):
            rows[...] = jnp.zeros_like(rows)
            for r, first in spots:
                rows[r : r + 1, :place] = table[row : row + 1, first : first + place]
            found = dot(ranks, rows[...].astype(bf16), TN)
            lane = lax.broadcasted_iota(jnp.int32, (width, LANES), 1)
            found = jnp.where(owner_rows(width, shards, place) & (lane < place), found, 0.0).astype(bf16)
            block = block + dot(found, lane_picks(at, place // shards), NT)
        ref[...] = block.astype(bf16)


def kernel_pack(
    ln1_gain, ln1_bias, b_proj, ln2_gain, ln2_bias, b_down, w_qkv, b_qv, w_proj, w_up, b_up, w_down,
    first_attn, first_mlp, later, rows, vec,
):
    layers, parts, heads, per, _ = w_qkv.shape
    half = heads * HEAD
    ca, cm = first_attn.shape[1], first_mlp.shape[1]
    for l in range(layers):
        attn, mlp = (first_attn, first_mlp) if l == 0 else (later.at[:, :ca], later.at[:, ca:])
        for h in range(heads):
            for part in range(parts):
                at = part * half + h * HEAD
                attn[:, at : at + HEAD] = w_qkv[l, part, h]
            at = parts * half + h * HEAD
            attn[:, at : at + HEAD] = w_proj[l, h]
        rows[...] = jnp.zeros_like(rows)
        for j, ref in enumerate((ln1_gain, ln1_bias, b_proj, ln2_gain, ln2_bias, b_down)):
            rows[j : j + 1, :per] = ref[l : l + 1, :].astype(f32)
        vec[...] = jnp.zeros_like(vec)
        vec[:, 0:16] = dot(unit_rows(per, LANES), rows[...].astype(bf16), NT)
        unit = b_qv.shape[3]
        for h in range(heads):
            for part in range(2):
                r = part * heads + h
                vec[r : r + 1, QV_AT : QV_AT + unit] = b_qv[l, h, part : part + 1, :].astype(f32)
        unit = b_up.shape[2]
        for r in range(b_up.shape[0]):
            vec[r : r + 1, UP_AT : UP_AT + unit] = b_up[r, l : l + 1, :].astype(f32)
        attn[:, ca - LANES :] = vec[...].astype(bf16)
        mlp[:, : cm // 2] = w_up[l]
        mlp[:, cm // 2 :] = w_down[l]


def kernel_unpack(count, *refs):
    pieces, outs = refs[: 3 * count], refs[3 * count :]
    sixes, (w_qkv, b_qv, w_proj, w_up, b_up, w_down) = outs[:6], outs[6:]
    layers, parts, heads, per, _ = w_qkv.shape
    half = heads * HEAD
    hidden = w_up.shape[2]

    def total(group, cols):
        found = [ref[:, cols].astype(f32) for ref in pieces[group * count : (group + 1) * count]]
        return functools.reduce(lambda a, b: a + b, found)

    ca = parts * half + half + LANES
    for l in range(layers):
        attn, mlp, base = (0, 1, 0) if l == 0 else (2, 2, ca)
        whole_attn = total(attn, slice(0, ca))
        for h in range(heads):
            for part in range(parts):
                at = part * half + h * HEAD
                w_qkv[l, part, h] = whole_attn[:, at : at + HEAD]
            at = parts * half + h * HEAD
            w_proj[l, h] = whole_attn[:, at : at + HEAD]
        vec = whole_attn[:, ca - LANES :]
        columns = vec.T
        for j, ref in enumerate(sixes):
            ref[l : l + 1, :] = columns[j : j + 1, :per]
        unit = b_qv.shape[3]
        for h in range(heads):
            for part in range(2):
                r = part * heads + h
                b_qv[l, h, part : part + 1, :] = vec[r : r + 1, QV_AT : QV_AT + unit]
        unit = b_up.shape[2]
        for r in range(b_up.shape[0]):
            b_up[r, l : l + 1, :] = vec[r : r + 1, UP_AT : UP_AT + unit]
        w_up[l] = total(mlp, slice(base, base + hidden))
        w_down[l] = total(mlp, slice(base + hidden, base + 2 * hidden))


def norm_parts(x):
    c = x - jnp.mean(x, -1, keepdims=True)
    s = lax.rsqrt(jnp.mean(c * c, -1, keepdims=True) + epsilon)
    return c * s, s


def norm_back(dh, u, s, gain):
    t = dh * gain
    return s * (t - jnp.mean(t, -1, keepdims=True) - u * jnp.mean(t * u, -1, keepdims=True))


def row_sum(x):
    return jnp.sum(x, 0, keepdims=True)


def halves_of_lanes(x):
    low = lax.broadcasted_iota(jnp.int32, x.shape, 1) < HEAD
    zero = jnp.zeros_like(x)
    return jnp.where(low, x, zero), jnp.where(low, zero, x)


def probs_t(scores, length):
    row = lax.broadcasted_iota(jnp.int32, scores.shape, 0)
    scores = jnp.where(row < length, scores, -1e30)
    high = jnp.max(scores, 0, keepdims=True)
    e = jnp.exp2((scores - high) * (HEAD**-0.5 * log2_e))
    return (e * (1.0 / jnp.sum(e, 0, keepdims=True))).astype(bf16)


def pair(qkv, width, at):
    return [qkv[:, part * width + at : part * width + at + LANES] for part in range(3)]


def attention(qkv, p_ref, o_ref, width, length):
    images, pairs = qkv.shape[0], width // LANES

    def probs(j):
        found = []
        for g in range(images):
            q, k, _ = pair(qkv.at[g], width, LANES * j)
            found.append([probs_t(dot(k, q_one, NT), length) for q_one in halves_of_lanes(q)])
        return found

    def mix(j, found):
        at = LANES * j
        for g in range(images):
            v = pair(qkv.at[g], width, at)[2]
            parts = [dot(p, v_one, TN) for p, v_one in zip(found[g], halves_of_lanes(v))]
            o_ref[g, :, at : at + LANES] = (parts[0] + parts[1]).astype(bf16)
            for h, p in enumerate(found[g]):
                p_ref[g, 2 * j + h] = p

    in_turn(pairs, probs, mix, 1)


def in_turn(count, first, second, ahead):
    waiting = []
    for j in range(count):
        waiting.append((j, first(j)))
        if len(waiting) > ahead:
            second(*waiting.pop(0))
    for item in waiting:
        second(*item)


def attention_back(qkv, p_ref, do, dz_ref, width):
    images, rows, _ = qkv.shape

    def slopes(j):
        at = LANES * j
        found = []
        for g in range(images):
            v = pair(qkv.at[g], width, at)[2]
            do_pair = do[g * rows : (g + 1) * rows, at : at + LANES]
            for h, v_one in enumerate(halves_of_lanes(v)):
                pf = p_ref[g, 2 * j + h].astype(f32)
                t = pf * dot(v_one, do_pair, NT)
                found.append((t - pf * row_sum(t)).astype(bf16))
        return found

    def products(j, found):
        at = LANES * j
        for g in range(images):
            q, k, _ = pair(qkv.at[g], width, at)
            do_pair = do[g * rows : (g + 1) * rows, at : at + LANES]
            sums = [None] * 3
            split = zip(*(halves_of_lanes(x) for x in (q * HEAD**-0.5, k * HEAD**-0.5, do_pair)))
            for h, (q_one, k_one, do_one) in enumerate(split):
                ds = found[2 * g + h]
                parts = (dot(ds, k_one, TN), dot(ds, q_one, NN), dot(p_ref[g, 2 * j + h], do_one, NN))
                sums = [x if y is None else x + y for x, y in zip(parts, sums)]
            for part in range(3):
                dz_ref[g, :, part * width + at : part * width + at + LANES] = sums[part].astype(bf16)

    in_turn(width // LANES, slopes, products, 1)


def place_attn_weights(a_refs, w_qkv, w_proj):
    width = w_qkv.shape[0]
    half = width // 2
    for i, ref in enumerate(a_refs):
        for part in range(3):
            to = part * width + i * half
            w_qkv[:, to : to + half] = ref[:, part * half : (part + 1) * half]
        w_proj[:, i * half : (i + 1) * half] = ref[:, 3 * half : 4 * half]


def store_attn_grads(acc_qkv, acc_proj, outs):
    width = acc_qkv.shape[0]
    half = width // 2
    for i, ref in enumerate(outs):
        for part in range(3):
            at = part * width + i * half
            ref[:, part * half : (part + 1) * half] = acc_qkv[:, at : at + half].astype(bf16)
        ref[:, 3 * half : 4 * half] = acc_proj[:, i * half : (i + 1) * half].astype(bf16)


def store_mlp_grads(acc_up, acc_down, outs):
    half = acc_up.shape[1] // 2
    for i, ref in enumerate(outs):
        ref[:, :half] = acc_up[:, i * half : (i + 1) * half].astype(bf16)
        ref[:, half:] = acc_down[:, i * half : (i + 1) * half].astype(bf16)


def attn_forward(x, table, w_qkv, w_proj, qkv, p_all, o_all, mid, length):
    group, rows, width = x.shape
    gain, shift = table[0:1, :width], table[1:2, :width]
    xs = x[...].reshape(group * rows, width)
    u, _ = norm_parts(xs)
    h = (u * gain + shift).astype(bf16)
    z = dot(h, w_qkv[...], NN) + table[6:7, : 3 * width]
    qkv[...] = z.astype(bf16).reshape(qkv.shape)
    attention(qkv, p_all, o_all, width, length)
    o = o_all[...].reshape(group * rows, width)
    a = dot(o, w_proj[...], NT)
    mid[...] = (xs + a + table[2:3, :width]).reshape(mid.shape)


def mlp_forward(mid, table, m_refs, g_all, slope_all):
    group, rows, width = mid.shape
    ms = mid[...].reshape(group * rows, width)
    u, _ = norm_parts(ms)
    h = (u * table[3:4, :width] + table[4:5, :width]).astype(bf16)
    half = m_refs[0].shape[1] // 2
    pres = [dot(h, ref[:, :half], NN) for ref in m_refs]
    total = None
    for i, (ref, pre) in enumerate(zip(m_refs, pres)):
        cols = slice(i * half, (i + 1) * half)
        pre = pre + table[7:8, cols]
        phi = 0.5 * (1.0 + lax.erf(pre * inv_root_two))
        g = (pre * phi).astype(bf16)
        g_all[:, :, cols] = g.reshape(group, rows, half)
        slope = phi + pre * jnp.exp(-0.5 * pre * pre) * inv_root_two_pi
        slope_all[:, :, cols] = slope.astype(bf16).reshape(group, rows, half)
        t = dot(g, ref[:, half:], NT)
        total = t if total is None else total + t
    return ms + total + table[5:6, :width]


def mlp_backward(e, mid, table, sums, m_refs, g_all, slope_all, acc_up, acc_down):
    group, rows, width = mid.shape
    half = m_refs[0].shape[1] // 2
    sums[5:6, :width] += row_sum(e)
    e_low = e.astype(bf16)
    u, s = norm_parts(mid[...].reshape(group * rows, width))
    gain = table[3:4, :width]
    h = (u * gain + table[4:5, :width]).astype(bf16)
    dgs = [dot(e_low, ref[:, half:], NN) for ref in m_refs]
    dpres = []
    for i, dg in enumerate(dgs):
        slope = slope_all[:, :, i * half : (i + 1) * half].reshape(group * rows, half).astype(f32)
        dpres.append((dg * slope).astype(bf16))
    dh = dot(dpres[0], m_refs[0][:, :half], NT) + dot(dpres[1], m_refs[1][:, :half], NT)
    for i, dpre in enumerate(dpres):
        cols = slice(i * half, (i + 1) * half)
        acc_up[:, cols] += dot(h, dpre, TN)
        acc_down[:, cols] += dot(e_low, g_all[:, :, cols].reshape(group * rows, half), TN)
        sums[7:8, cols] += row_sum(dpre.astype(f32))
    sums[3:4, :width] += row_sum(dh * u)
    sums[4:5, :width] += row_sum(dh)
    return e + norm_back(dh, u, s, gain)


def attn_backward(dmid, x, table, sums, w_qkv, w_proj, qkv, p_all, o_all, dz, acc_qkv, acc_proj):
    group, rows, width = x.shape
    sums[2:3, :width] += row_sum(dmid)
    da = dmid.astype(bf16)
    do = dot(da, w_proj[...], NN).astype(bf16)
    acc_proj[...] += dot(da, o_all[...].reshape(group * rows, width), TN)
    u, s = norm_parts(x[...].reshape(group * rows, width))
    gain = table[0:1, :width]
    h = (u * gain + table[1:2, :width]).astype(bf16)
    attention_back(qkv, p_all, do, dz, width)
    dzs = dz[...].reshape(group * rows, 3 * width)
    dh = dot(dzs, w_qkv[...], NT)
    acc_qkv[...] += dot(h, dzs, TN)
    sums[6:7, : 3 * width] += row_sum(dzs.astype(f32))
    sums[0:1, :width] += row_sum(dh * u)
    sums[1:2, :width] += row_sum(dh)
    return dmid + norm_back(dh, u, s, gain)


def turn_rows(images, tokens):
    r = lax.broadcasted_iota(jnp.int32, (tokens * images, images * tokens), 0)
    c = lax.broadcasted_iota(jnp.int32, (tokens * images, images * tokens), 1)
    return jnp.where((r % images == c // tokens) & (r // images == c % tokens), 1.0, 0.0).astype(bf16)


def token_runs(length):
    return [(at, min(32, length - at)) for at in range(0, length, 32)]


def spread_images(ref, x_all):
    length, images, width = ref.shape
    x_all[...] = jnp.zeros_like(x_all)
    turn = turn_rows(images, 32)
    for at, count in token_runs(length):
        part = ref[at : at + count].astype(f32).reshape(count * images, width).astype(bf16)
        whole_turn = turn if count == 32 else turn_rows(images, 32)[: count * images]
        found = dot(whole_turn, part, TN)
        for i in range(images):
            x_all[i, at : at + count, :] = found[i * 32 : i * 32 + count].astype(x_all.dtype)


def join_images(all_images, out):
    length, images, width = out.shape
    turn = turn_rows(images, 32)
    for at, count in token_runs(length):
        rows = jnp.concatenate([all_images[i, at : at + 32, :] for i in range(images)], 0)
        found = dot(turn[: count * images], rows, NN).reshape(count, images, width)
        out[at : at + count] = found.astype(out.dtype)


def kernel_place(core, mine, other, full):
    images = mine.shape[1]
    for c in range(2):
        @pl.when(core[0] == c)
        def _():
            full[:, c * images : (c + 1) * images, :] = mine[...].astype(full.dtype)
            full[:, (1 - c) * images : (2 - c) * images, :] = other[...].astype(full.dtype)


def vec_of(ref):
    return ref.at[:, ref.shape[1] - LANES :]


def start_attn_forward(a_mine, a_other, table, w_qkv, w_proj, shards):
    place_attn_weights((a_mine, a_other), w_qkv, w_proj)
    expand_vec([vec_of(r) for r in (a_mine, a_other)], table, shards)


def kernel_spread(core, tok, cot, x_all, cot_all):
    spread_images(tok, x_all)
    spread_images(cot, cot_all)


def kernel_first_attn_forward(
    shards, length, x_low, a_mine, a_other, qkv, p_all, o_all, mid, table, w_qkv, w_proj, x
):
    @pl.when(pl.program_id(0) == 0)
    def _():
        start_attn_forward(a_mine, a_other, table, w_qkv, w_proj, shards)

    x[...] = x_low[...].astype(f32)
    attn_forward(x, table, w_qkv, w_proj, qkv, p_all, o_all, mid, length)


def kernel_attn_forward(shards, length, x, a_mine, a_other, qkv, p_all, o_all, mid, table, w_qkv, w_proj):
    @pl.when(pl.program_id(0) == 0)
    def _():
        start_attn_forward(a_mine, a_other, table, w_qkv, w_proj, shards)

    attn_forward(x, table, w_qkv, w_proj, qkv, p_all, o_all, mid, length)


def kernel_mlp_forward(mid, table, m_mine, m_other, stream, g_all, slope_all):
    out = mlp_forward(mid, table, (m_mine, m_other), g_all, slope_all)
    stream[...] = out.reshape(stream.shape)


def kernel_mlp_both(
    mid, cot, table, m_mine, m_other,
    out, dmid, sums, gm_mine, gm_other, g_all, slope_all, out_all, acc_up, acc_down,
):
    step = pl.program_id(0)

    @pl.when(step == 0)
    def _():
        for ref in (out_all, sums, acc_up, acc_down):
            ref[...] = jnp.zeros_like(ref)

    group, rows, width = mid.shape
    m_refs = (m_mine, m_other)
    result = mlp_forward(mid, table, m_refs, g_all, slope_all)
    for g in range(group):
        out_all[step * group + g, :rows, :] = result[g * rows : (g + 1) * rows].astype(bf16)
    e = cot[...].astype(f32).reshape(group * rows, width)
    back = mlp_backward(e, mid, table, sums, m_refs, g_all, slope_all, acc_up, acc_down)
    dmid[...] = back.reshape(dmid.shape)

    @pl.when(step == pl.num_programs(0) - 1)
    def _():
        store_mlp_grads(acc_up, acc_down, (gm_mine, gm_other))
        join_images(out_all, out)


def kernel_mlp_backward(
    e, mid, table, g_all, slope_all, m_mine, m_other,
    dmid, sums, gm_mine, gm_other, acc_up, acc_down,
):
    step = pl.program_id(0)

    @pl.when(step == 0)
    def _():
        for ref in (sums, acc_up, acc_down):
            ref[...] = jnp.zeros_like(ref)

    group, rows, width = mid.shape
    back = mlp_backward(
        e[...].reshape(group * rows, width), mid, table, sums, (m_mine, m_other),
        g_all, slope_all, acc_up, acc_down,
    )
    dmid[...] = back.reshape(dmid.shape)

    @pl.when(step == pl.num_programs(0) - 1)
    def _():
        store_mlp_grads(acc_up, acc_down, (gm_mine, gm_other))


def attn_backward_step(
    shards, dmid, x, table, sums_in, qkv, p_all, o_all, a_mine, a_other,
    ga_mine, ga_other, sums, vec_rows, w_qkv, w_proj, dz, acc_qkv, acc_proj, keep, finish,
):
    step = pl.program_id(0)

    @pl.when(step == 0)
    def _():
        place_attn_weights((a_mine, a_other), w_qkv, w_proj)
        sums[...] = sums_in[...]
        for ref in (acc_qkv, acc_proj):
            ref[...] = jnp.zeros_like(ref)

    group, rows, width = x.shape
    back = attn_backward(
        dmid[...].reshape(group * rows, width), x, table, sums, w_qkv, w_proj,
        qkv, p_all, o_all, dz, acc_qkv, acc_proj,
    )
    keep(back)

    @pl.when(step == pl.num_programs(0) - 1)
    def _():
        store_attn_grads(acc_qkv, acc_proj, (ga_mine, ga_other))
        pack_vec(sums, [vec_of(r) for r in (ga_mine, ga_other)], vec_rows, shards)
        finish()


def kernel_attn_backward(shards, dmid, x, table, sums_in, qkv, p_all, o_all, a_mine, a_other, e_out, *rest):
    def keep(back):
        e_out[...] = back.reshape(e_out.shape)

    attn_backward_step(
        shards, dmid, x, table, sums_in, qkv, p_all, o_all, a_mine, a_other, *rest, keep, lambda: None
    )


def kernel_first_attn_backward(
    shards, dmid, x_low, table, sums_in, qkv, p_all, o_all, a_mine, a_other, grad, *rest
):
    *rest, grad_all, x = rest
    step = pl.program_id(0)
    group, rows, _ = x.shape

    @pl.when(step == 0)
    def _():
        grad_all[...] = jnp.zeros_like(grad_all)

    def keep(back):
        for g in range(group):
            grad_all[step * group + g, :rows, :] = back[g * rows : (g + 1) * rows].astype(bf16)

    x[...] = x_low[...].astype(f32)
    attn_backward_step(
        shards, dmid, x, table, sums_in, qkv, p_all, o_all, a_mine, a_other, *rest, keep,
        lambda: join_images(grad_all, grad),
    )


def whole(shape):
    zeros = (0,) * len(shape)
    return pl.BlockSpec(shape, lambda i, *_: zeros, pipeline_mode=pl.Buffered(1))


def whole_out(shape):
    zeros = (0,) * len(shape)
    return pl.BlockSpec(shape, lambda i, *_: zeros)


def by_group(shape):
    rest = (0,) * (len(shape) - 1)
    return pl.BlockSpec((GROUP, *shape[1:]), lambda i, *_: (i, *rest))


def of_core(shape):
    return pl.BlockSpec(
        (shape[0], shape[1] // 2, shape[2]), lambda i, core: (0, core[0], 0), pipeline_mode=pl.Buffered(1)
    )


def call(kernel, steps, core, args, in_specs, outs, out_specs, scratch, flops, name, limit=32):
    moved = sum(a.size * a.dtype.itemsize for a in args)
    moved += sum(math.prod(o.shape) * o.dtype.itemsize for o in outs)
    return pl.pallas_call(
        kernel,
        out_shape=outs,
        grid_spec=pltpu.PrefetchScalarGridSpec(
            num_scalar_prefetch=0 if core is None else 1,
            grid=(steps,),
            in_specs=in_specs,
            out_specs=out_specs,
            scratch_shapes=[pltpu.VMEM(s, d) for s, d in scratch],
        ),
        compiler_params=pltpu.CompilerParams(vmem_limit_bytes=limit * 2**20),
        cost_estimate=pl.CostEstimate(flops=int(flops), bytes_accessed=int(moved), transcendentals=0),
        name=name,
    )(*(() if core is None else (core,)), *args)


def both_cores(core, mine, other, dtype, parts=4):
    length, images, width = mine.shape
    run = -(-length // parts)
    block = pl.BlockSpec((run, images, width), lambda i, core: (i, 0, 0))
    return pl.pallas_call(
        kernel_place,
        out_shape=arr((length, 2 * images, width), dtype),
        grid_spec=pltpu.PrefetchScalarGridSpec(
            num_scalar_prefetch=1,
            grid=(parts,),
            in_specs=[block, block],
            out_specs=pl.BlockSpec((run, 2 * images, width), lambda i, core: (i, 0, 0)),
        ),
        compiler_params=pltpu.CompilerParams(vmem_limit_bytes=16 * 2**20),
        name="both_cores",
    )(core, mine, other)


def in_vmem(kernel, args, outs, scratch, name):
    spec = pl.BlockSpec(memory_space=pltpu.VMEM)
    return pl.pallas_call(
        kernel,
        out_shape=outs,
        in_specs=[spec] * len(args),
        out_specs=[spec] * len(outs),
        scratch_shapes=[pltpu.VMEM(s, d) for s, d in scratch],
        compiler_params=pltpu.CompilerParams(vmem_limit_bytes=VMEM_LIMIT),
        name=name,
    )(*args)


def arr(shape, dtype):
    return jax.ShapeDtypeStruct(shape, dtype)


def in_hbm(shape, dtype):
    return pltpu.HBM(shape, dtype)


def kept(*arrays):
    return [pltpu.with_memory_space_constraint(x, pltpu.HBM) for x in arrays]


def after(x, *others):
    return lax.optimization_barrier((x, *others))[0]


def after_all(xs, *others):
    return list(lax.optimization_barrier((*xs, *others))[: len(xs)])


def bit_groups(shards):
    bits = [1 << k for k in range(shards.bit_length() - 1)]
    groups = [bits[k : k + 2] for k in range(0, len(bits), 2)]
    return groups[::-1]


def masks_of(group):
    masks = [0]
    for b in group:
        masks = masks + [m | b for m in masks]
    return masks


def exchange(x, mask, shards):
    return lax.ppermute(x, "shard", [(i, i ^ mask) for i in range(shards)])


def swap_cores(x):
    return lax.ppermute(x, "tensor", [(0, 1), (1, 0)])


def fetch(x, group, shards):
    return [x if m == 0 else exchange(x, m, shards) for m in masks_of(group)]


def in_order(got, group):
    me = lax.axis_index("shard")
    for k, b in enumerate(group):
        flag = (me & b) != 0
        got = [jnp.where(flag, got[i ^ (1 << k)], got[i]) for i in range(len(got))]
    return jnp.stack(got, 1).reshape(-1, *got[0].shape[1:])


def flat_rows(x):
    return x.reshape(-1, x.shape[-1])


def pieces_for(h, group):
    count = len(masks_of(group))
    h = h.reshape(-1, count, *h.shape[1:])
    here = (lax.axis_index("shard") // group[0]) % count
    return [lax.dynamic_index_in_dim(h, here ^ k, 1, keepdims=False) for k in range(count)]


def send_pieces(pieces, group, shards):
    return [p if m == 0 else exchange(p, m, shards) for p, m in zip(pieces, masks_of(group))]


def add_up(found):
    return functools.reduce(lambda a, b: a + b, [f.astype(f32) for f in found])


def core_sum(mine, other, shards):
    h = mine.astype(f32) + other.astype(f32)
    return h.astype(bf16).reshape(shards, mine.shape[0] // shards, -1)


def core_pieces(pairs, group, shards):
    cut = [
        [pieces_for(x.reshape(shards, x.shape[0] // shards, -1), group) for x in pair] for pair in pairs
    ]
    return [
        jnp.concatenate([add_up([mine[k], other[k]]).astype(bf16) for mine, other in cut], -1)
        for k in range(len(masks_of(group)))
    ]


def body(
    tokens, cotangent, ln1_gain, ln1_bias, w_qkv, b_qv, w_proj, b_proj,
    ln2_gain, ln2_bias, w_up, b_up, w_down, b_down, *, shards,
):
    images_all, length, width = tokens.shape
    layers, per = ln1_gain.shape
    images = images_all // 2
    steps = images // GROUP
    rows = -(-length // 16) * 16
    hidden = 2 * w_up.shape[2]
    heads = width // HEAD
    ca, cm = 2 * width + LANES, hidden
    t = lax.axis_index("tensor")
    core = t.astype(jnp.int32).reshape(1)
    groups = bit_groups(shards)

    def turned(which):
        one = [(0, 1)] * 6 + [(0, 2, 3, 1, 4), (0, 2, 1, 3), (0, 1, 3, 2), (0, 1, 2), (1, 0, 2), (0, 2, 1)]
        back = [tuple(sorted(range(len(p)), key=lambda i: p[i])) for p in one]
        return one if which == "in" else back

    raw = (ln1_gain, ln1_bias, b_proj, ln2_gain, ln2_bias, b_down, w_qkv, b_qv, w_proj, w_up, b_up, w_down)
    raw = [x.transpose(p) for x, p in zip(raw, turned("in"))]
    first_attn, first_mlp, later = in_vmem(
        kernel_pack, raw, [arr((per, c), bf16) for c in (ca, cm, ca + cm)],
        [((16, LANES), f32), ((per, LANES), f32)], "pack",
    )

    tok = images * length
    proj_flops = 2 * tok * width
    attn_flops = images * heads * 4 * length * length * HEAD
    aspec, mspec = whole((width, ca)), whole((width, cm))
    table_shape = (16, hidden)
    tspec = whole(table_shape)
    half_shape = (length, images, width)
    pad_shape = (images, rows, width)
    join_shape = (images, -(-length // 32) * 32, width)
    vec_shape = (16, LANES)
    qkv_shape = (images, rows, 3 * width)
    p_shape = (images, heads, rows, rows)
    g_shape = (images, rows, hidden)
    tokens_in, cotangent_in = kept(*(x.transpose(1, 0, 2) for x in (tokens, cotangent)))

    def g_of(shape):
        return (GROUP, *shape[1:])


    x_all, cot_all = call(
        kernel_spread, 1, core, (tokens_in, cotangent_in), [of_core(tokens_in.shape)] * 2,
        [in_hbm(pad_shape, bf16)] * 2, [whole_out(pad_shape)] * 2, [], 0, "spread", 16,
    )

    def early(x, stages):
        x = x[None]
        for group in stages:
            x = in_order(fetch(x, group, shards), group)
        return x

    last, before = groups[-1], groups[-2]
    got_z0 = fetch(early(first_attn, groups[:-2]), before, shards)
    z0 = in_order(after_all(got_z0, x_all, cot_all), before)
    got_m0 = fetch(early(after(first_mlp, z0), groups[:-2]), before, shards)
    got_a0 = fetch(z0, last, shards)
    l1 = early(after(later, z0), groups[:-2])
    near = [exchange(l1, before[0], shards)]
    a0 = flat_rows(in_order(got_a0, last))
    a0_other = swap_cores(a0)
    *got_m0, near[0] = after_all(got_m0 + near, a0)
    far = after(l1, a0)
    got_l1 = [l1] + near + [exchange(far, m, shards) for m in masks_of(before)[2:]]
    got_m0 = fetch(in_order(got_m0, before), last, shards)

    saved = [in_hbm(qkv_shape, bf16), in_hbm(p_shape, bf16), in_hbm(pad_shape, bf16),
             arr(pad_shape, f32), arr(table_shape, f32)]
    saved_specs = [by_group(qkv_shape), by_group(p_shape), by_group(pad_shape), by_group(pad_shape),
                   whole_out(table_shape)]
    attn_weights = [((width, 3 * width), bf16), ((width, width), bf16)]
    mlp_sums = [((width, hidden), f32), ((width, hidden), f32)]
    forward_flops = 4 * proj_flops * width + attn_flops
    qkv, p_all, o_all, mid, table = call(
        functools.partial(kernel_first_attn_forward, shards, length), steps, None,
        (*kept(x_all), a0, a0_other),
        [by_group(pad_shape), aspec, aspec], saved, saved_specs,
        attn_weights + [(g_of(pad_shape), f32)], forward_flops, "attn_forward_0",
    )
    got = after_all(got_m0 + got_l1, mid)
    m0, l1 = got[: len(got_m0)], got[len(got_m0) :]
    m0 = flat_rows(in_order(m0, last))
    m0_other = swap_cores(m0)
    l1 = in_order(l1, before)
    got_a1 = fetch(l1[:, :, :ca], last, shards)
    stream, g_all, slope_all = call(
        kernel_mlp_forward, steps, None,
        (mid, table, m0, m0_other),
        [by_group(pad_shape), tspec, mspec, mspec],
        [arr(pad_shape, f32), in_hbm(g_shape, bf16), in_hbm(g_shape, bf16)],
        [by_group(pad_shape), by_group(g_shape), by_group(g_shape)],
        [], 2 * proj_flops * hidden, "mlp_forward",
    )
    a1 = flat_rows(in_order(after_all(got_a1, stream), last))
    a1_other = swap_cores(a1)
    got_m1 = fetch(after(l1[:, :, ca:], a1), last, shards)
    qkv1, p1, o1, mid1, table1 = call(
        functools.partial(kernel_attn_forward, shards, length), steps, None,
        (stream, a1, a1_other),
        [by_group(pad_shape), aspec, aspec], saved, saved_specs,
        attn_weights, forward_flops, "attn_forward_1",
    )
    m1 = flat_rows(in_order(after_all(got_m1, mid1), last))
    m1_other = swap_cores(m1)
    out, dmid1, sums1, gm1_mine, gm1_other = call(
        kernel_mlp_both, steps, None,
        (mid1, *kept(cot_all), table1, m1, m1_other),
        [by_group(pad_shape), by_group(pad_shape), tspec, mspec, mspec],
        [arr(half_shape, bf16), arr(pad_shape, f32), arr(table_shape, f32)] + [arr((width, cm), bf16)] * 2,
        [whole_out(half_shape), by_group(pad_shape), whole_out(table_shape)] + [whole_out((width, cm))] * 2,
        [(g_of(g_shape), bf16), (g_of(g_shape), bf16), (join_shape, bf16)] + mlp_sums,
        6 * proj_flops * hidden, "mlp_both", 40,
    )
    back_specs = [by_group(pad_shape), by_group(pad_shape), tspec, tspec, by_group(qkv_shape),
                  by_group(p_shape), by_group(pad_shape), aspec, aspec]
    back_scratch = [
        (table_shape, f32), (vec_shape, f32), *attn_weights, (g_of(qkv_shape), bf16),
        ((width, 3 * width), f32), ((width, width), f32),
    ]
    ga_outs, ga_specs = [arr((width, ca), bf16)] * 2, [whole_out((width, ca))] * 2
    back_flops = 8 * proj_flops * width + 2.5 * attn_flops
    hm1 = swap_cores(gm1_other)
    e, ga1_mine, ga1_other = call(
        functools.partial(kernel_attn_backward, shards), steps, None,
        (dmid1, stream, table1, sums1, *kept(qkv1, p1, o1), a1, a1_other),
        back_specs, [arr(pad_shape, f32)] + ga_outs, [by_group(pad_shape)] + ga_specs,
        back_scratch, back_flops, "attn_backward_1",
    )
    hm1, ga1_mine, ga1_other = after_all((hm1, ga1_mine, ga1_other), e)
    h1 = core_sum(
        jnp.concatenate([ga1_mine, gm1_mine], 1), jnp.concatenate([swap_cores(ga1_other), hm1], 1), shards
    )
    h1 = pieces_for(h1, last)
    out_other = swap_cores(out)
    e = after(e, out_other, *h1)
    dmid, sums, gm_mine, gm_other = call(
        kernel_mlp_backward, steps, None,
        (e, mid, table, *kept(g_all, slope_all), m0, m0_other),
        [by_group(pad_shape), by_group(pad_shape), tspec, by_group(g_shape), by_group(g_shape), mspec, mspec],
        [arr(pad_shape, f32), arr(table_shape, f32)] + [arr((width, cm), bf16)] * 2,
        [by_group(pad_shape), whole_out(table_shape)] + [whole_out((width, cm))] * 2,
        mlp_sums, 4 * proj_flops * hidden, "mlp_backward",
    )
    middle = groups[:-1][::-1]
    h1 = add_up(after_all(send_pieces(h1, last, shards), dmid)).astype(bf16)
    h1 = pieces_for(h1, middle[0])
    h0m = core_pieces([(gm_mine, swap_cores(gm_other))], last, shards)
    dmid = after(dmid, *h0m, *h1)
    grad, ga_mine, ga_other = call(
        functools.partial(kernel_first_attn_backward, shards), steps, None,
        (dmid, *kept(x_all), table, sums, *kept(qkv, p_all, o_all), a0, a0_other),
        back_specs, [arr(half_shape, bf16)] + ga_outs, [whole_out(half_shape)] + ga_specs,
        back_scratch + [(join_shape, bf16), (g_of(pad_shape), f32)], back_flops, "attn_backward_0",
    )
    h0m = send_pieces(h0m, last, shards)
    h1 = send_pieces(h1, middle[0], shards)
    n = len(h0m)
    got = after_all(h0m + h1 + [ga_mine, ga_other, grad], grad)
    h0m, h1, (ga_mine, ga_other, grad) = got[:n], got[n:-3], got[-3:]
    h0a = core_pieces([(ga_mine, swap_cores(ga_other))], last, shards)
    grad_other = swap_cores(after(grad, *h0a))
    h0m = after_all(pieces_for(add_up(h0m).astype(bf16), middle[0]), grad_other, *h0a)
    h0a = send_pieces(h0a, last, shards)
    h0m = send_pieces(h0m, middle[0], shards)
    out_full = both_cores(core, out, out_other, bf16)
    got = after_all(h0a + h0m, out_full)
    h0a, h0m = got[: len(h0a)], got[len(h0a) :]
    h0a = send_pieces(pieces_for(add_up(h0a).astype(bf16), middle[0]), middle[0], shards)
    for group in middle[1:]:
        h0a, h0m, h1 = (
            send_pieces(pieces_for(add_up(h).astype(bf16), group), group, shards) for h in (h0a, h0m, h1)
        )

    grad_full = both_cores(core, grad, grad_other, f32)
    h0a = after_all(h0a, grad_full)
    grads = in_vmem(
        functools.partial(kernel_unpack, len(h1)),
        [x.reshape(per, -1) for h in (h0a, h0m, h1) for x in h],
        [arr(x.shape, f32) for x in raw], [], "unpack",
    )
    grads = [g.transpose(p) for g, p in zip(grads, turned("out"))]
    g1, b1, bp, g2, b2, bd, gq, gb, gp, gu, gbu, gd = grads
    return (
        out_full.transpose(1, 0, 2), grad_full.transpose(1, 0, 2),
        g1, b1, gq, gb, gp, bp, g2, b2, gu, gbu, gd, bd,
    )


def solution(mesh):
    args = (
        P("shard", None, None),
        P("shard", None, None),
        P(None, "shard"),
        P(None, "shard"),
        P(None, "shard", None, "tensor", None),
        P(None, None, "tensor", "shard"),
        P(None, "tensor", None, "shard"),
        P(None, "shard"),
        P(None, "shard"),
        P(None, "shard"),
        P(None, "shard", "tensor"),
        P(None, "tensor", "shard"),
        P(None, "tensor", "shard"),
        P(None, "shard"),
    )
    return jax.shard_map(
        functools.partial(body, shards=mesh.shape["shard"]),
        mesh=mesh,
        in_specs=args,
        out_specs=args,
        check_vma=False,
    )
```

```python
import functools
import math

import jax
import jax.numpy as jnp
from jax import lax
from jax.experimental import pallas as pl
from jax.experimental.pallas import tpu as pltpu
from jax.sharding import PartitionSpec as P

bf16, f32 = jnp.bfloat16, jnp.float32
epsilon = 1e-06
inv_root_two = 0.7071067811865476
inv_root_two_pi = 0.3989422804014327
log2_e = 1.4426950408889634
NN, NT, TN = ((1,), (0,)), ((1,), (1,)), ((0,), (0,))
VMEM_LIMIT = 60 * 2**20
GROUP = 2
HEAD = 64
LANES = 128


def dot(a, b, dims):
    return lax.dot_general(a, b, (dims, ((), ())), preferred_element_type=f32)


QV_AT, UP_AT = 16, 24


def owner_rows(width, shards, place):
    n = lax.broadcasted_iota(jnp.int32, (width, LANES), 0)
    m = lax.broadcasted_iota(jnp.int32, (width, LANES), 1)
    per = width // shards
    return n // per == (m % place) // (place // shards)


def lane_picks(at, unit):
    r = lax.broadcasted_iota(jnp.int32, (LANES, LANES), 0)
    m = lax.broadcasted_iota(jnp.int32, (LANES, LANES), 1)
    return jnp.where(r == at + m % unit, 1.0, 0.0).astype(bf16)


def rank_rows(width, shards):
    r = lax.broadcasted_iota(jnp.int32, (16, width), 0)
    n = lax.broadcasted_iota(jnp.int32, (16, width), 1)
    return jnp.where(n % (width // shards) == r, 1.0, 0.0).astype(bf16)


def unit_rows(rows, columns):
    r = lax.broadcasted_iota(jnp.int32, (rows, columns), 0)
    c = lax.broadcasted_iota(jnp.int32, (rows, columns), 1)
    return jnp.where(r == c, 1.0, 0.0).astype(bf16)


def qv_spots(width, half):
    heads = width // HEAD // 2
    for part in range(2):
        for h in range(heads):
            yield part * heads + h, part * 2 * width + half * (width // 2) + h * HEAD


def up_spots(hidden, half):
    rows = hidden // 2 // LANES
    return [(r, (half * rows + r) * LANES) for r in range(rows)]


def expand_vec(vec_refs, table, shards):
    width, hidden = vec_refs[0].shape[0], table.shape[1]
    table[...] = jnp.zeros_like(table)
    ranks = rank_rows(width, shards)
    for half, ref in enumerate(vec_refs):
        block = ref[...]
        if half == 0:
            table[0:6, 0:width] = dot(unit_rows(16, LANES), block, NT)[0:6]
        for at, place, row, spots in (
            (QV_AT, HEAD, 6, qv_spots(width, half)),
            (UP_AT, LANES, 7, up_spots(hidden, half)),
        ):
            found = dot(block, lane_picks(at, place // shards), NN)
            found = jnp.where(owner_rows(width, shards, place), found, 0.0).astype(bf16)
            found = dot(ranks, found, NN)
            for r, first in spots:
                table[row : row + 1, first : first + place] = found[r : r + 1, :place]


def pack_vec(table, outs, rows, shards):
    width, hidden = outs[0].shape[0], table.shape[1]
    index = lax.broadcasted_iota(jnp.int32, (16, width), 0)
    six = jnp.where(index < 6, table[0:16, :width], 0.0).astype(bf16)
    six = dot(six, unit_rows(16, LANES), TN)
    ranks = rank_rows(width, shards)
    for half, ref in enumerate(outs):
        block = six
        for at, place, row, spots in (
            (QV_AT, HEAD, 6, qv_spots(width, half)),
            (UP_AT, LANES, 7, up_spots(hidden, half)),
        ):
            rows[...] = jnp.zeros_like(rows)
            for r, first in spots:
                rows[r : r + 1, :place] = table[row : row + 1, first : first + place]
            found = dot(ranks, rows[...].astype(bf16), TN)
            lane = lax.broadcasted_iota(jnp.int32, (width, LANES), 1)
            found = jnp.where(owner_rows(width, shards, place) & (lane < place), found, 0.0).astype(bf16)
            block = block + dot(found, lane_picks(at, place // shards), NT)
        ref[...] = block.astype(bf16)


def kernel_pack(
    ln1_gain, ln1_bias, b_proj, ln2_gain, ln2_bias, b_down, w_qkv, b_qv, w_proj, w_up, b_up, w_down,
    first_attn, first_mlp, later, rows, vec,
):
    layers, parts, heads, per, _ = w_qkv.shape
    half = heads * HEAD
    ca, cm = first_attn.shape[1], first_mlp.shape[1]
    for l in range(layers):
        attn, mlp = (first_attn, first_mlp) if l == 0 else (later.at[:, :ca], later.at[:, ca:])
        for h in range(heads):
            for part in range(parts):
                at = part * half + h * HEAD
                attn[:, at : at + HEAD] = w_qkv[l, part, h]
            at = parts * half + h * HEAD
            attn[:, at : at + HEAD] = w_proj[l, h]
        rows[...] = jnp.zeros_like(rows)
        for j, ref in enumerate((ln1_gain, ln1_bias, b_proj, ln2_gain, ln2_bias, b_down)):
            rows[j : j + 1, :per] = ref[l : l + 1, :].astype(f32)
        vec[...] = jnp.zeros_like(vec)
        vec[:, 0:16] = dot(unit_rows(per, LANES), rows[...].astype(bf16), NT)
        unit = b_qv.shape[3]
        for h in range(heads):
            for part in range(2):
                r = part * heads + h
                vec[r : r + 1, QV_AT : QV_AT + unit] = b_qv[l, h, part : part + 1, :].astype(f32)
        unit = b_up.shape[2]
        for r in range(b_up.shape[0]):
            vec[r : r + 1, UP_AT : UP_AT + unit] = b_up[r, l : l + 1, :].astype(f32)
        attn[:, ca - LANES :] = vec[...].astype(bf16)
        mlp[:, : cm // 2] = w_up[l]
        mlp[:, cm // 2 :] = w_down[l]


def kernel_unpack(count, *refs):
    pieces, outs = refs[: 3 * count], refs[3 * count :]
    sixes, (w_qkv, b_qv, w_proj, w_up, b_up, w_down) = outs[:6], outs[6:]
    layers, parts, heads, per, _ = w_qkv.shape
    half = heads * HEAD
    hidden = w_up.shape[2]

    def total(group, cols):
        found = [ref[:, cols].astype(f32) for ref in pieces[group * count : (group + 1) * count]]
        return functools.reduce(lambda a, b: a + b, found)

    ca = parts * half + half + LANES
    for l in range(layers):
        attn, mlp, base = (0, 1, 0) if l == 0 else (2, 2, ca)
        whole_attn = total(attn, slice(0, ca))
        for h in range(heads):
            for part in range(parts):
                at = part * half + h * HEAD
                w_qkv[l, part, h] = whole_attn[:, at : at + HEAD]
            at = parts * half + h * HEAD
            w_proj[l, h] = whole_attn[:, at : at + HEAD]
        vec = whole_attn[:, ca - LANES :]
        columns = vec.T
        for j, ref in enumerate(sixes):
            ref[l : l + 1, :] = columns[j : j + 1, :per]
        unit = b_qv.shape[3]
        for h in range(heads):
            for part in range(2):
                r = part * heads + h
                b_qv[l, h, part : part + 1, :] = vec[r : r + 1, QV_AT : QV_AT + unit]
        unit = b_up.shape[2]
        for r in range(b_up.shape[0]):
            b_up[r, l : l + 1, :] = vec[r : r + 1, UP_AT : UP_AT + unit]
        w_up[l] = total(mlp, slice(base, base + hidden))
        w_down[l] = total(mlp, slice(base + hidden, base + 2 * hidden))


def norm_parts(x):
    c = x - jnp.mean(x, -1, keepdims=True)
    s = lax.rsqrt(jnp.mean(c * c, -1, keepdims=True) + epsilon)
    return c * s, s


def norm_back(dh, u, s, gain):
    t = dh * gain
    return s * (t - jnp.mean(t, -1, keepdims=True) - u * jnp.mean(t * u, -1, keepdims=True))


def row_sum(x):
    return jnp.sum(x, 0, keepdims=True)


def halves_of_lanes(x):
    low = lax.broadcasted_iota(jnp.int32, x.shape, 1) < HEAD
    zero = jnp.zeros_like(x)
    return jnp.where(low, x, zero), jnp.where(low, zero, x)


def probs_t(scores, length):
    row = lax.broadcasted_iota(jnp.int32, scores.shape, 0)
    scores = jnp.where(row < length, scores, -1e30)
    high = jnp.max(scores, 0, keepdims=True)
    e = jnp.exp2((scores - high) * (HEAD**-0.5 * log2_e))
    return (e * (1.0 / jnp.sum(e, 0, keepdims=True))).astype(bf16)


def pair(qkv, width, at):
    return [qkv[:, part * width + at : part * width + at + LANES] for part in range(3)]


def attention(qkv, p_ref, o_ref, width, length):
    images, pairs = qkv.shape[0], width // LANES

    def probs(j):
        found = []
        for g in range(images):
            q, k, _ = pair(qkv.at[g], width, LANES * j)
            found.append([probs_t(dot(k, q_one, NT), length) for q_one in halves_of_lanes(q)])
        return found

    def mix(j, found):
        at = LANES * j
        for g in range(images):
            v = pair(qkv.at[g], width, at)[2]
            parts = [dot(p, v_one, TN) for p, v_one in zip(found[g], halves_of_lanes(v))]
            o_ref[g, :, at : at + LANES] = (parts[0] + parts[1]).astype(bf16)
            for h, p in enumerate(found[g]):
                p_ref[g, 2 * j + h] = p

    in_turn(pairs, probs, mix, 1)


def in_turn(count, first, second, ahead):
    waiting = []
    for j in range(count):
        waiting.append((j, first(j)))
        if len(waiting) > ahead:
            second(*waiting.pop(0))
    for item in waiting:
        second(*item)


def attention_back(qkv, p_ref, do, dz_ref, width):
    images, rows, _ = qkv.shape

    def slopes(j):
        at = LANES * j
        found = []
        for g in range(images):
            v = pair(qkv.at[g], width, at)[2]
            do_pair = do[g * rows : (g + 1) * rows, at : at + LANES]
            for h, v_one in enumerate(halves_of_lanes(v)):
                pf = p_ref[g, 2 * j + h].astype(f32)
                t = pf * dot(v_one, do_pair, NT)
                found.append((t - pf * row_sum(t)).astype(bf16))
        return found

    def products(j, found):
        at = LANES * j
        for g in range(images):
            q, k, _ = pair(qkv.at[g], width, at)
            do_pair = do[g * rows : (g + 1) * rows, at : at + LANES]
            sums = [None] * 3
            split = zip(*(halves_of_lanes(x) for x in (q * HEAD**-0.5, k * HEAD**-0.5, do_pair)))
            for h, (q_one, k_one, do_one) in enumerate(split):
                ds = found[2 * g + h]
                parts = (dot(ds, k_one, TN), dot(ds, q_one, NN), dot(p_ref[g, 2 * j + h], do_one, NN))
                sums = [x if y is None else x + y for x, y in zip(parts, sums)]
            for part in range(3):
                dz_ref[g, :, part * width + at : part * width + at + LANES] = sums[part].astype(bf16)

    in_turn(width // LANES, slopes, products, 1)


def place_attn_weights(a_refs, w_qkv, w_proj):
    width = w_qkv.shape[0]
    half = width // 2
    for i, ref in enumerate(a_refs):
        for part in range(3):
            to = part * width + i * half
            w_qkv[:, to : to + half] = ref[:, part * half : (part + 1) * half]
        w_proj[:, i * half : (i + 1) * half] = ref[:, 3 * half : 4 * half]


def store_attn_grads(acc_qkv, acc_proj, outs):
    width = acc_qkv.shape[0]
    half = width // 2
    for i, ref in enumerate(outs):
        for part in range(3):
            at = part * width + i * half
            ref[:, part * half : (part + 1) * half] = acc_qkv[:, at : at + half].astype(bf16)
        ref[:, 3 * half : 4 * half] = acc_proj[:, i * half : (i + 1) * half].astype(bf16)


def store_mlp_grads(acc_up, acc_down, outs):
    half = acc_up.shape[1] // 2
    for i, ref in enumerate(outs):
        ref[:, :half] = acc_up[:, i * half : (i + 1) * half].astype(bf16)
        ref[:, half:] = acc_down[:, i * half : (i + 1) * half].astype(bf16)


def attn_forward(x, table, w_qkv, w_proj, qkv, p_all, o_all, mid, length):
    group, rows, width = x.shape
    gain, shift = table[0:1, :width], table[1:2, :width]
    xs = x[...].reshape(group * rows, width)
    u, _ = norm_parts(xs)
    h = (u * gain + shift).astype(bf16)
    z = dot(h, w_qkv[...], NN) + table[6:7, : 3 * width]
    qkv[...] = z.astype(bf16).reshape(qkv.shape)
    attention(qkv, p_all, o_all, width, length)
    o = o_all[...].reshape(group * rows, width)
    a = dot(o, w_proj[...], NT)
    mid[...] = (xs + a + table[2:3, :width]).reshape(mid.shape)


def mlp_forward(mid, table, m_refs, g_all, slope_all):
    group, rows, width = mid.shape
    ms = mid[...].reshape(group * rows, width)
    u, _ = norm_parts(ms)
    h = (u * table[3:4, :width] + table[4:5, :width]).astype(bf16)
    half = m_refs[0].shape[1] // 2
    pres = [dot(h, ref[:, :half], NN) for ref in m_refs]
    total = None
    for i, (ref, pre) in enumerate(zip(m_refs, pres)):
        cols = slice(i * half, (i + 1) * half)
        pre = pre + table[7:8, cols]
        phi = 0.5 * (1.0 + lax.erf(pre * inv_root_two))
        g = (pre * phi).astype(bf16)
        g_all[:, :, cols] = g.reshape(group, rows, half)
        slope = phi + pre * jnp.exp(-0.5 * pre * pre) * inv_root_two_pi
        slope_all[:, :, cols] = slope.astype(bf16).reshape(group, rows, half)
        t = dot(g, ref[:, half:], NT)
        total = t if total is None else total + t
    return ms + total + table[5:6, :width]


def mlp_backward(e, mid, table, sums, m_refs, g_all, slope_all, acc_up, acc_down):
    group, rows, width = mid.shape
    half = m_refs[0].shape[1] // 2
    sums[5:6, :width] += row_sum(e)
    e_low = e.astype(bf16)
    u, s = norm_parts(mid[...].reshape(group * rows, width))
    gain = table[3:4, :width]
    h = (u * gain + table[4:5, :width]).astype(bf16)
    dgs = [dot(e_low, ref[:, half:], NN) for ref in m_refs]
    dpres = []
    for i, dg in enumerate(dgs):
        slope = slope_all[:, :, i * half : (i + 1) * half].reshape(group * rows, half).astype(f32)
        dpres.append((dg * slope).astype(bf16))
    dh = dot(dpres[0], m_refs[0][:, :half], NT) + dot(dpres[1], m_refs[1][:, :half], NT)
    for i, dpre in enumerate(dpres):
        cols = slice(i * half, (i + 1) * half)
        acc_up[:, cols] += dot(h, dpre, TN)
        acc_down[:, cols] += dot(e_low, g_all[:, :, cols].reshape(group * rows, half), TN)
        sums[7:8, cols] += row_sum(dpre.astype(f32))
    sums[3:4, :width] += row_sum(dh * u)
    sums[4:5, :width] += row_sum(dh)
    return e + norm_back(dh, u, s, gain)


def attn_backward(dmid, x, table, sums, w_qkv, w_proj, qkv, p_all, o_all, dz, acc_qkv, acc_proj):
    group, rows, width = x.shape
    sums[2:3, :width] += row_sum(dmid)
    da = dmid.astype(bf16)
    do = dot(da, w_proj[...], NN).astype(bf16)
    acc_proj[...] += dot(da, o_all[...].reshape(group * rows, width), TN)
    u, s = norm_parts(x[...].reshape(group * rows, width))
    gain = table[0:1, :width]
    h = (u * gain + table[1:2, :width]).astype(bf16)
    attention_back(qkv, p_all, do, dz, width)
    dzs = dz[...].reshape(group * rows, 3 * width)
    dh = dot(dzs, w_qkv[...], NT)
    acc_qkv[...] += dot(h, dzs, TN)
    sums[6:7, : 3 * width] += row_sum(dzs.astype(f32))
    sums[0:1, :width] += row_sum(dh * u)
    sums[1:2, :width] += row_sum(dh)
    return dmid + norm_back(dh, u, s, gain)


def turn_rows(images, tokens):
    r = lax.broadcasted_iota(jnp.int32, (tokens * images, images * tokens), 0)
    c = lax.broadcasted_iota(jnp.int32, (tokens * images, images * tokens), 1)
    return jnp.where((r % images == c // tokens) & (r // images == c % tokens), 1.0, 0.0).astype(bf16)


def token_runs(length):
    return [(at, min(32, length - at)) for at in range(0, length, 32)]


def spread_images(ref, x_all):
    length, images, width = ref.shape
    x_all[...] = jnp.zeros_like(x_all)
    turn = turn_rows(images, 32)
    for at, count in token_runs(length):
        part = ref[at : at + count].astype(f32).reshape(count * images, width).astype(bf16)
        whole_turn = turn if count == 32 else turn_rows(images, 32)[: count * images]
        found = dot(whole_turn, part, TN)
        for i in range(images):
            x_all[i, at : at + count, :] = found[i * 32 : i * 32 + count].astype(x_all.dtype)


def join_images(all_images, out):
    length, images, width = out.shape
    turn = turn_rows(images, 32)
    for at, count in token_runs(length):
        rows = jnp.concatenate([all_images[i, at : at + 32, :] for i in range(images)], 0)
        found = dot(turn[: count * images], rows, NN).reshape(count, images, width)
        out[at : at + count] = found.astype(out.dtype)


def kernel_place(core, mine, other, full):
    images = mine.shape[1]
    for c in range(2):
        @pl.when(core[0] == c)
        def _():
            full[:, c * images : (c + 1) * images, :] = mine[...].astype(full.dtype)
            full[:, (1 - c) * images : (2 - c) * images, :] = other[...].astype(full.dtype)


def vec_of(ref):
    return ref.at[:, ref.shape[1] - LANES :]


def start_attn_forward(a_mine, a_other, table, w_qkv, w_proj, shards):
    place_attn_weights((a_mine, a_other), w_qkv, w_proj)
    expand_vec([vec_of(r) for r in (a_mine, a_other)], table, shards)


def kernel_spread(core, tok, cot, x_all, cot_all):
    spread_images(tok, x_all)
    spread_images(cot, cot_all)


def kernel_first_attn_forward(
    shards, length, x_low, a_mine, a_other, qkv, p_all, o_all, mid, table, w_qkv, w_proj, x
):
    @pl.when(pl.program_id(0) == 0)
    def _():
        start_attn_forward(a_mine, a_other, table, w_qkv, w_proj, shards)

    x[...] = x_low[...].astype(f32)
    attn_forward(x, table, w_qkv, w_proj, qkv, p_all, o_all, mid, length)


def kernel_attn_forward(shards, length, x, a_mine, a_other, qkv, p_all, o_all, mid, table, w_qkv, w_proj):
    @pl.when(pl.program_id(0) == 0)
    def _():
        start_attn_forward(a_mine, a_other, table, w_qkv, w_proj, shards)

    attn_forward(x, table, w_qkv, w_proj, qkv, p_all, o_all, mid, length)


def kernel_mlp_forward(mid, table, m_mine, m_other, stream, g_all, slope_all):
    out = mlp_forward(mid, table, (m_mine, m_other), g_all, slope_all)
    stream[...] = out.reshape(stream.shape)


def kernel_mlp_both(
    mid, cot, table, m_mine, m_other,
    out, dmid, sums, gm_mine, gm_other, g_all, slope_all, out_all, acc_up, acc_down,
):
    step = pl.program_id(0)

    @pl.when(step == 0)
    def _():
        for ref in (out_all, sums, acc_up, acc_down):
            ref[...] = jnp.zeros_like(ref)

    group, rows, width = mid.shape
    m_refs = (m_mine, m_other)
    result = mlp_forward(mid, table, m_refs, g_all, slope_all)
    for g in range(group):
        out_all[step * group + g, :rows, :] = result[g * rows : (g + 1) * rows].astype(bf16)
    e = cot[...].astype(f32).reshape(group * rows, width)
    back = mlp_backward(e, mid, table, sums, m_refs, g_all, slope_all, acc_up, acc_down)
    dmid[...] = back.reshape(dmid.shape)

    @pl.when(step == pl.num_programs(0) - 1)
    def _():
        store_mlp_grads(acc_up, acc_down, (gm_mine, gm_other))
        join_images(out_all, out)


def kernel_mlp_backward(
    e, mid, table, g_all, slope_all, m_mine, m_other,
    dmid, sums, gm_mine, gm_other, acc_up, acc_down,
):
    step = pl.program_id(0)

    @pl.when(step == 0)
    def _():
        for ref in (sums, acc_up, acc_down):
            ref[...] = jnp.zeros_like(ref)

    group, rows, width = mid.shape
    back = mlp_backward(
        e[...].reshape(group * rows, width), mid, table, sums, (m_mine, m_other),
        g_all, slope_all, acc_up, acc_down,
    )
    dmid[...] = back.reshape(dmid.shape)

    @pl.when(step == pl.num_programs(0) - 1)
    def _():
        store_mlp_grads(acc_up, acc_down, (gm_mine, gm_other))


def attn_backward_step(
    shards, dmid, x, table, sums_in, qkv, p_all, o_all, a_mine, a_other,
    ga_mine, ga_other, sums, vec_rows, w_qkv, w_proj, dz, acc_qkv, acc_proj, keep, finish,
):
    step = pl.program_id(0)

    @pl.when(step == 0)
    def _():
        place_attn_weights((a_mine, a_other), w_qkv, w_proj)
        sums[...] = sums_in[...]
        for ref in (acc_qkv, acc_proj):
            ref[...] = jnp.zeros_like(ref)

    group, rows, width = x.shape
    back = attn_backward(
        dmid[...].reshape(group * rows, width), x, table, sums, w_qkv, w_proj,
        qkv, p_all, o_all, dz, acc_qkv, acc_proj,
    )
    keep(back)

    @pl.when(step == pl.num_programs(0) - 1)
    def _():
        store_attn_grads(acc_qkv, acc_proj, (ga_mine, ga_other))
        pack_vec(sums, [vec_of(r) for r in (ga_mine, ga_other)], vec_rows, shards)
        finish()


def kernel_attn_backward(shards, dmid, x, table, sums_in, qkv, p_all, o_all, a_mine, a_other, e_out, *rest):
    def keep(back):
        e_out[...] = back.reshape(e_out.shape)

    attn_backward_step(
        shards, dmid, x, table, sums_in, qkv, p_all, o_all, a_mine, a_other, *rest, keep, lambda: None
    )


def kernel_first_attn_backward(
    shards, dmid, x_low, table, sums_in, qkv, p_all, o_all, a_mine, a_other, grad, *rest
):
    *rest, grad_all, x = rest
    step = pl.program_id(0)
    group, rows, _ = x.shape

    @pl.when(step == 0)
    def _():
        grad_all[...] = jnp.zeros_like(grad_all)

    def keep(back):
        for g in range(group):
            grad_all[step * group + g, :rows, :] = back[g * rows : (g + 1) * rows].astype(bf16)

    x[...] = x_low[...].astype(f32)
    attn_backward_step(
        shards, dmid, x, table, sums_in, qkv, p_all, o_all, a_mine, a_other, *rest, keep,
        lambda: join_images(grad_all, grad),
    )


def whole(shape):
    zeros = (0,) * len(shape)
    return pl.BlockSpec(shape, lambda i, *_: zeros, pipeline_mode=pl.Buffered(1))


def whole_out(shape):
    zeros = (0,) * len(shape)
    return pl.BlockSpec(shape, lambda i, *_: zeros)


def by_group(shape):
    rest = (0,) * (len(shape) - 1)
    return pl.BlockSpec((GROUP, *shape[1:]), lambda i, *_: (i, *rest))


def of_core(shape):
    return pl.BlockSpec(
        (shape[0], shape[1] // 2, shape[2]), lambda i, core: (0, core[0], 0), pipeline_mode=pl.Buffered(1)
    )


def call(kernel, steps, core, args, in_specs, outs, out_specs, scratch, flops, name, limit=32):
    moved = sum(a.size * a.dtype.itemsize for a in args)
    moved += sum(math.prod(o.shape) * o.dtype.itemsize for o in outs)
    return pl.pallas_call(
        kernel,
        out_shape=outs,
        grid_spec=pltpu.PrefetchScalarGridSpec(
            num_scalar_prefetch=0 if core is None else 1,
            grid=(steps,),
            in_specs=in_specs,
            out_specs=out_specs,
            scratch_shapes=[pltpu.VMEM(s, d) for s, d in scratch],
        ),
        compiler_params=pltpu.CompilerParams(vmem_limit_bytes=limit * 2**20),
        cost_estimate=pl.CostEstimate(flops=int(flops), bytes_accessed=int(moved), transcendentals=0),
        name=name,
    )(*(() if core is None else (core,)), *args)


def both_cores(core, mine, other, dtype, parts=4):
    length, images, width = mine.shape
    run = -(-length // parts)
    block = pl.BlockSpec((run, images, width), lambda i, core: (i, 0, 0))
    return pl.pallas_call(
        kernel_place,
        out_shape=arr((length, 2 * images, width), dtype),
        grid_spec=pltpu.PrefetchScalarGridSpec(
            num_scalar_prefetch=1,
            grid=(parts,),
            in_specs=[block, block],
            out_specs=pl.BlockSpec((run, 2 * images, width), lambda i, core: (i, 0, 0)),
        ),
        compiler_params=pltpu.CompilerParams(vmem_limit_bytes=16 * 2**20),
        name="both_cores",
    )(core, mine, other)


def in_vmem(kernel, args, outs, scratch, name):
    spec = pl.BlockSpec(memory_space=pltpu.VMEM)
    return pl.pallas_call(
        kernel,
        out_shape=outs,
        in_specs=[spec] * len(args),
        out_specs=[spec] * len(outs),
        scratch_shapes=[pltpu.VMEM(s, d) for s, d in scratch],
        compiler_params=pltpu.CompilerParams(vmem_limit_bytes=VMEM_LIMIT),
        name=name,
    )(*args)


def arr(shape, dtype):
    return jax.ShapeDtypeStruct(shape, dtype)


def in_hbm(shape, dtype):
    return pltpu.HBM(shape, dtype)


def kept(*arrays):
    return [pltpu.with_memory_space_constraint(x, pltpu.HBM) for x in arrays]


def after(x, *others):
    return lax.optimization_barrier((x, *others))[0]


def after_all(xs, *others):
    return list(lax.optimization_barrier((*xs, *others))[: len(xs)])


def bit_groups(shards):
    bits = [1 << k for k in range(shards.bit_length() - 1)]
    groups = [bits[k : k + 2] for k in range(0, len(bits), 2)]
    return groups[::-1]


def masks_of(group):
    masks = [0]
    for b in group:
        masks = masks + [m | b for m in masks]
    return masks


def exchange(x, mask, shards):
    return lax.ppermute(x, "shard", [(i, i ^ mask) for i in range(shards)])


def swap_cores(x):
    return lax.ppermute(x, "tensor", [(0, 1), (1, 0)])


def fetch(x, group, shards):
    return [x if m == 0 else exchange(x, m, shards) for m in masks_of(group)]


def in_order(got, group):
    me = lax.axis_index("shard")
    for k, b in enumerate(group):
        flag = (me & b) != 0
        got = [jnp.where(flag, got[i ^ (1 << k)], got[i]) for i in range(len(got))]
    return jnp.stack(got, 1).reshape(-1, *got[0].shape[1:])


def flat_rows(x):
    return x.reshape(-1, x.shape[-1])


def pieces_for(h, group):
    count = len(masks_of(group))
    h = h.reshape(-1, count, *h.shape[1:])
    here = (lax.axis_index("shard") // group[0]) % count
    return [lax.dynamic_index_in_dim(h, here ^ k, 1, keepdims=False) for k in range(count)]


def send_pieces(pieces, group, shards):
    return [p if m == 0 else exchange(p, m, shards) for p, m in zip(pieces, masks_of(group))]


def add_up(found):
    return functools.reduce(lambda a, b: a + b, [f.astype(f32) for f in found])


def core_pieces(pairs, group, shards):
    cut = [
        [pieces_for(x.reshape(shards, x.shape[0] // shards, -1), group) for x in pair] for pair in pairs
    ]
    return [
        jnp.concatenate([add_up([mine[k], other[k]]).astype(bf16) for mine, other in cut], -1)
        for k in range(len(masks_of(group)))
    ]


def body(
    tokens, cotangent, ln1_gain, ln1_bias, w_qkv, b_qv, w_proj, b_proj,
    ln2_gain, ln2_bias, w_up, b_up, w_down, b_down, *, shards,
):
    images_all, length, width = tokens.shape
    layers, per = ln1_gain.shape
    images = images_all // 2
    steps = images // GROUP
    rows = -(-length // 16) * 16
    hidden = 2 * w_up.shape[2]
    heads = width // HEAD
    ca, cm = 2 * width + LANES, hidden
    t = lax.axis_index("tensor")
    core = t.astype(jnp.int32).reshape(1)
    groups = bit_groups(shards)

    def turned(which):
        one = [(0, 1)] * 6 + [(0, 2, 3, 1, 4), (0, 2, 1, 3), (0, 1, 3, 2), (0, 1, 2), (1, 0, 2), (0, 2, 1)]
        back = [tuple(sorted(range(len(p)), key=lambda i: p[i])) for p in one]
        return one if which == "in" else back

    raw = (ln1_gain, ln1_bias, b_proj, ln2_gain, ln2_bias, b_down, w_qkv, b_qv, w_proj, w_up, b_up, w_down)
    raw = [x.transpose(p) for x, p in zip(raw, turned("in"))]
    first_attn, first_mlp, later = in_vmem(
        kernel_pack, raw, [arr((per, c), bf16) for c in (ca, cm, ca + cm)],
        [((16, LANES), f32), ((per, LANES), f32)], "pack",
    )

    tok = images * length
    proj_flops = 2 * tok * width
    attn_flops = images * heads * 4 * length * length * HEAD
    aspec, mspec = whole((width, ca)), whole((width, cm))
    table_shape = (16, hidden)
    tspec = whole(table_shape)
    half_shape = (length, images, width)
    pad_shape = (images, rows, width)
    join_shape = (images, -(-length // 32) * 32, width)
    vec_shape = (16, LANES)
    qkv_shape = (images, rows, 3 * width)
    p_shape = (images, heads, rows, rows)
    g_shape = (images, rows, hidden)
    tokens_in, cotangent_in = kept(*(x.transpose(1, 0, 2) for x in (tokens, cotangent)))

    def g_of(shape):
        return (GROUP, *shape[1:])


    x_all, cot_all = call(
        kernel_spread, 1, core, (tokens_in, cotangent_in), [of_core(tokens_in.shape)] * 2,
        [in_hbm(pad_shape, bf16)] * 2, [whole_out(pad_shape)] * 2, [], 0, "spread", 16,
    )

    def early(x, stages):
        x = x[None]
        for group in stages:
            x = in_order(fetch(x, group, shards), group)
        return x

    last, before = groups[-1], groups[-2]
    got_z0 = fetch(early(first_attn, groups[:-2]), before, shards)
    z0 = in_order(after_all(got_z0, x_all, cot_all), before)
    got_m0 = fetch(early(after(first_mlp, z0), groups[:-2]), before, shards)
    got_a0 = fetch(z0, last, shards)
    l1 = early(after(later, z0), groups[:-2])
    near = [exchange(l1, before[0], shards)]
    a0 = flat_rows(in_order(got_a0, last))
    a0_other = swap_cores(a0)
    *got_m0, near[0] = after_all(got_m0 + near, a0)
    far = after(l1, a0)
    got_l1 = [l1] + near + [exchange(far, m, shards) for m in masks_of(before)[2:]]
    got_m0 = fetch(in_order(got_m0, before), last, shards)

    saved = [in_hbm(qkv_shape, bf16), in_hbm(p_shape, bf16), in_hbm(pad_shape, bf16),
             arr(pad_shape, f32), arr(table_shape, f32)]
    saved_specs = [by_group(qkv_shape), by_group(p_shape), by_group(pad_shape), by_group(pad_shape),
                   whole_out(table_shape)]
    attn_weights = [((width, 3 * width), bf16), ((width, width), bf16)]
    mlp_sums = [((width, hidden), f32), ((width, hidden), f32)]
    forward_flops = 4 * proj_flops * width + attn_flops
    qkv, p_all, o_all, mid, table = call(
        functools.partial(kernel_first_attn_forward, shards, length), steps, None,
        (*kept(x_all), a0, a0_other),
        [by_group(pad_shape), aspec, aspec], saved, saved_specs,
        attn_weights + [(g_of(pad_shape), f32)], forward_flops, "attn_forward_0",
    )
    got = after_all(got_m0 + got_l1, mid)
    m0, l1 = got[: len(got_m0)], got[len(got_m0) :]
    m0 = flat_rows(in_order(m0, last))
    m0_other = swap_cores(m0)
    l1 = in_order(l1, before)
    got_a1 = fetch(l1[:, :, :ca], last, shards)
    stream, g_all, slope_all = call(
        kernel_mlp_forward, steps, None,
        (mid, table, m0, m0_other),
        [by_group(pad_shape), tspec, mspec, mspec],
        [arr(pad_shape, f32), in_hbm(g_shape, bf16), in_hbm(g_shape, bf16)],
        [by_group(pad_shape), by_group(g_shape), by_group(g_shape)],
        [], 2 * proj_flops * hidden, "mlp_forward",
    )
    a1 = flat_rows(in_order(after_all(got_a1, stream), last))
    a1_other = swap_cores(a1)
    got_m1 = fetch(after(l1[:, :, ca:], a1), last, shards)
    qkv1, p1, o1, mid1, table1 = call(
        functools.partial(kernel_attn_forward, shards, length), steps, None,
        (stream, a1, a1_other),
        [by_group(pad_shape), aspec, aspec], saved, saved_specs,
        attn_weights, forward_flops, "attn_forward_1",
    )
    m1 = flat_rows(in_order(after_all(got_m1, mid1), last))
    m1_other = swap_cores(m1)
    out, dmid1, sums1, gm1_mine, gm1_other = call(
        kernel_mlp_both, steps, None,
        (mid1, *kept(cot_all), table1, m1, m1_other),
        [by_group(pad_shape), by_group(pad_shape), tspec, mspec, mspec],
        [arr(half_shape, bf16), arr(pad_shape, f32), arr(table_shape, f32)] + [arr((width, cm), bf16)] * 2,
        [whole_out(half_shape), by_group(pad_shape), whole_out(table_shape)] + [whole_out((width, cm))] * 2,
        [(g_of(g_shape), bf16), (g_of(g_shape), bf16), (join_shape, bf16)] + mlp_sums,
        6 * proj_flops * hidden, "mlp_both", 40,
    )
    back_specs = [by_group(pad_shape), by_group(pad_shape), tspec, tspec, by_group(qkv_shape),
                  by_group(p_shape), by_group(pad_shape), aspec, aspec]
    back_scratch = [
        (table_shape, f32), (vec_shape, f32), *attn_weights, (g_of(qkv_shape), bf16),
        ((width, 3 * width), f32), ((width, width), f32),
    ]
    ga_outs, ga_specs = [arr((width, ca), bf16)] * 2, [whole_out((width, ca))] * 2
    back_flops = 8 * proj_flops * width + 2.5 * attn_flops
    hm1 = swap_cores(gm1_other)
    e, ga1_mine, ga1_other = call(
        functools.partial(kernel_attn_backward, shards), steps, None,
        (dmid1, stream, table1, sums1, *kept(qkv1, p1, o1), a1, a1_other),
        back_specs, [in_hbm(pad_shape, f32)] + ga_outs, [by_group(pad_shape)] + ga_specs,
        back_scratch, back_flops, "attn_backward_1",
    )
    hm1, ga1_mine, ga1_other = after_all((hm1, ga1_mine, ga1_other), e)
    h1 = core_pieces([(ga1_mine, swap_cores(ga1_other)), (gm1_mine, hm1)], last, shards)
    out_other = swap_cores(out)
    e = after(e, out_other, *h1)
    dmid, sums, gm_mine, gm_other = call(
        kernel_mlp_backward, steps, None,
        (*kept(e), mid, table, *kept(g_all, slope_all), m0, m0_other),
        [by_group(pad_shape), by_group(pad_shape), tspec, by_group(g_shape), by_group(g_shape), mspec, mspec],
        [in_hbm(pad_shape, f32), arr(table_shape, f32)] + [arr((width, cm), bf16)] * 2,
        [by_group(pad_shape), whole_out(table_shape)] + [whole_out((width, cm))] * 2,
        mlp_sums, 4 * proj_flops * hidden, "mlp_backward",
    )
    middle = groups[:-1][::-1]
    h1 = add_up(after_all(send_pieces(h1, last, shards), dmid)).astype(bf16)
    h1 = pieces_for(h1, middle[0])
    h0m = core_pieces([(gm_mine, swap_cores(gm_other))], last, shards)
    dmid = after(dmid, *h0m, *h1)
    grad, ga_mine, ga_other = call(
        functools.partial(kernel_first_attn_backward, shards), steps, None,
        (*kept(dmid, x_all), table, sums, *kept(qkv, p_all, o_all), a0, a0_other),
        back_specs, [arr(half_shape, bf16)] + ga_outs, [whole_out(half_shape)] + ga_specs,
        back_scratch + [(join_shape, bf16), (g_of(pad_shape), f32)], back_flops, "attn_backward_0",
    )
    h0m = send_pieces(h0m, last, shards)
    h1 = send_pieces(h1, middle[0], shards)
    n = len(h0m)
    got = after_all(h0m + h1 + [ga_mine, ga_other, grad], grad)
    h0m, h1, (ga_mine, ga_other, grad) = got[:n], got[n:-3], got[-3:]
    h0a = core_pieces([(ga_mine, swap_cores(ga_other))], last, shards)
    grad_other = swap_cores(after(grad, *h0a))
    h0m = after_all(pieces_for(add_up(h0m).astype(bf16), middle[0]), grad_other, *h0a)
    h0a = send_pieces(h0a, last, shards)
    h0m = send_pieces(h0m, middle[0], shards)
    out_full = both_cores(core, out, out_other, bf16)
    got = after_all(h0a + h0m, out_full)
    h0a, h0m = got[: len(h0a)], got[len(h0a) :]
    h0a = send_pieces(pieces_for(add_up(h0a).astype(bf16), middle[0]), middle[0], shards)
    for group in middle[1:]:
        h0a, h0m, h1 = (
            send_pieces(pieces_for(add_up(h).astype(bf16), group), group, shards) for h in (h0a, h0m, h1)
        )

    grad_full = both_cores(core, grad, grad_other, f32)
    h0a = after_all(h0a, grad_full)
    grads = in_vmem(
        functools.partial(kernel_unpack, len(h1)),
        [x.reshape(per, -1) for h in (h0a, h0m, h1) for x in h],
        [arr(x.shape, f32) for x in raw], [], "unpack",
    )
    grads = [g.transpose(p) for g, p in zip(grads, turned("out"))]
    g1, b1, bp, g2, b2, bd, gq, gb, gp, gu, gbu, gd = grads
    return (
        out_full.transpose(1, 0, 2), grad_full.transpose(1, 0, 2),
        g1, b1, gq, gb, gp, bp, g2, b2, gu, gbu, gd, bd,
    )


def solution(mesh):
    args = (
        P("shard", None, None),
        P("shard", None, None),
        P(None, "shard"),
        P(None, "shard"),
        P(None, "shard", None, "tensor", None),
        P(None, None, "tensor", "shard"),
        P(None, "tensor", None, "shard"),
        P(None, "shard"),
        P(None, "shard"),
        P(None, "shard"),
        P(None, "shard", "tensor"),
        P(None, "tensor", "shard"),
        P(None, "tensor", "shard"),
        P(None, "shard"),
    )
    return jax.shard_map(
        functools.partial(body, shards=mesh.shape["shard"]),
        mesh=mesh,
        in_specs=args,
        out_specs=args,
        check_vma=False,
    )
```
